32 devices in a mesh: dp: 8 (over z, core), tensor: 4 (over y, x).
Axes of the slice: x: 2, y: 2, z: 4, core: 2. Of those that a mesh axis runs over, the one named last changes fastest.
Arguments:
- tokens: bfloat16 [8192, 1536], P(('dp', 'tensor')), may hold values from -6 to 6
- segments: int32 [8192], P('dp'), may hold values from 0 to 2, as said below
- attn_gain: float32 [1536], replicated, may hold values from 0.1 to 1.9
- w_query: bfloat16 [1536, 1536], P('dp', 'tensor'), may hold values from -0.15625 to 0.15625
- key_weight: bfloat16 [1536, 512], P('dp', 'tensor'), may hold values from -0.15625 to 0.15625
- value_weight: bfloat16 [1536, 512], P('dp', 'tensor'), may hold values from -0.15625 to 0.15625
- query_gain: float32 [64], replicated, may hold values from 0.1 to 1.9
- key_gain: float32 [64], replicated, may hold values from 0.1 to 1.9
- w_out: bfloat16 [1536, 1536], P('tensor', 'dp'), may hold values from -0.625 to 0.625
- ffn_gain: float32 [1536], replicated, may hold values from 0.1 to 1.9
- w_gate: bfloat16 [1536, 6912], P('dp', 'tensor'), may hold values from -0.15625 to 0.15625
- w_up: bfloat16 [1536, 6912], P('dp', 'tensor'), may hold values from -0.15625 to 0.15625
- w_down: bfloat16 [6912, 1536], P('tensor', 'dp'), may hold values from -0.078125 to 0.078125
- cotangent: bfloat16 [8192, 1536], P(('dp', 'tensor')), may hold values from -6 to 6
Outputs:
- output: float32 [8192, 1536], P(('dp', 'tensor'))
- tokens_grad: float32 [8192, 1536], P(('dp', 'tensor'))
- attn_gain_grad: float32 [1536], replicated
- w_query_grad: float32 [1536, 1536], P('dp', 'tensor')
- w_key_grad: float32 [1536, 512], P('dp', 'tensor')
- w_value_grad: float32 [1536, 512], P('dp', 'tensor')
- query_gain_grad: float32 [64], replicated
- key_gain_grad: float32 [64], replicated
- w_out_grad: float32 [1536, 1536], P('tensor', 'dp')
- ffn_gain_grad: float32 [1536], replicated
- w_gate_grad: float32 [1536, 6912], P('dp', 'tensor')
- w_up_grad: float32 [1536, 6912], P('dp', 'tensor')
- w_down_grad: float32 [6912, 1536], P('tensor', 'dp')
The draws below stay inside these ranges and needn't reach their ends.
Inputs may be any that keep to these rules, and one draw needn't show every extreme that they name: `segments`: within each sequence of 1024 tokens the segment numbers are 0, 1, 2 in order, never falling, each present; documents 0 and 2 have fewer than 256 tokens each.
All inputs are finite; a program needn't handle non-finite values.
Results may differ from the reference program's by a relative error of at most 0.02.
Values may be sent and summed in bfloat16 or wider, within the bound.
No kernel may reach another device: no remote copies, remote signals or barrier semaphores. Data moves between devices by JAX's collectives and lax.ppermute only.
A program may use at most 192 MiB of HBM per device.

```python
import jax
import jax.numpy as jnp
from jax import lax

MODEL_WIDTH = 1536
QUERY_HEADS = 24
KEY_VALUE_HEADS = 8
HEAD_SIZE = 64
FF = 6912
TOK_DEV = 256
SEQUENCE_LENGTH = 1024
TOKEN_COUNT = 8192


def draw_segments(key, part):
    key = jax.random.fold_in(key, 7)
    sequence_number = TOKEN_COUNT // SEQUENCE_LENGTH
    first_key, second_key = jax.random.split(key)
    head_len = jax.random.randint(first_key, (sequence_number, 1), 1, TOK_DEV, dtype=jnp.int32)
    tail_len = jax.random.randint(second_key, (sequence_number, 1), 1, TOK_DEV, dtype=jnp.int32)
    places = jnp.arange(SEQUENCE_LENGTH, dtype=jnp.int32)[None, :]
    numbers = (places >= head_len).astype(jnp.int32) + (places >= SEQUENCE_LENGTH - tail_len).astype(jnp.int32)
    return numbers.reshape(TOKEN_COUNT)


def levels(own_key, shape, shards, low, high):
    def one(position, blocks):
        heights = jax.random.uniform(jax.random.fold_in(jax.random.fold_in(own_key, 6), position), (blocks,), jnp.float32, low / len(shards), high / len(shards))
        return jnp.repeat(jnp.exp(heights), shape[position] // blocks).reshape((-1,) + (1,) * (len(shape) - position - 1))

    level = one(*shards[0])
    for cut in shards[1:]:
        level = level * one(*cut)
    return level


def scatter_about(own_key, shape, width, most, cuts=(), held_as=jnp.bfloat16):
    values = jax.random.normal(own_key, shape, jnp.float32) * width
    if len(cuts) > 0:
        values = levels(own_key, shape, cuts, -0.22, 0.18) * values
    return jnp.clip(values, min=-most, max=most).astype(held_as)


def setup_inputs(seed: int = 0) -> dict:
    splits = jax.random.split(jax.random.key(seed), 15)
    tokens = scatter_about(splits[0], (TOKEN_COUNT, MODEL_WIDTH), 1.0, 6.0, ((0, 32),))
    segments = draw_segments(jax.random.fold_in(splits[14], 71), 0)
    attn_gain = jnp.clip(1.0 + 0.18 * jax.random.normal(splits[2], (MODEL_WIDTH,), jnp.float32), 0.1, 1.9)
    w_query = scatter_about(splits[3], (MODEL_WIDTH, QUERY_HEADS * HEAD_SIZE), MODEL_WIDTH ** -0.5, 0.15625, ((0, 8), (1, 4)))
    key_weight = scatter_about(splits[4], (MODEL_WIDTH, KEY_VALUE_HEADS * HEAD_SIZE), MODEL_WIDTH ** -0.5, 0.15625, ((0, 8), (1, 4)))
    value_weight = scatter_about(splits[5], (MODEL_WIDTH, KEY_VALUE_HEADS * HEAD_SIZE), MODEL_WIDTH ** -0.5, 0.15625, ((0, 8), (1, 4)))
    query_gain = jnp.clip(1.0 + 0.18 * jax.random.normal(splits[6], (HEAD_SIZE,), jnp.float32), 0.1, 1.9)
    key_gain = jnp.clip(1.0 + 0.18 * jax.random.normal(splits[7], (HEAD_SIZE,), jnp.float32), 0.1, 1.9)
    w_out = scatter_about(splits[8], (QUERY_HEADS * HEAD_SIZE, MODEL_WIDTH), (QUERY_HEADS * HEAD_SIZE // 16) ** -0.5, 0.625, ((0, 4), (1, 8)))
    ffn_gain = jnp.clip(1.0 + 0.18 * jax.random.normal(splits[9], (MODEL_WIDTH,), jnp.float32), 0.1, 1.9)
    w_gate = scatter_about(splits[10], (MODEL_WIDTH, FF), MODEL_WIDTH ** -0.5, 0.15625, ((0, 8), (1, 4)))
    w_up = scatter_about(splits[11], (MODEL_WIDTH, FF), MODEL_WIDTH ** -0.5, 0.15625, ((0, 8), (1, 4)))
    w_down = scatter_about(splits[12], (FF, MODEL_WIDTH), FF ** -0.5, 0.078125, ((0, 4), (1, 8)))
    cotangent = scatter_about(splits[13], (TOKEN_COUNT, MODEL_WIDTH), 1.0, 6.0, ((0, 32),))
    return dict(tokens=tokens, segments=segments, attn_gain=attn_gain, w_query=w_query, key_weight=key_weight, value_weight=value_weight, query_gain=query_gain, key_gain=key_gain, w_out=w_out, ffn_gain=ffn_gain, w_gate=w_gate, w_up=w_up, w_down=w_down, cotangent=cotangent)


@jax.custom_vjp
def reduced_precision(v):
    return lax.optimization_barrier(v.astype(jnp.bfloat16)).astype(jnp.float32)

@jax.custom_vjp
def reduced_precision_backward(v):
    return v

def low_keep(v):
    return (reduced_precision(v), None)

def low_pass(kept, grad):
    return (grad,)

def back_keep(v):
    return (v, None)

def back_low(kept, grad):
    return (reduced_precision(grad),)
reduced_precision.defvjp(low_keep, low_pass)
reduced_precision_backward.defvjp(back_keep, back_low)
EPSILON = 1e-05
ROTARY_BASE = 1000000.0
NEGATIVE_FILL = -1e+30

def product_highest_precision(left, right):
    return jnp.dot(left, right, precision=lax.Precision.HIGHEST, preferred_element_type=jnp.float32)

def norm_rows(values_in, gain):
    return values_in * lax.rsqrt(lax.optimization_barrier(jnp.mean(values_in * values_in, axis=-1, keepdims=True)) + EPSILON) * gain

def rotate(heads, positions):
    half_size = heads.shape[-1] // 2
    freqs = ROTARY_BASE ** (-2.0 * jnp.arange(half_size, dtype=jnp.float32) / heads.shape[-1])
    angles = positions.astype(jnp.float32)[:, None] * freqs[None, :]
    cosine = jnp.cos(angles)[:, None, :]
    sine = jnp.sin(angles)[:, None, :]
    first_half = heads[..., :half_size]
    second_half = heads[..., half_size:]
    return jnp.concatenate([first_half * cosine - second_half * sine, second_half * cosine + first_half * sine], axis=-1)

def position_table(seq_segments):
    length_total = seq_segments.shape[0]
    indices = jnp.arange(length_total, dtype=jnp.int32)
    boundary = jnp.concatenate([jnp.ones((1,), jnp.bool_), seq_segments[1:] != seq_segments[:-1]])
    starts = lax.cummax(jnp.where(boundary, indices, jnp.zeros_like(indices)), axis=0)
    return indices - starts

def attend_heads(packed):
    query_matrix, key_matrix, value_matrix, seq_segments = packed
    length_total = query_matrix.shape[0]
    group_width = QUERY_HEADS // KEY_VALUE_HEADS
    grouped_queries = query_matrix.reshape(length_total, KEY_VALUE_HEADS, group_width, HEAD_SIZE)
    scores = jnp.einsum('ikgd,jkd->kgij', grouped_queries, key_matrix, precision=lax.Precision.HIGHEST) * HEAD_SIZE ** (-0.5)
    scores = reduced_precision_backward(scores)
    indices = jnp.arange(length_total, dtype=jnp.int32)
    allowed = (indices[None, :] <= indices[:, None]) & (seq_segments[:, None] == seq_segments[None, :])
    scores = jnp.where(allowed[None, None], scores, NEGATIVE_FILL)
    row_peak = lax.optimization_barrier(jnp.max(scores, axis=-1, keepdims=True))
    exps = jnp.exp(scores - row_peak)
    softmax_rows = reduced_precision(exps / lax.optimization_barrier(jnp.sum(exps, axis=-1, keepdims=True)))
    mixed = jnp.einsum('kgij,jkd->ikgd', softmax_rows, value_matrix, precision=lax.Precision.HIGHEST)
    return mixed.reshape(length_total, QUERY_HEADS * HEAD_SIZE)

def reference(tokens, segments, attn_gain, w_query, key_weight, value_weight, query_gain, key_gain, w_out, ffn_gain, w_gate, w_up, w_down, cotangent):
    sequence_number = TOKEN_COUNT // SEQUENCE_LENGTH
    positions = jax.vmap(position_table)(segments.reshape(sequence_number, SEQUENCE_LENGTH)).reshape(TOKEN_COUNT)

    def forward(inputs, gain_one, query_w, key_weight_local, value_weight_local, gain_query, gain_key, out_w, gain_two, gate_w, up_w, down_w):
        first_normalized = reduced_precision(norm_rows(inputs, gain_one))
        query_raw = reduced_precision_backward(product_highest_precision(first_normalized, query_w)).reshape(TOKEN_COUNT, QUERY_HEADS, HEAD_SIZE)
        query_matrix = reduced_precision(rotate(norm_rows(query_raw, gain_query), positions))
        key_unrotated = reduced_precision_backward(product_highest_precision(first_normalized, key_weight_local)).reshape(TOKEN_COUNT, KEY_VALUE_HEADS, HEAD_SIZE)
        key_matrix = reduced_precision(rotate(norm_rows(key_unrotated, gain_key), positions))
        value_matrix = reduced_precision(reduced_precision_backward(product_highest_precision(first_normalized, value_weight_local))).reshape(TOKEN_COUNT, KEY_VALUE_HEADS, HEAD_SIZE)
        attended_rows = lax.map(jax.checkpoint(attend_heads), (query_matrix.reshape(sequence_number, SEQUENCE_LENGTH, QUERY_HEADS, HEAD_SIZE), key_matrix.reshape(sequence_number, SEQUENCE_LENGTH, KEY_VALUE_HEADS, HEAD_SIZE), value_matrix.reshape(sequence_number, SEQUENCE_LENGTH, KEY_VALUE_HEADS, HEAD_SIZE), segments.reshape(sequence_number, SEQUENCE_LENGTH)))
        attended_rows = reduced_precision(reduced_precision_backward(attended_rows.reshape(TOKEN_COUNT, QUERY_HEADS * HEAD_SIZE)))
        hidden = inputs + reduced_precision_backward(product_highest_precision(attended_rows, out_w))
        normed_two = reduced_precision(norm_rows(hidden, gain_two))
        gating = reduced_precision_backward(product_highest_precision(normed_two, gate_w))
        lifted = reduced_precision_backward(product_highest_precision(normed_two, up_w))
        activation = reduced_precision(jax.nn.silu(gating) * lifted)
        return hidden + reduced_precision_backward(product_highest_precision(activation, down_w))
    output, pull = jax.vjp(forward, tokens.astype(jnp.float32), attn_gain.astype(jnp.float32), w_query.astype(jnp.float32), key_weight.astype(jnp.float32), value_weight.astype(jnp.float32), query_gain.astype(jnp.float32), key_gain.astype(jnp.float32), w_out.astype(jnp.float32), ffn_gain.astype(jnp.float32), w_gate.astype(jnp.float32), w_up.astype(jnp.float32), w_down.astype(jnp.float32))
    grads = pull(cotangent.astype(jnp.float32))
    return (output, grads[0], grads[1], grads[2], grads[3], grads[4], grads[5], grads[6], grads[7], grads[8], grads[9], grads[10], grads[11])
```

```python
import functools

import jax
import jax.numpy as jnp
from jax import lax
from jax.experimental import pallas as pl
from jax.experimental.pallas import tpu as pltpu
from jax.sharding import PartitionSpec as P

QUERY_HEADS = 24
KEY_VALUE_HEADS = 8
HEAD_SIZE = 64
GROUP = QUERY_HEADS // KEY_VALUE_HEADS
EPSILON = 1e-05
ROTARY_BASE = 1000000.0
NEGATIVE_FILL = -1e30
F32 = jnp.float32
LOW = jnp.bfloat16
SCALE = HEAD_SIZE ** (-0.5)


def norm_rows(values_in, gain):
    return (
        values_in
        * lax.rsqrt(jnp.mean(values_in * values_in, axis=-1, keepdims=True) + EPSILON)
        * gain
    )


def norm_back(values, gain, grad):
    inverse = lax.rsqrt(jnp.mean(values * values, axis=-1, keepdims=True) + EPSILON)
    hat = values * inverse
    scaled = grad * gain
    inner = jnp.mean(scaled * hat, axis=-1, keepdims=True)
    return (scaled - hat * inner) * inverse, jnp.sum(grad * hat, axis=0)


def mm(left, right):
    return jnp.dot(left, right, preferred_element_type=F32)


def cross_rows(left, right):
    return lax.dot_general(left, right, (((1,), (1,)), ((), ())), preferred_element_type=F32)


def cross_cols(left, right):
    return lax.dot_general(left, right, (((0,), (0,)), ((), ())), preferred_element_type=F32)


NT = (((1,), (1,)), ((), ()))
NN = (((1,), (0,)), ((), ()))
TN = (((0,), (0,)), ((), ()))


def kdot(left, right, dims):
    return lax.dot_general(left, right, dims, preferred_element_type=F32)


def stack_heads(block, head):
    first = head * GROUP * HEAD_SIZE
    return jnp.concatenate(
        [block[:, first + g * HEAD_SIZE : first + (g + 1) * HEAD_SIZE] for g in range(GROUP)], axis=0
    )


def attend_kernel(heads, rows, me_ref, q_ref, k_ref, v_ref, lo_ref, out_ref, lse_ref):
    me = me_ref[0]
    block = pl.program_id(0) ^ me
    low_bound = jnp.concatenate([lo_ref[0]] * GROUP, axis=1)
    row_ids = block * rows + lax.broadcasted_iota(jnp.int32, (1, rows), 1)
    row_ids = jnp.concatenate([row_ids] * GROUP, axis=1)
    width = GROUP * rows
    queries = q_ref[...] * SCALE
    pieces = []
    for head in range(heads):
        q3 = stack_heads(queries, head)
        cols = slice(head * HEAD_SIZE, (head + 1) * HEAD_SIZE)

        def step(other, carry, q3=q3, cols=cols):
            peak, total, acc = carry
            first = pl.multiple_of((other ^ me) * rows, rows)
            keys = k_ref[pl.ds(first, rows), cols]
            vals = v_ref[pl.ds(first, rows), cols]
            ids = other * rows + lax.broadcasted_iota(jnp.int32, (rows, 1), 0)
            scores = kdot(keys, q3, NT)
            scores = jnp.where((ids <= row_ids) & (ids >= low_bound), scores, NEGATIVE_FILL)
            higher = jnp.maximum(peak, jnp.max(scores, axis=0, keepdims=True))
            fade = jnp.exp(peak - higher)
            exps = jnp.exp(scores - higher)
            total = total * fade + jnp.sum(exps, axis=0, keepdims=True)
            acc = acc * fade + kdot(vals, exps.astype(LOW), TN)
            return higher, total, acc

        start = (
            jnp.full((1, width), NEGATIVE_FILL, F32),
            jnp.zeros((1, width), F32),
            jnp.zeros((HEAD_SIZE, width), F32),
        )
        start = step(block, start)
        peak, total, acc = lax.fori_loop(0, block, step, start)
        acc = acc / total
        lse_ref[0, head : head + 1, :] = peak + jnp.log(total)
        pieces += [acc[:, g * rows : (g + 1) * rows] for g in range(GROUP)]
    out_ref[...] = jnp.concatenate(pieces, axis=0).T.astype(LOW)


def attend_back_kernel(
    heads, rows, me_ref, q_ref, k_ref, v_ref, lo_ref, o_ref, do_ref, lse_ref, dq_ref, dk_ref, dv_ref
):
    me = me_ref[0]

    @pl.when(pl.program_id(0) == 0)
    def _():
        dk_ref[...] = jnp.zeros_like(dk_ref)
        dv_ref[...] = jnp.zeros_like(dv_ref)

    block = pl.program_id(0) ^ me
    low_bound = jnp.concatenate([lo_ref[0]] * GROUP, axis=1)
    row_ids = block * rows + lax.broadcasted_iota(jnp.int32, (1, rows), 1)
    row_ids = jnp.concatenate([row_ids] * GROUP, axis=1)
    width = GROUP * rows
    queries = q_ref[...] * SCALE
    grads = do_ref[...]
    product = (grads.astype(F32) * o_ref[...].astype(F32)).T
    pieces = []
    for head in range(heads):
        q3 = stack_heads(queries, head)
        do3 = stack_heads(grads, head)
        cols = slice(head * HEAD_SIZE, (head + 1) * HEAD_SIZE)
        first_row = head * GROUP * HEAD_SIZE
        inner = jnp.concatenate(
            [
                jnp.sum(
                    product[first_row + g * HEAD_SIZE : first_row + (g + 1) * HEAD_SIZE],
                    axis=0,
                    keepdims=True,
                )
                for g in range(GROUP)
            ],
            axis=1,
        )
        lse = lse_ref[0, head : head + 1, :]

        def step(other, acc, q3=q3, do3=do3, cols=cols, inner=inner, lse=lse):
            first = pl.multiple_of((other ^ me) * rows, rows)
            place = pl.ds(first, rows)
            keys = k_ref[place, cols]
            vals = v_ref[place, cols]
            ids = other * rows + lax.broadcasted_iota(jnp.int32, (rows, 1), 0)
            scores = kdot(keys, q3, NT)
            scores = jnp.where((ids <= row_ids) & (ids >= low_bound), scores, NEGATIVE_FILL)
            probs = jnp.exp(scores - lse)
            d_probs = kdot(vals, do3, NT)
            d_scores = (probs * (d_probs - inner)).astype(LOW)
            dk_ref[place, cols] += kdot(d_scores, q3, NN)
            dv_ref[place, cols] += kdot(probs.astype(LOW), do3, NN)
            return acc + kdot(keys, d_scores, TN)

        acc = lax.fori_loop(0, block + 1, step, jnp.zeros((HEAD_SIZE, width), F32))
        pieces += [acc[:, g * rows : (g + 1) * rows] for g in range(GROUP)]
    dq_ref[...] = jnp.concatenate(pieces, axis=0).T * SCALE


def attention_specs(ranks, rows, heads):
    length = ranks * rows
    q_spec = pl.BlockSpec((rows, heads * GROUP * HEAD_SIZE), lambda i, me: (i, 0))
    kv_spec = pl.BlockSpec((length, heads * HEAD_SIZE), lambda i, me: (0, 0))
    lo_spec = pl.BlockSpec((1, 1, rows), lambda i, me: (i, 0, 0))
    lse_spec = pl.BlockSpec((1, heads, GROUP * rows), lambda i, me: (i, 0, 0))
    return q_spec, kv_spec, lo_spec, lse_spec


def attend(me, queries, keys, values, bounds, ranks, heads):
    length = queries.shape[0]
    rows = length // ranks
    q_spec, kv_spec, lo_spec, lse_spec = attention_specs(ranks, rows, heads)
    return pl.pallas_call(
        functools.partial(attend_kernel, heads, rows),
        grid_spec=pltpu.PrefetchScalarGridSpec(
            num_scalar_prefetch=1,
            grid=(ranks,),
            in_specs=[q_spec, kv_spec, kv_spec, lo_spec],
            out_specs=[q_spec, lse_spec],
        ),
        out_shape=[
            jax.ShapeDtypeStruct(queries.shape, LOW),
            jax.ShapeDtypeStruct((ranks, heads, GROUP * rows), F32),
        ],
        compiler_params=pltpu.CompilerParams(vmem_limit_bytes=48 * 2**20),
        cost_estimate=pl.CostEstimate(
            flops=8 * length * length * heads * GROUP * HEAD_SIZE,
            bytes_accessed=8 * length * heads * GROUP * HEAD_SIZE,
            transcendentals=length * length * heads * GROUP,
        ),
        name="attend",
    )(me, queries, keys, values, bounds)


def attend_back(me, queries, keys, values, bounds, attended, d_attended, lse, ranks, heads):
    length = queries.shape[0]
    rows = length // ranks
    q_spec, kv_spec, lo_spec, lse_spec = attention_specs(ranks, rows, heads)
    return pl.pallas_call(
        functools.partial(attend_back_kernel, heads, rows),
        grid_spec=pltpu.PrefetchScalarGridSpec(
            num_scalar_prefetch=1,
            grid=(ranks,),
            in_specs=[q_spec, kv_spec, kv_spec, lo_spec, q_spec, q_spec, lse_spec],
            out_specs=[q_spec, kv_spec, kv_spec],
        ),
        out_shape=[
            jax.ShapeDtypeStruct(queries.shape, F32),
            jax.ShapeDtypeStruct(keys.shape, F32),
            jax.ShapeDtypeStruct(keys.shape, F32),
        ],
        compiler_params=pltpu.CompilerParams(vmem_limit_bytes=48 * 2**20),
        cost_estimate=pl.CostEstimate(
            flops=20 * length * length * heads * GROUP * HEAD_SIZE,
            bytes_accessed=16 * length * heads * GROUP * HEAD_SIZE,
            transcendentals=length * length * heads * GROUP,
        ),
        name="attend_back",
    )(me, queries, keys, values, bounds, attended, d_attended, lse)


def rotate(heads, cosine, sine):
    half_size = heads.shape[-1] // 2
    first_half = heads[..., :half_size]
    second_half = heads[..., half_size:]
    return jnp.concatenate(
        [first_half * cosine - second_half * sine, second_half * cosine + first_half * sine],
        axis=-1,
    )


def shards(
    dp_size,
    ranks,
    tokens,
    segments,
    attn_gain,
    w_query,
    key_weight,
    value_weight,
    query_gain,
    key_gain,
    w_out,
    ffn_gain,
    w_gate,
    w_up,
    w_down,
    cotangent,
):
    ring = dp_size // 2
    place = lax.axis_index("dp")
    stage = place // 2
    core = place % 2
    me = lax.axis_index("tensor")
    swap_pairs = [(i, i ^ 1) for i in range(dp_size)]
    ring_pairs = [(i, (i + 2) % dp_size) for i in range(dp_size)]
    heads = KEY_VALUE_HEADS // ranks
    rows = tokens.shape[0]
    length = segments.shape[0]
    q_cols = w_query.shape[1]
    kv_cols = key_weight.shape[1]

    def swap(v):
        return lax.ppermute(v, "dp", swap_pairs)

    def onward(v):
        return lax.ppermute(v, "dp", ring_pairs)

    def gather_dp(weight):
        depth, cols = weight.shape
        full = jnp.zeros((dp_size * depth, cols), weight.dtype)
        block = weight
        for hop in range(ring):
            owner = lax.rem(stage - hop + ring, ring)
            full = lax.dynamic_update_slice(full, block, ((owner * 2 + core) * depth, 0))
            full = lax.dynamic_update_slice(full, swap(block), ((owner * 2 + 1 - core) * depth, 0))
            if hop < ring - 1:
                block = onward(block)
        return full

    def by_core(matrix):
        count = matrix.shape[0]
        split = matrix.reshape(count, ring, 2, -1)
        even = split[:, :, 0].reshape(count, -1)
        odd = split[:, :, 1].reshape(count, -1)
        return jnp.where(core == 0, odd, even), jnp.where(core == 0, even, odd)

    def reduce_dp(left_pair, right):
        far = swap(cross_cols(left_pair[0], right).astype(LOW))
        near = (cross_cols(left_pair[1], right) + far.astype(F32)).astype(LOW)
        near = near.reshape(ring, -1, right.shape[1])

        def mine(hop):
            owner = lax.rem(stage - 1 - hop + 2 * ring, ring)
            return lax.dynamic_index_in_dim(near, owner, 0, keepdims=False)

        block = mine(0)
        for hop in range(1, ring):
            block = onward(block).astype(F32) + mine(hop).astype(F32)
            if hop < ring - 1:
                block = block.astype(LOW)
        return block

    def spread(block):
        return [block] + [
            lax.ppermute(block, "tensor", [(i, i ^ j) for i in range(ranks)]) for j in range(1, ranks)
        ]

    def collect(parts):
        total = parts[0].astype(F32)
        for j in range(1, ranks):
            total = total + lax.ppermute(
                parts[j].astype(LOW), "tensor", [(i, i ^ j) for i in range(ranks)]
            ).astype(F32)
        return total

    def cut(matrix):
        return [matrix[j * rows : (j + 1) * rows] for j in range(ranks)]

    tokens_wide = tokens.astype(F32)
    normed_own = norm_rows(tokens_wide, attn_gain).astype(LOW)
    normed_one = spread(normed_own)
    w_qkv = gather_dp(jnp.concatenate([w_query, key_weight, value_weight], axis=1))
    out_t = gather_dp(w_out.T)
    down_t = gather_dp(w_down.T)
    gate_full = gather_dp(w_gate)
    up_full = gather_dp(w_up)
    grad_blocks = spread(cotangent)

    first_start = jnp.sum((segments < 1).astype(jnp.int32))
    second_start = jnp.sum((segments < 2).astype(jnp.int32))
    ids = jnp.arange(length, dtype=jnp.int32).reshape(ranks, rows)
    begins = jnp.where(segments == 0, 0, jnp.where(segments == 1, first_start, second_start))
    begins = begins.astype(jnp.int32).reshape(ranks, rows)
    order = [me ^ j for j in range(ranks)]
    bounds = jnp.stack([lax.dynamic_index_in_dim(begins, o, 0, keepdims=False) for o in order])
    here = jnp.stack([lax.dynamic_index_in_dim(ids, o, 0, keepdims=False) for o in order])
    positions = (here - bounds).reshape(length).astype(F32)
    bounds = bounds.reshape(ranks, 1, rows)
    half = HEAD_SIZE // 2
    freqs = ROTARY_BASE ** (-2.0 * jnp.arange(half, dtype=F32) / HEAD_SIZE)
    angles = positions[:, None] * freqs[None, :]
    cosine = jnp.cos(angles)[:, None, :]
    sine = jnp.sin(angles)[:, None, :]

    raw = jnp.concatenate([mm(block, w_qkv) for block in normed_one], axis=0)
    normed_all = jnp.concatenate(normed_one, axis=0)

    def head_prepare(raw_rows, gain):
        return rotate(norm_rows(raw_rows.reshape(length, -1, HEAD_SIZE), gain), cosine, sine)

    query_rot, query_pull = jax.vjp(head_prepare, raw[:, :q_cols], query_gain)
    key_rot, key_pull = jax.vjp(head_prepare, raw[:, q_cols : q_cols + kv_cols], key_gain)
    query_low = query_rot.astype(LOW).reshape(length, -1)
    key_low = key_rot.astype(LOW).reshape(length, -1)
    value_low = raw[:, q_cols + kv_cols :].astype(LOW)
    me_array = me.astype(jnp.int32).reshape(1)
    attended, lse = attend(me_array, query_low, key_low, value_low, bounds, ranks, heads)

    attn_sum = collect([cross_rows(block, out_t) for block in cut(attended)])
    hidden = tokens_wide + attn_sum
    normed_two = spread(norm_rows(hidden, ffn_gain).astype(LOW))
    normed_two_all = jnp.concatenate(normed_two, axis=0)
    grad_all = jnp.concatenate(grad_blocks, axis=0)

    d_activation = mm(grad_all, down_t)
    gating = mm(normed_two_all, gate_full)
    lifted = mm(normed_two_all, up_full)
    gate_sig = jax.nn.sigmoid(gating)
    silu = gating * gate_sig
    activation = (silu * lifted).astype(LOW)
    d_gating = (d_activation * lifted * gate_sig * (1.0 + gating * (1.0 - gate_sig))).astype(LOW)
    d_lifted = (d_activation * silu).astype(LOW)

    d_normed_two = collect(
        [
            cross_rows(g, gate_full) + cross_rows(u, up_full)
            for g, u in zip(cut(d_gating), cut(d_lifted))
        ]
    )
    output = hidden + collect([cross_rows(block, down_t) for block in cut(activation)])
    grad_pair = by_core(grad_all)
    normed_two_pair = by_core(normed_two_all)
    down_grad = reduce_dp(grad_pair, activation)
    gate_grad = reduce_dp(normed_two_pair, d_gating)
    lift_grad = reduce_dp(normed_two_pair, d_lifted)

    d_hidden_norm, ffn_gain_part = norm_back(hidden, ffn_gain, d_normed_two)
    d_hidden = cotangent.astype(F32) + d_hidden_norm
    hidden_grad = spread(d_hidden.astype(LOW))
    d_attended = jnp.concatenate([mm(block, out_t) for block in hidden_grad], axis=0).astype(LOW)
    hidden_grad_pair = by_core(jnp.concatenate(hidden_grad, axis=0))
    d_queries, d_keys, d_values = attend_back(
        me_array, query_low, key_low, value_low, bounds, attended, d_attended, lse, ranks, heads
    )
    d_query_raw, query_gain_part = query_pull(d_queries.reshape(length, -1, HEAD_SIZE))
    d_key_raw, key_gain_part = key_pull(d_keys.reshape(length, -1, HEAD_SIZE))
    d_raw = jnp.concatenate(
        [d_query_raw.astype(LOW), d_key_raw.astype(LOW), d_values.astype(LOW)], axis=1
    )
    d_normed_one = collect([cross_rows(block, w_qkv) for block in cut(d_raw)])
    qkv_grad = reduce_dp(by_core(normed_all), d_raw)
    out_grad = reduce_dp(hidden_grad_pair, attended)
    d_tokens_norm, attn_gain_part = norm_back(tokens_wide, attn_gain, d_normed_one)
    tokens_grad = d_hidden + d_tokens_norm

    sizes = [attn_gain.shape[0], ffn_gain.shape[0], HEAD_SIZE, HEAD_SIZE]
    gains = jnp.concatenate([attn_gain_part, ffn_gain_part, query_gain_part, key_gain_part])
    gains = gains.reshape(1, -1)
    total = gains
    span = 1
    while span < ranks:
        total = total + lax.ppermute(total, "tensor", [(i, i ^ span) for i in range(ranks)])
        span *= 2
    span = 1
    while span < dp_size:
        total = total + lax.ppermute(total, "dp", [(i, i ^ span) for i in range(dp_size)])
        span *= 2
    total = total.reshape(-1)
    a, b = sizes[0], sizes[0] + sizes[1]
    return (
        output,
        tokens_grad,
        total[:a],
        qkv_grad[:, :q_cols],
        qkv_grad[:, q_cols : q_cols + kv_cols],
        qkv_grad[:, q_cols + kv_cols :],
        total[b : b + HEAD_SIZE],
        total[b + HEAD_SIZE :],
        out_grad.T,
        total[a:b],
        gate_grad,
        lift_grad,
        down_grad.T,
    )


def solution(mesh):
    in_specs = (
        P(("dp", "tensor"), None),
        P("dp"),
        P(),
        P("dp", "tensor"),
        P("dp", "tensor"),
        P("dp", "tensor"),
        P(),
        P(),
        P("tensor", "dp"),
        P(),
        P("dp", "tensor"),
        P("dp", "tensor"),
        P("tensor", "dp"),
        P(("dp", "tensor"), None),
    )
    out_specs = (
        P(("dp", "tensor"), None),
        P(("dp", "tensor"), None),
        P(),
        P("dp", "tensor"),
        P("dp", "tensor"),
        P("dp", "tensor"),
        P(),
        P(),
        P("tensor", "dp"),
        P(),
        P("dp", "tensor"),
        P("dp", "tensor"),
        P("tensor", "dp"),
    )
    body = functools.partial(shards, mesh.shape["dp"], mesh.shape["tensor"])
    return jax.shard_map(body, mesh=mesh, in_specs=in_specs, out_specs=out_specs, check_vma=False)
```

```python
import functools

import jax
import jax.numpy as jnp
from jax import lax
from jax.experimental import pallas as pl
from jax.experimental.pallas import tpu as pltpu
from jax.sharding import PartitionSpec as P

QUERY_HEADS = 24
KEY_VALUE_HEADS = 8
HEAD_SIZE = 64
GROUP = QUERY_HEADS // KEY_VALUE_HEADS
EPSILON = 1e-05
ROTARY_BASE = 1000000.0
NEGATIVE_FILL = -1e30
F32 = jnp.float32
LOW = jnp.bfloat16
SCALE = HEAD_SIZE ** (-0.5)
FREE = pl.CostEstimate(flops=0, bytes_accessed=0, transcendentals=0)


def norm_rows(values_in, gain):
    return (
        values_in
        * lax.rsqrt(jnp.mean(values_in * values_in, axis=-1, keepdims=True) + EPSILON)
        * gain
    )


def norm_back(values, gain, grad):
    inverse = lax.rsqrt(jnp.mean(values * values, axis=-1, keepdims=True) + EPSILON)
    hat = values * inverse
    scaled = grad * gain
    inner = jnp.mean(scaled * hat, axis=-1, keepdims=True)
    return (scaled - hat * inner) * inverse, jnp.sum(grad * hat, axis=0)


def mm(left, right):
    return jnp.dot(left, right, preferred_element_type=F32)


def cross_rows(left, right):
    return lax.dot_general(left, right, (((1,), (1,)), ((), ())), preferred_element_type=F32)


def cross_cols(left, right):
    return lax.dot_general(left, right, (((0,), (0,)), ((), ())), preferred_element_type=F32)


NT = (((1,), (1,)), ((), ()))
NN = (((1,), (0,)), ((), ()))
TN = (((0,), (0,)), ((), ()))


def kdot(left, right, dims):
    return lax.dot_general(left, right, dims, preferred_element_type=F32)


def stack_heads(block, head):
    first = head * GROUP * HEAD_SIZE
    return jnp.concatenate(
        [block[:, first + g * HEAD_SIZE : first + (g + 1) * HEAD_SIZE] for g in range(GROUP)], axis=0
    )


def attend_kernel(heads, rows, me_ref, q_ref, k_ref, v_ref, lo_ref, out_ref, lse_ref):
    me = me_ref[0]
    block = pl.program_id(0) ^ me
    low_bound = jnp.concatenate([lo_ref[0]] * GROUP, axis=1)
    row_ids = block * rows + lax.broadcasted_iota(jnp.int32, (1, rows), 1)
    row_ids = jnp.concatenate([row_ids] * GROUP, axis=1)
    width = GROUP * rows
    queries = q_ref[...] * SCALE
    pieces = []
    for head in range(heads):
        q3 = stack_heads(queries, head)
        cols = slice(head * HEAD_SIZE, (head + 1) * HEAD_SIZE)

        def step(other, carry, q3=q3, cols=cols):
            peak, total, acc = carry
            first = pl.multiple_of((other ^ me) * rows, rows)
            keys = k_ref[pl.ds(first, rows), cols]
            vals = v_ref[pl.ds(first, rows), cols]
            ids = other * rows + lax.broadcasted_iota(jnp.int32, (rows, 1), 0)
            scores = kdot(keys, q3, NT)
            scores = jnp.where((ids <= row_ids) & (ids >= low_bound), scores, NEGATIVE_FILL)
            higher = jnp.maximum(peak, jnp.max(scores, axis=0, keepdims=True))
            fade = jnp.exp(peak - higher)
            exps = jnp.exp(scores - higher)
            total = total * fade + jnp.sum(exps, axis=0, keepdims=True)
            acc = acc * fade + kdot(vals, exps.astype(LOW), TN)
            return higher, total, acc

        start = (
            jnp.full((1, width), NEGATIVE_FILL, F32),
            jnp.zeros((1, width), F32),
            jnp.zeros((HEAD_SIZE, width), F32),
        )
        start = step(block, start)
        peak, total, acc = lax.fori_loop(0, block, step, start)
        acc = acc / total
        lse_ref[0, head : head + 1, :] = peak + jnp.log(total)
        pieces += [acc[:, g * rows : (g + 1) * rows] for g in range(GROUP)]
    out_ref[...] = jnp.concatenate(pieces, axis=0).T.astype(LOW)


def attend_back_kernel(
    heads, rows, me_ref, q_ref, k_ref, v_ref, lo_ref, o_ref, do_ref, lse_ref, dq_ref, dk_ref, dv_ref
):
    me = me_ref[0]

    @pl.when(pl.program_id(0) == 0)
    def _():
        dk_ref[...] = jnp.zeros_like(dk_ref)
        dv_ref[...] = jnp.zeros_like(dv_ref)

    block = pl.program_id(0) ^ me
    low_bound = jnp.concatenate([lo_ref[0]] * GROUP, axis=1)
    row_ids = block * rows + lax.broadcasted_iota(jnp.int32, (1, rows), 1)
    row_ids = jnp.concatenate([row_ids] * GROUP, axis=1)
    width = GROUP * rows
    queries = q_ref[...] * SCALE
    grads = do_ref[...]
    product = (grads.astype(F32) * o_ref[...].astype(F32)).T
    pieces = []
    for head in range(heads):
        q3 = stack_heads(queries, head)
        do3 = stack_heads(grads, head)
        cols = slice(head * HEAD_SIZE, (head + 1) * HEAD_SIZE)
        first_row = head * GROUP * HEAD_SIZE
        inner = jnp.concatenate(
            [
                jnp.sum(
                    product[first_row + g * HEAD_SIZE : first_row + (g + 1) * HEAD_SIZE],
                    axis=0,
                    keepdims=True,
                )
                for g in range(GROUP)
            ],
            axis=1,
        )
        lse = lse_ref[0, head : head + 1, :]

        def step(other, acc, q3=q3, do3=do3, cols=cols, inner=inner, lse=lse):
            first = pl.multiple_of((other ^ me) * rows, rows)
            place = pl.ds(first, rows)
            keys = k_ref[place, cols]
            vals = v_ref[place, cols]
            ids = other * rows + lax.broadcasted_iota(jnp.int32, (rows, 1), 0)
            scores = kdot(keys, q3, NT)
            scores = jnp.where((ids <= row_ids) & (ids >= low_bound), scores, NEGATIVE_FILL)
            probs = jnp.exp(scores - lse)
            d_probs = kdot(vals, do3, NT)
            d_scores = (probs * (d_probs - inner)).astype(LOW)
            dk_ref[place, cols] += kdot(d_scores, q3, NN)
            dv_ref[place, cols] += kdot(probs.astype(LOW), do3, NN)
            return acc + kdot(keys, d_scores, TN)

        acc = lax.fori_loop(0, block + 1, step, jnp.zeros((HEAD_SIZE, width), F32))
        pieces += [acc[:, g * rows : (g + 1) * rows] for g in range(GROUP)]
    dq_ref[...] = jnp.concatenate(pieces, axis=0).T * SCALE


def attention_specs(ranks, rows, heads):
    length = ranks * rows
    q_spec = pl.BlockSpec((rows, heads * GROUP * HEAD_SIZE), lambda i, me: (i, 0))
    kv_spec = pl.BlockSpec((length, heads * HEAD_SIZE), lambda i, me: (0, 0))
    lo_spec = pl.BlockSpec((1, 1, rows), lambda i, me: (i, 0, 0))
    lse_spec = pl.BlockSpec((1, heads, GROUP * rows), lambda i, me: (i, 0, 0))
    return q_spec, kv_spec, lo_spec, lse_spec


def attend(me, queries, keys, values, bounds, ranks, heads):
    length = queries.shape[0]
    rows = length // ranks
    q_spec, kv_spec, lo_spec, lse_spec = attention_specs(ranks, rows, heads)
    return pl.pallas_call(
        functools.partial(attend_kernel, heads, rows),
        grid_spec=pltpu.PrefetchScalarGridSpec(
            num_scalar_prefetch=1,
            grid=(ranks,),
            in_specs=[q_spec, kv_spec, kv_spec, lo_spec],
            out_specs=[q_spec, lse_spec],
        ),
        out_shape=[
            jax.ShapeDtypeStruct(queries.shape, LOW),
            jax.ShapeDtypeStruct((ranks, heads, GROUP * rows), F32),
        ],
        compiler_params=pltpu.CompilerParams(vmem_limit_bytes=48 * 2**20),
        cost_estimate=FREE,
        name="attend",
    )(me, queries, keys, values, bounds)


def attend_back(me, queries, keys, values, bounds, attended, d_attended, lse, ranks, heads):
    length = queries.shape[0]
    rows = length // ranks
    q_spec, kv_spec, lo_spec, lse_spec = attention_specs(ranks, rows, heads)
    return pl.pallas_call(
        functools.partial(attend_back_kernel, heads, rows),
        grid_spec=pltpu.PrefetchScalarGridSpec(
            num_scalar_prefetch=1,
            grid=(ranks,),
            in_specs=[q_spec, kv_spec, kv_spec, lo_spec, q_spec, q_spec, lse_spec],
            out_specs=[q_spec, kv_spec, kv_spec],
        ),
        out_shape=[
            jax.ShapeDtypeStruct(queries.shape, F32),
            jax.ShapeDtypeStruct(keys.shape, F32),
            jax.ShapeDtypeStruct(keys.shape, F32),
        ],
        compiler_params=pltpu.CompilerParams(vmem_limit_bytes=48 * 2**20),
        cost_estimate=FREE,
        name="attend_back",
    )(me, queries, keys, values, bounds, attended, d_attended, lse)


def fold_kernel(ranks, ring, rows, split, core_ref, *refs):
    blocks, all_ref, outs = refs[:ranks], refs[ranks], refs[ranks + 1 :]
    core = core_ref[0]
    turned = outs[-1]
    depth = turned.shape[0] // (2 * ring)
    for j in range(ranks):
        block = blocks[j][...]
        span = slice(j * rows, (j + 1) * rows)
        all_ref[span, :] = block
        if not split:
            turned[:, span] = block.T
            continue
        turned[...] = block.T
        for i in range(ring):
            to = slice(i * depth, (i + 1) * depth)
            for side_ref, side in zip(outs[:2], (1 - core, core)):
                first = pl.multiple_of((2 * i + side) * depth, 16)
                side_ref[to, span] = turned[pl.ds(first, depth), :]


def fold(core, blocks, ring, split=False):
    ranks = len(blocks)
    rows, width = blocks[0].shape
    length = ranks * rows
    whole = lambda shape: pl.BlockSpec(shape, lambda i: (0, 0))
    shapes = [(length, width)] + ([(width // 2, length)] * 2 if split else [(width, length)])
    return pl.pallas_call(
        functools.partial(fold_kernel, ranks, ring, rows, split),
        grid=(1,),
        in_specs=[pl.BlockSpec(memory_space=pltpu.SMEM)] + [whole((rows, width))] * ranks,
        out_specs=[whole(shape) for shape in shapes],
        out_shape=[jax.ShapeDtypeStruct(shape, LOW) for shape in shapes],
        scratch_shapes=[pltpu.VMEM((width, rows), LOW)] if split else [],
        compiler_params=pltpu.CompilerParams(vmem_limit_bytes=40 * 2**20),
        cost_estimate=FREE,
        name="fold",
    )(core, *blocks)


def place_kernel(ring, depth, at_ref, *refs):
    blocks = refs[: 2 * ring]
    full_ref, sems = refs[2 * ring :]
    stage, core = at_ref[0], at_ref[1]
    copies = []
    for hop in range(ring):
        owner = lax.rem(stage - hop + ring, ring)
        for half, side in enumerate((core, 1 - core)):
            first = pl.multiple_of((owner * 2 + side) * depth, 16)
            copies.append(
                pltpu.make_async_copy(
                    blocks[2 * hop + half], full_ref.at[pl.ds(first, depth)], sems.at[2 * hop + half]
                )
            )
    for copy in copies:
        copy.start()
    for copy in copies:
        copy.wait()


def place(at, blocks, ring):
    depth, cols = blocks[0].shape
    return pl.pallas_call(
        functools.partial(place_kernel, ring, depth),
        in_specs=[pl.BlockSpec(memory_space=pltpu.SMEM)]
        + [pl.BlockSpec(memory_space=pl.ANY)] * (2 * ring),
        grid=(1,),
        out_specs=pl.BlockSpec((2 * ring * depth, cols), lambda i: (0, 0)),
        out_shape=jax.ShapeDtypeStruct((2 * ring * depth, cols), LOW),
        scratch_shapes=[pltpu.SemaphoreType.DMA((2 * ring,))],
        compiler_params=pltpu.CompilerParams(vmem_limit_bytes=24 * 2**20),
        cost_estimate=FREE,
        name="place",
    )(at, *blocks)


def product_kernel(tiles, left_ref, *refs):
    for k, right in enumerate(refs[:-1]):

        @pl.when(pl.program_id(0) // tiles == k)
        def _(right=right):
            refs[-1][...] = jnp.dot(
                left_ref[...], right[...], preferred_element_type=F32
            ).astype(LOW)


def product(left, rights):
    depth, length = left.shape
    cols = rights[0].shape[1]
    tile = 256 if cols % 256 == 0 else 128
    tiles = cols // tile
    return pl.pallas_call(
        functools.partial(product_kernel, tiles),
        grid=(tiles * len(rights),),
        in_specs=[pl.BlockSpec((depth, length), lambda i: (0, 0))]
        + [
            pl.BlockSpec((length, tile), lambda i, k=k: (0, jnp.clip(i - k * tiles, 0, tiles - 1)))
            for k in range(len(rights))
        ],
        out_specs=pl.BlockSpec((depth, tile), lambda i: (0, i)),
        out_shape=jax.ShapeDtypeStruct((depth, cols * len(rights)), LOW),
        compiler_params=pltpu.CompilerParams(vmem_limit_bytes=32 * 2**20),
        cost_estimate=FREE,
        name="product",
    )(left, *rights)


def attn_products_kernel(*refs):
    lefts, rights, out_ref = refs[:2], refs[2:4], refs[4]
    first = 0
    for left, right in zip(lefts, rights):
        cols = right.shape[1]
        out_ref[:, first : first + cols] = jnp.dot(
            left[...], right[...], preferred_element_type=F32
        ).astype(LOW)
        first += cols


def attn_products(lefts, rights):
    depth = lefts[0].shape[0]
    tiles = 4
    part = lambda a: pl.BlockSpec((depth // tiles, a.shape[1]), lambda i: (i, 0))
    whole = lambda a: pl.BlockSpec(a.shape, lambda i: (0, 0))
    shape = jax.ShapeDtypeStruct((depth, sum(a.shape[1] for a in rights)), LOW)
    return pl.pallas_call(
        attn_products_kernel,
        grid=(tiles,),
        in_specs=[part(a) for a in lefts] + [whole(a) for a in rights],
        out_specs=part(shape),
        out_shape=shape,
        compiler_params=pltpu.CompilerParams(vmem_limit_bytes=40 * 2**20),
        cost_estimate=FREE,
        name="attn_products",
    )(*lefts, *rights)


def back_parts_kernel(rows, count, *refs):
    total = sum(kdot(refs[k][...], refs[count + k][0], NT) for k in range(count))
    for j, out_ref in enumerate(refs[2 * count :]):
        out_ref[...] = total[j * rows : (j + 1) * rows].astype(LOW)


def back_parts(lefts, weights, which, ranks):
    length, cols = lefts[0].shape
    width = weights.shape[1]
    rows = length // ranks
    tile = 256
    return pl.pallas_call(
        functools.partial(back_parts_kernel, rows, len(lefts)),
        grid=(width // tile,),
        in_specs=[pl.BlockSpec((length, cols), lambda i: (0, 0))] * len(lefts)
        + [pl.BlockSpec((1, tile, cols), lambda i, k=k: (k, i, 0)) for k in which],
        out_specs=[pl.BlockSpec((rows, tile), lambda i: (0, i))] * ranks,
        out_shape=[jax.ShapeDtypeStruct((rows, width), LOW)] * ranks,
        compiler_params=pltpu.CompilerParams(vmem_limit_bytes=40 * 2**20),
        cost_estimate=FREE,
        name="back_parts",
    )(*lefts, *([weights] * len(which)))


def join_kernel(flows, at_ref, *refs):
    total = refs[flows][...].astype(F32) + refs[flows + 1][...].astype(F32)
    if flows:
        total = total + refs[0][...].astype(F32)
    refs[-1][...] = total.astype(refs[-1].dtype)


def join(owner, flow, near, other, ring, dtype):
    depth, cols = near.shape[0] // ring, near.shape[1]
    flows = [] if flow is None else [flow]
    half = cols // 2 if cols % 256 == 0 else cols
    row = pl.BlockSpec((depth, half), lambda i, at: (0, i))
    chosen = pl.BlockSpec((depth, half), lambda i, at: (at[0], i))
    return pl.pallas_call(
        functools.partial(join_kernel, len(flows)),
        grid_spec=pltpu.PrefetchScalarGridSpec(
            num_scalar_prefetch=1,
            grid=(cols // half,),
            in_specs=[row] * len(flows) + [chosen] * 2,
            out_specs=row,
        ),
        out_shape=jax.ShapeDtypeStruct((depth, cols), dtype),
        compiler_params=pltpu.CompilerParams(vmem_limit_bytes=24 * 2**20),
        cost_estimate=FREE,
        name="join",
    )(owner.astype(jnp.int32).reshape(1), *flows, near, other)


def sum_kernel(count, base_ref, *refs):
    total = base_ref[...].astype(F32)
    arrived = refs[0][...].astype(F32)
    for ref in refs[1:count]:
        arrived = arrived + ref[...].astype(F32)
    total = total + arrived
    refs[-1 if len(refs) == count + 1 else -2][...] = total
    if len(refs) > count + 1:
        gain_ref = refs[count]
        inverse = lax.rsqrt(jnp.mean(total * total, axis=-1, keepdims=True) + EPSILON)
        refs[-1][...] = (total * inverse * gain_ref[...]).astype(LOW)


def sum_up(base, parts, gain=None):
    rows, width = base.shape
    step = rows // 2
    by_row = pl.BlockSpec((step, width), lambda i: (i, 0))
    gains = [] if gain is None else [gain.reshape(1, -1)]
    outs = [jax.ShapeDtypeStruct((rows, width), F32)]
    if gains:
        outs.append(jax.ShapeDtypeStruct((rows, width), LOW))
    return pl.pallas_call(
        functools.partial(sum_kernel, len(parts)),
        grid=(2,),
        in_specs=[by_row] * (1 + len(parts)) + [pl.BlockSpec((1, width), lambda i: (0, 0))] * len(gains),
        out_specs=[by_row] * len(outs),
        out_shape=outs,
        compiler_params=pltpu.CompilerParams(vmem_limit_bytes=24 * 2**20),
        cost_estimate=FREE,
        name="sum_up",
    )(base, *parts, *gains)


def norm_back_kernel(count, value_ref, gain_ref, rest_ref, *refs):
    parts, outs = refs[:count], refs[count:]
    value = value_ref[...].astype(F32)
    grad = parts[0][...].astype(F32)
    for ref in parts[1:]:
        grad = grad + ref[...].astype(F32)
    inverse = lax.rsqrt(jnp.mean(value * value, axis=-1, keepdims=True) + EPSILON)
    hat = value * inverse
    scaled = grad * gain_ref[...]
    inner = jnp.mean(scaled * hat, axis=-1, keepdims=True)
    total = rest_ref[...].astype(F32) + (scaled - hat * inner) * inverse
    outs[0][...] = total
    if len(outs) > 1:
        outs[1][...] = total.astype(LOW)

        @pl.when(pl.program_id(0) == 0)
        def _():
            outs[2][...] = jnp.zeros_like(outs[2])

        outs[2][...] += jnp.sum(grad * hat, axis=0, keepdims=True)


def norm_back_sum(value, gain, rest, parts, more):
    rows, width = value.shape
    step = rows // 2
    by_row = pl.BlockSpec((step, width), lambda i: (i, 0))
    fixed = pl.BlockSpec((1, width), lambda i: (0, 0))
    shapes = [jax.ShapeDtypeStruct((rows, width), F32)]
    if more:
        shapes += [jax.ShapeDtypeStruct((rows, width), LOW), jax.ShapeDtypeStruct((1, width), F32)]
    return pl.pallas_call(
        functools.partial(norm_back_kernel, len(parts)),
        grid=(2,),
        in_specs=[by_row, fixed, by_row] + [by_row] * len(parts),
        out_specs=[by_row, by_row, fixed][: len(shapes)],
        out_shape=shapes,
        compiler_params=pltpu.CompilerParams(vmem_limit_bytes=24 * 2**20),
        cost_estimate=FREE,
        name="norm_back_sum",
    )(value, gain.reshape(1, -1), rest, *parts)


def rows_product_kernel(left_ref, right_ref, out_ref):
    out_ref[...] = jnp.dot(left_ref[...], right_ref[...], preferred_element_type=F32).astype(LOW)


def rows_product(left, right, ranks):
    length, depth = left.shape
    rows = length // ranks
    return pl.pallas_call(
        rows_product_kernel,
        grid=(ranks,),
        in_specs=[
            pl.BlockSpec((rows, depth), lambda i: (i, 0)),
            pl.BlockSpec(right.shape, lambda i: (0, 0)),
        ],
        out_specs=pl.BlockSpec((rows, right.shape[1]), lambda i: (i, 0)),
        out_shape=jax.ShapeDtypeStruct((length, right.shape[1]), LOW),
        compiler_params=pltpu.CompilerParams(vmem_limit_bytes=24 * 2**20),
        cost_estimate=FREE,
        name="rows_product",
    )(left, right)


def gain_part_kernel(normed_ref, gain_ref, *refs):
    rows = refs[0].shape[0]
    total = jnp.zeros(refs[-1].shape, F32)
    for j, ref in enumerate(refs[:-1]):
        block = normed_ref[j * rows : (j + 1) * rows, :].astype(F32)
        total = total + jnp.sum(block * ref[...].astype(F32), axis=0, keepdims=True)
    refs[-1][...] = total / gain_ref[...]


def gain_part(normed, gain, parts):
    width = normed.shape[1]
    tile = 512
    column = lambda a: pl.BlockSpec((a.shape[0], tile), lambda i: (0, i))
    row = gain.reshape(1, -1)
    return pl.pallas_call(
        gain_part_kernel,
        grid=(width // tile,),
        in_specs=[column(normed), column(row)] + [column(part) for part in parts],
        out_specs=column(row),
        out_shape=jax.ShapeDtypeStruct((1, width), F32),
        compiler_params=pltpu.CompilerParams(vmem_limit_bytes=24 * 2**20),
        cost_estimate=FREE,
        name="gain_part",
    )(normed, row, *parts)


def group_mean(values):
    width = values.shape[1]
    part = 2 * HEAD_SIZE
    left = lax.broadcasted_iota(jnp.int32, (part, part), 0) // HEAD_SIZE
    right = lax.broadcasted_iota(jnp.int32, (part, part), 1) // HEAD_SIZE
    spread = jnp.where(left == right, 1.0 / HEAD_SIZE, 0.0).astype(F32)
    pieces = []
    for first in range(0, width, part):
        size = min(part, width - first)
        pieces.append(
            lax.dot_general(
                values[:, first : first + size],
                spread[:size, :size],
                NN,
                precision=lax.Precision.HIGHEST,
                preferred_element_type=F32,
            )
        )
    return jnp.concatenate(pieces, axis=1) if len(pieces) > 1 else pieces[0]


def across(table, width):
    part = table.shape[1]
    if width < part:
        return table[:, :width]
    return jnp.concatenate([table] * (width // part) + ([table[:, : width % part]] if width % part else []), axis=1)


def partner(values):
    width = values.shape[1]
    half = HEAD_SIZE // 2
    lane = lax.broadcasted_iota(jnp.int32, values.shape, 1) % HEAD_SIZE
    return jnp.where(lane < half, pltpu.roll(values, width - half, 1), pltpu.roll(values, half, 1))


def prepare_kernel(q_cols, kv_cols, x_ref, w_ref, cos_ref, sin_ref, gain_ref, q_ref, k_ref, v_ref, raw_ref):
    product = jnp.dot(x_ref[...], w_ref[...], preferred_element_type=F32)
    for first, cols, to in ((0, q_cols, q_ref), (q_cols, kv_cols, k_ref)):
        raw = product[:, first : first + cols]
        scaled = raw * lax.rsqrt(group_mean(raw * raw) + EPSILON) * gain_ref[:, first : first + cols]
        cos = across(cos_ref[...], cols)
        sin = across(sin_ref[...], cols)
        to[...] = (scaled * cos + partner(scaled) * sin).astype(LOW)
        raw_ref[:, first : first + cols] = raw
    v_ref[...] = product[:, q_cols + kv_cols :].astype(LOW)


def prepare(normed, weight, cosine, sine, gains, q_cols, kv_cols, ranks):
    length, width = normed.shape
    rows = length // ranks
    at_row = lambda i: (i, 0)
    fixed = lambda i: (0, 0)
    return pl.pallas_call(
        functools.partial(prepare_kernel, q_cols, kv_cols),
        grid=(ranks,),
        in_specs=[
            pl.BlockSpec((rows, width), at_row),
            pl.BlockSpec(weight.shape, fixed),
            pl.BlockSpec((rows, cosine.shape[1]), at_row),
            pl.BlockSpec((rows, cosine.shape[1]), at_row),
            pl.BlockSpec((1, q_cols + kv_cols), fixed),
        ],
        out_specs=[
            pl.BlockSpec((rows, q_cols), at_row),
            pl.BlockSpec((rows, kv_cols), at_row),
            pl.BlockSpec((rows, kv_cols), at_row),
            pl.BlockSpec((rows, q_cols + kv_cols), at_row),
        ],
        out_shape=[
            jax.ShapeDtypeStruct((length, q_cols), LOW),
            jax.ShapeDtypeStruct((length, kv_cols), LOW),
            jax.ShapeDtypeStruct((length, kv_cols), LOW),
            jax.ShapeDtypeStruct((length, q_cols + kv_cols), F32),
        ],
        compiler_params=pltpu.CompilerParams(vmem_limit_bytes=40 * 2**20),
        cost_estimate=FREE,
        name="prepare",
    )(normed, weight, cosine, sine, gains)


def prepare_back_kernel(
    q_cols, kv_cols, dq_ref, dk_ref, dv_ref, raw_ref, cos_ref, sin_ref, gain_ref, out_ref, gain_grad_ref
):
    @pl.when(pl.program_id(0) == 0)
    def _():
        gain_grad_ref[...] = jnp.zeros_like(gain_grad_ref)

    for first, cols, grad_ref in ((0, q_cols, dq_ref), (q_cols, kv_cols, dk_ref)):
        span = slice(first, first + cols)
        grad = grad_ref[...]
        turned = grad * across(cos_ref[...], cols) - partner(grad) * across(sin_ref[...], cols)
        raw = raw_ref[:, span]
        inverse = lax.rsqrt(group_mean(raw * raw) + EPSILON)
        hat = raw * inverse
        gain_grad_ref[:, span] += jnp.sum(turned * hat, axis=0, keepdims=True)
        scaled = turned * gain_ref[:, span]
        out_ref[:, span] = ((scaled - hat * group_mean(scaled * hat)) * inverse).astype(LOW)
    out_ref[:, q_cols + kv_cols :] = dv_ref[...].astype(LOW)


def prepare_back(d_queries, d_keys, d_values, raw, cosine, sine, gains, ranks):
    length, q_cols = d_queries.shape
    kv_cols = d_keys.shape[1]
    rows = length // ranks
    at_row = lambda i: (i, 0)
    fixed = lambda i: (0, 0)
    return pl.pallas_call(
        functools.partial(prepare_back_kernel, q_cols, kv_cols),
        grid=(ranks,),
        in_specs=[
            pl.BlockSpec((rows, q_cols), at_row),
            pl.BlockSpec((rows, kv_cols), at_row),
            pl.BlockSpec((rows, kv_cols), at_row),
            pl.BlockSpec((rows, q_cols + kv_cols), at_row),
            pl.BlockSpec((rows, cosine.shape[1]), at_row),
            pl.BlockSpec((rows, cosine.shape[1]), at_row),
            pl.BlockSpec((1, q_cols + kv_cols), fixed),
        ],
        out_specs=[
            pl.BlockSpec((rows, q_cols + 2 * kv_cols), at_row),
            pl.BlockSpec((1, q_cols + kv_cols), fixed),
        ],
        out_shape=[
            jax.ShapeDtypeStruct((length, q_cols + 2 * kv_cols), LOW),
            jax.ShapeDtypeStruct((1, q_cols + kv_cols), F32),
        ],
        compiler_params=pltpu.CompilerParams(vmem_limit_bytes=40 * 2**20),
        cost_estimate=FREE,
        name="prepare_back",
    )(d_queries, d_keys, d_values, raw, cosine, sine, gains)


def shards(
    dp_size,
    ranks,
    tokens,
    segments,
    attn_gain,
    w_query,
    key_weight,
    value_weight,
    query_gain,
    key_gain,
    w_out,
    ffn_gain,
    w_gate,
    w_up,
    w_down,
    cotangent,
):
    ring = dp_size // 2
    index = lax.axis_index("dp")
    stage = index // 2
    core = index % 2
    me = lax.axis_index("tensor")
    swap_pairs = [(i, i ^ 1) for i in range(dp_size)]
    ring_pairs = [(i, (i + 2) % dp_size) for i in range(dp_size)]
    heads = KEY_VALUE_HEADS // ranks
    rows = tokens.shape[0]
    length = segments.shape[0]
    q_cols = w_query.shape[1]
    kv_cols = key_weight.shape[1]

    hidden_cols = w_gate.shape[1]
    hidden_pad = -hidden_cols % 128

    def widen(weight):
        return jnp.pad(weight, ((0, 0), (0, hidden_pad)))

    def swap(v):
        return lax.ppermute(v, "dp", swap_pairs)

    def onward(v):
        return lax.ppermute(v, "dp", ring_pairs)

    core_array = core.astype(jnp.int32).reshape(1)
    at = jnp.stack([stage, core]).astype(jnp.int32)

    def ring_gather(label, block):
        blocks = []
        for hop in range(ring):
            with jax.named_scope(f"{label}_swap{hop}"):
                blocks += [block, swap(block)]
            if hop < ring - 1:
                with jax.named_scope(f"{label}_hop{hop + 1}"):
                    block = onward(block)
        return blocks

    def hop(label, block):
        with jax.named_scope(label):
            return onward(block)

    def owner_after(count):
        return lax.rem(stage - 1 - count + 2 * ring, ring)

    def spread(label, block):
        with jax.named_scope(label):
            return [block] + [
                lax.ppermute(block, "tensor", [(i, i ^ j) for i in range(ranks)])
                for j in range(1, ranks)
            ]

    def send_parts(label, parts):
        with jax.named_scope(label):
            return [
                lax.ppermute(parts[j], "tensor", [(i, i ^ j) for i in range(ranks)])
                for j in range(1, ranks)
            ]

    def add_up(own, arrived):
        total = own.astype(F32)
        for piece in arrived:
            total = total + piece.astype(F32)
        return total

    def cut(matrix):
        return [matrix[j * rows : (j + 1) * rows] for j in range(ranks)]

    def tie(value, *others):
        return lax.optimization_barrier((value,) + others)[0]

    tokens_wide = tokens.astype(F32)
    normed_own = norm_rows(tokens_wide, attn_gain).astype(LOW)
    normed_one = spread("one_spread", normed_own)
    a_blocks = ring_gather("attn", jnp.concatenate([w_query, key_weight, value_weight, w_out.T], axis=1))
    ffn_full = lax.all_gather(
        jnp.stack([widen(w_down.T), widen(w_gate), widen(w_up)]), "dp", axis=1, tiled=True
    )
    grad_blocks = spread("cot_spread", tie(cotangent, *normed_one))
    wide = hidden_cols + hidden_pad
    down_t, gate_full, up_full = ffn_full[0], ffn_full[1], ffn_full[2]

    first_start = jnp.sum((segments < 1).astype(jnp.int32))
    second_start = jnp.sum((segments < 2).astype(jnp.int32))
    ids = jnp.arange(length, dtype=jnp.int32).reshape(ranks, rows)
    begins = jnp.where(segments == 0, 0, jnp.where(segments == 1, first_start, second_start))
    begins = begins.astype(jnp.int32).reshape(ranks, rows)
    order = [me ^ j for j in range(ranks)]
    bounds = jnp.stack([lax.dynamic_index_in_dim(begins, o, 0, keepdims=False) for o in order])
    here = jnp.stack([lax.dynamic_index_in_dim(ids, o, 0, keepdims=False) for o in order])
    positions = (here - bounds).reshape(length).astype(F32)
    bounds = bounds.reshape(ranks, 1, rows)
    half = HEAD_SIZE // 2
    freqs = ROTARY_BASE ** (-2.0 * jnp.arange(half, dtype=F32) / HEAD_SIZE)
    angles = positions[:, None] * jnp.concatenate([freqs] * 4)[None, :]
    signs = jnp.concatenate([-jnp.ones(half, F32), jnp.ones(half, F32)] * 2)
    cosine = jnp.cos(angles)
    sine = jnp.sin(angles) * signs[None, :]
    head_gains = jnp.concatenate(
        [query_gain] * (q_cols // HEAD_SIZE) + [key_gain] * (kv_cols // HEAD_SIZE)
    ).reshape(1, -1)

    normed_all, normed_one_t = fold(core_array, normed_one, ring)
    a_blocks[-2] = tie(a_blocks[-2], normed_all, cosine, sine)
    attn_full = place(at, a_blocks, ring)
    w_qkv = attn_full[:, : q_cols + 2 * kv_cols]
    out_t = attn_full[:, q_cols + 2 * kv_cols :]
    query_low, key_low, value_low, raw = prepare(
        normed_all, w_qkv, cosine, sine, head_gains, q_cols, kv_cols, ranks
    )
    me_array = me.astype(jnp.int32).reshape(1)
    attended, lse = attend(me_array, query_low, key_low, value_low, bounds, ranks, heads)

    attended_go = tie(attended, *grad_blocks)
    attn_parts = back_parts([attended_go], out_t[None], (0,), ranks)
    attn_arrived = send_parts("attn_sum", attn_parts)
    grad_all, *grad_pair = fold(
        core_array, [tie(grad_blocks[0], *attn_parts)] + grad_blocks[1:], ring, True
    )
    attn_arrived[0] = tie(attn_arrived[0], grad_all)
    hidden, normed_two_own = sum_up(tokens, [attn_parts[0]] + attn_arrived, ffn_gain)
    normed_two = spread("two_spread", normed_two_own)
    d_activation = mm(grad_all, down_t).astype(LOW)
    normed_two[-1] = tie(normed_two[-1], d_activation)
    normed_two_all, *normed_two_pair = fold(core_array, normed_two, ring, True)

    gating = mm(normed_two_all, gate_full).astype(LOW).astype(F32)
    lifted = mm(normed_two_all, up_full)
    gate_sig = jax.nn.sigmoid(gating)
    silu = gating * gate_sig
    activation = (silu * lifted).astype(LOW)
    d_act_wide = d_activation.astype(F32)
    d_gating = (d_act_wide * lifted * gate_sig * (1.0 + gating * (1.0 - gate_sig))).astype(LOW)
    d_lifted = (d_act_wide * silu).astype(LOW)

    last = ring - 1

    def advance(label, flow, near, other, count):
        if count == last:
            return join(owner_after(count), flow, near, other, ring, F32), None
        block = join(owner_after(count), flow, near, other, ring, LOW)
        return block, hop(f"{label}_hop{count + 1}", block)

    def several(label, block, flow, near, other, first, end, *after):
        for count in range(first, end):
            block, flow = advance(label, tie(flow, *after), near, other, count)
        return block, flow

    down_far = product(grad_pair[0], [activation])
    down_other = swap(down_far)
    down_near = product(grad_pair[1], [tie(activation, down_far)])
    down_block, down_flow = advance("down_grad", None, down_near, down_other, 0)
    both_far = product(normed_two_pair[0], [tie(d_gating, down_block), d_lifted])
    both_other = swap(both_far)
    both_near = product(normed_two_pair[1], [tie(d_gating, both_far), d_lifted])
    two_parts = back_parts([tie(d_gating, both_near), d_lifted], ffn_full, (1, 2), ranks)
    down_block, down_flow = advance("down_grad", tie(down_flow, *two_parts), down_near, down_other, 1)
    two_go = lax.optimization_barrier(tuple(two_parts) + (down_block,))[:-1]
    two_arrived = send_parts("two_sum", two_go)
    both_block, both_flow = advance("both_grad", None, tie(both_near, *two_go), both_other, 0)
    ffn_parts = back_parts([tie(activation, both_block)], ffn_full, (0,), ranks)
    two_arrived = list(lax.optimization_barrier(tuple(two_arrived) + (ffn_parts[0],))[:-1])
    d_hidden, d_hidden_low, ffn_gain_part = norm_back_sum(
        hidden, ffn_gain, cotangent, [two_parts[0]] + two_arrived, True
    )
    hidden_grad = spread("dh_spread", d_hidden_low)
    down_block, down_flow = several(
        "down_grad", down_block, down_flow, down_near, down_other, 2, last, hidden_grad[1]
    )
    both_block, both_flow = several(
        "both_grad", both_block, both_flow, both_near, both_other, 1, last - 1, hidden_grad[1], down_block
    )
    hidden_grad[-1] = tie(hidden_grad[-1], both_block)
    hidden_grad_all, hidden_grad_t = fold(core_array, hidden_grad, ring)
    ffn_go = lax.optimization_barrier(tuple(ffn_parts) + tuple(hidden_grad))[:ranks]
    ffn_arrived = send_parts("ffn_sum", ffn_go)
    d_attended = rows_product(hidden_grad_all, out_t, ranks)
    d_queries, d_keys, d_values = attend_back(
        me_array, query_low, key_low, value_low, bounds, attended, d_attended, lse, ranks, heads
    )
    d_raw, head_gain_parts = prepare_back(
        d_queries, d_keys, d_values, raw, cosine, sine, head_gains, ranks
    )
    down_grad, _ = advance("down_grad", tie(down_flow, *ffn_arrived), down_near, down_other, last)
    both_block, both_flow = advance(
        "both_grad", tie(both_flow, down_grad), both_near, both_other, last - 1
    )
    one_parts = back_parts([tie(d_raw, both_block, *ffn_arrived)], w_qkv[None], (0,), ranks)
    one_arrived = send_parts("one_sum", one_parts)
    attn_full_grad = attn_products([normed_one_t, hidden_grad_t], [tie(d_raw, *one_parts), attended])
    attn_grad = lax.psum_scatter(attn_full_grad, "dp", scatter_dimension=0, tiled=True).astype(F32)
    attn_gain_part = gain_part(tie(normed_all, attn_full_grad), attn_gain, one_parts).reshape(-1)
    (output,) = sum_up(tie(hidden, attn_gain_part), [ffn_parts[0]] + ffn_arrived)
    one_arrived[-1] = tie(one_arrived[-1], output)
    (tokens_grad,) = norm_back_sum(tokens, attn_gain, d_hidden, [one_parts[0]] + one_arrived, False)
    both_grad, _ = advance("both_grad", tie(both_flow, tokens_grad), both_near, both_other, last)
    qkv_cols = q_cols + 2 * kv_cols
    qkv_grad = attn_grad[:, :qkv_cols]
    out_grad = attn_grad[:, qkv_cols:]
    down_grad = down_grad[:, :hidden_cols]
    gate_grad = both_grad[:, :hidden_cols]
    lift_grad = both_grad[:, wide : wide + hidden_cols]

    head_gain_parts = head_gain_parts.reshape(-1, HEAD_SIZE)
    query_gain_part = jnp.sum(head_gain_parts[: q_cols // HEAD_SIZE], axis=0)
    key_gain_part = jnp.sum(head_gain_parts[q_cols // HEAD_SIZE :], axis=0)
    sizes = [attn_gain.shape[0], ffn_gain.shape[0], HEAD_SIZE, HEAD_SIZE]
    gains = jnp.concatenate([attn_gain_part, ffn_gain_part.reshape(-1), query_gain_part, key_gain_part])
    gains = gains.reshape(1, -1)
    total = gains
    span = 1
    while span < ranks:
        total = total + lax.ppermute(total, "tensor", [(i, i ^ span) for i in range(ranks)])
        span *= 2
    total = tie(total, both_grad, tokens_grad)
    span = 1
    while span < dp_size:
        total = total + lax.ppermute(total, "dp", [(i, i ^ span) for i in range(dp_size)])
        span *= 2
    total = total.reshape(-1)
    a, b = sizes[0], sizes[0] + sizes[1]
    return (
        output,
        tokens_grad,
        total[:a],
        qkv_grad[:, :q_cols],
        qkv_grad[:, q_cols : q_cols + kv_cols],
        qkv_grad[:, q_cols + kv_cols :],
        total[b : b + HEAD_SIZE],
        total[b + HEAD_SIZE :],
        out_grad.T,
        total[a:b],
        gate_grad,
        lift_grad,
        down_grad.T,
    )


def solution(mesh):
    in_specs = (
        P(("dp", "tensor"), None),
        P("dp"),
        P(),
        P("dp", "tensor"),
        P("dp", "tensor"),
        P("dp", "tensor"),
        P(),
        P(),
        P("tensor", "dp"),
        P(),
        P("dp", "tensor"),
        P("dp", "tensor"),
        P("tensor", "dp"),
        P(("dp", "tensor"), None),
    )
    out_specs = (
        P(("dp", "tensor"), None),
        P(("dp", "tensor"), None),
        P(),
        P("dp", "tensor"),
        P("dp", "tensor"),
        P("dp", "tensor"),
        P(),
        P(),
        P("tensor", "dp"),
        P(),
        P("dp", "tensor"),
        P("dp", "tensor"),
        P("tensor", "dp"),
    )
    body = functools.partial(shards, mesh.shape["dp"], mesh.shape["tensor"])
    return jax.shard_map(body, mesh=mesh, in_specs=in_specs, out_specs=out_specs, check_vma=False)
```

```python
import functools

import jax
import jax.numpy as jnp
from jax import lax
from jax.experimental import pallas as pl
from jax.experimental.pallas import tpu as pltpu
from jax.sharding import PartitionSpec as P

QUERY_HEADS = 24
KEY_VALUE_HEADS = 8
HEAD_SIZE = 64
GROUP = QUERY_HEADS // KEY_VALUE_HEADS
EPSILON = 1e-05
ROTARY_BASE = 1000000.0
NEGATIVE_FILL = -1e30
F32 = jnp.float32
LOW = jnp.bfloat16
SCALE = HEAD_SIZE ** (-0.5)
FREE = pl.CostEstimate(flops=0, bytes_accessed=0, transcendentals=0)


def norm_rows(values_in, gain):
    return (
        values_in
        * lax.rsqrt(jnp.mean(values_in * values_in, axis=-1, keepdims=True) + EPSILON)
        * gain
    )


def norm_back(values, gain, grad):
    inverse = lax.rsqrt(jnp.mean(values * values, axis=-1, keepdims=True) + EPSILON)
    hat = values * inverse
    scaled = grad * gain
    inner = jnp.mean(scaled * hat, axis=-1, keepdims=True)
    return (scaled - hat * inner) * inverse, jnp.sum(grad * hat, axis=0)


def mm(left, right):
    return jnp.dot(left, right, preferred_element_type=F32)


def cross_rows(left, right):
    return lax.dot_general(left, right, (((1,), (1,)), ((), ())), preferred_element_type=F32)


def cross_cols(left, right):
    return lax.dot_general(left, right, (((0,), (0,)), ((), ())), preferred_element_type=F32)


NT = (((1,), (1,)), ((), ()))
NN = (((1,), (0,)), ((), ()))
TN = (((0,), (0,)), ((), ()))


def kdot(left, right, dims):
    return lax.dot_general(left, right, dims, preferred_element_type=F32)


def stack_heads(block, head):
    first = head * GROUP * HEAD_SIZE
    return jnp.concatenate(
        [block[:, first + g * HEAD_SIZE : first + (g + 1) * HEAD_SIZE] for g in range(GROUP)], axis=0
    )


def attend_kernel(heads, rows, me_ref, q_ref, k_ref, v_ref, lo_ref, out_ref, lse_ref):
    me = me_ref[0]
    block = pl.program_id(0) ^ me
    low_bound = jnp.concatenate([lo_ref[0]] * GROUP, axis=1)
    row_ids = block * rows + lax.broadcasted_iota(jnp.int32, (1, rows), 1)
    row_ids = jnp.concatenate([row_ids] * GROUP, axis=1)
    width = GROUP * rows
    queries = q_ref[...] * SCALE
    pieces = []
    for head in range(heads):
        q3 = stack_heads(queries, head)
        cols = slice(head * HEAD_SIZE, (head + 1) * HEAD_SIZE)

        def step(other, carry, q3=q3, cols=cols):
            peak, total, acc = carry
            first = pl.multiple_of((other ^ me) * rows, rows)
            keys = k_ref[pl.ds(first, rows), cols]
            vals = v_ref[pl.ds(first, rows), cols]
            ids = other * rows + lax.broadcasted_iota(jnp.int32, (rows, 1), 0)
            scores = kdot(keys, q3, NT)
            scores = jnp.where((ids <= row_ids) & (ids >= low_bound), scores, NEGATIVE_FILL)
            higher = jnp.maximum(peak, jnp.max(scores, axis=0, keepdims=True))
            fade = jnp.exp(peak - higher)
            exps = jnp.exp(scores - higher)
            total = total * fade + jnp.sum(exps, axis=0, keepdims=True)
            acc = acc * fade + kdot(vals, exps.astype(LOW), TN)
            return higher, total, acc

        start = (
            jnp.full((1, width), NEGATIVE_FILL, F32),
            jnp.zeros((1, width), F32),
            jnp.zeros((HEAD_SIZE, width), F32),
        )
        start = step(block, start)
        peak, total, acc = lax.fori_loop(0, block, step, start)
        acc = acc / total
        lse_ref[0, head : head + 1, :] = peak + jnp.log(total)
        pieces += [acc[:, g * rows : (g + 1) * rows] for g in range(GROUP)]
    out_ref[...] = jnp.concatenate(pieces, axis=0).T.astype(LOW)


def attend_back_kernel(
    heads, rows, me_ref, q_ref, k_ref, v_ref, lo_ref, o_ref, do_ref, lse_ref, dq_ref, dk_ref, dv_ref
):
    me = me_ref[0]

    @pl.when(pl.program_id(0) == 0)
    def _():
        dk_ref[...] = jnp.zeros_like(dk_ref)
        dv_ref[...] = jnp.zeros_like(dv_ref)

    block = pl.program_id(0) ^ me
    low_bound = jnp.concatenate([lo_ref[0]] * GROUP, axis=1)
    row_ids = block * rows + lax.broadcasted_iota(jnp.int32, (1, rows), 1)
    row_ids = jnp.concatenate([row_ids] * GROUP, axis=1)
    width = GROUP * rows
    queries = q_ref[...] * SCALE
    grads = do_ref[...]
    product = (grads.astype(F32) * o_ref[...].astype(F32)).T
    pieces = []
    for head in range(heads):
        q3 = stack_heads(queries, head)
        do3 = stack_heads(grads, head)
        cols = slice(head * HEAD_SIZE, (head + 1) * HEAD_SIZE)
        first_row = head * GROUP * HEAD_SIZE
        inner = jnp.concatenate(
            [
                jnp.sum(
                    product[first_row + g * HEAD_SIZE : first_row + (g + 1) * HEAD_SIZE],
                    axis=0,
                    keepdims=True,
                )
                for g in range(GROUP)
            ],
            axis=1,
        )
        lse = lse_ref[0, head : head + 1, :]

        def step(other, acc, q3=q3, do3=do3, cols=cols, inner=inner, lse=lse):
            first = pl.multiple_of((other ^ me) * rows, rows)
            place = pl.ds(first, rows)
            keys = k_ref[place, cols]
            vals = v_ref[place, cols]
            ids = other * rows + lax.broadcasted_iota(jnp.int32, (rows, 1), 0)
            scores = kdot(keys, q3, NT)
            scores = jnp.where((ids <= row_ids) & (ids >= low_bound), scores, NEGATIVE_FILL)
            probs = jnp.exp(scores - lse)
            d_probs = kdot(vals, do3, NT)
            d_scores = (probs * (d_probs - inner)).astype(LOW)
            dk_ref[place, cols] += kdot(d_scores, q3, NN)
            dv_ref[place, cols] += kdot(probs.astype(LOW), do3, NN)
            return acc + kdot(keys, d_scores, TN)

        acc = lax.fori_loop(0, block + 1, step, jnp.zeros((HEAD_SIZE, width), F32))
        pieces += [acc[:, g * rows : (g + 1) * rows] for g in range(GROUP)]
    dq_ref[...] = jnp.concatenate(pieces, axis=0).T * SCALE


def attention_specs(ranks, rows, heads):
    length = ranks * rows
    q_spec = pl.BlockSpec((rows, heads * GROUP * HEAD_SIZE), lambda i, me: (i, 0))
    kv_spec = pl.BlockSpec((length, heads * HEAD_SIZE), lambda i, me: (0, 0))
    lo_spec = pl.BlockSpec((1, 1, rows), lambda i, me: (i, 0, 0))
    lse_spec = pl.BlockSpec((1, heads, GROUP * rows), lambda i, me: (i, 0, 0))
    return q_spec, kv_spec, lo_spec, lse_spec


def attend(me, queries, keys, values, bounds, ranks, heads):
    length = queries.shape[0]
    rows = length // ranks
    q_spec, kv_spec, lo_spec, lse_spec = attention_specs(ranks, rows, heads)
    return pl.pallas_call(
        functools.partial(attend_kernel, heads, rows),
        grid_spec=pltpu.PrefetchScalarGridSpec(
            num_scalar_prefetch=1,
            grid=(ranks,),
            in_specs=[q_spec, kv_spec, kv_spec, lo_spec],
            out_specs=[q_spec, lse_spec],
        ),
        out_shape=[
            jax.ShapeDtypeStruct(queries.shape, LOW),
            jax.ShapeDtypeStruct((ranks, heads, GROUP * rows), F32),
        ],
        compiler_params=pltpu.CompilerParams(vmem_limit_bytes=48 * 2**20),
        cost_estimate=pl.CostEstimate(
            flops=16 * length * length * heads * GROUP * HEAD_SIZE,
            bytes_accessed=32 * 2**20,
            transcendentals=length * length * heads * GROUP,
        ),
        name="attend",
    )(me, queries, keys, values, bounds)


def attend_back(me, queries, keys, values, bounds, attended, d_attended, lse, ranks, heads):
    length = queries.shape[0]
    rows = length // ranks
    q_spec, kv_spec, lo_spec, lse_spec = attention_specs(ranks, rows, heads)
    return pl.pallas_call(
        functools.partial(attend_back_kernel, heads, rows),
        grid_spec=pltpu.PrefetchScalarGridSpec(
            num_scalar_prefetch=1,
            grid=(ranks,),
            in_specs=[q_spec, kv_spec, kv_spec, lo_spec, q_spec, q_spec, lse_spec],
            out_specs=[q_spec, kv_spec, kv_spec],
        ),
        out_shape=[
            jax.ShapeDtypeStruct(queries.shape, F32),
            jax.ShapeDtypeStruct(keys.shape, F32),
            jax.ShapeDtypeStruct(keys.shape, F32),
        ],
        compiler_params=pltpu.CompilerParams(vmem_limit_bytes=48 * 2**20),
        cost_estimate=FREE,
        name="attend_back",
    )(me, queries, keys, values, bounds, attended, d_attended, lse)


def fold_kernel(ranks, ring, rows, split, core_ref, *refs):
    blocks, all_ref, outs = refs[:ranks], refs[ranks], refs[ranks + 1 :]
    core = core_ref[0]
    turned = outs[-1]
    depth = turned.shape[0] // (2 * ring)
    for j in range(ranks):
        block = blocks[j][...]
        span = slice(j * rows, (j + 1) * rows)
        all_ref[span, :] = block
        if not split:
            turned[:, span] = block.T
            continue
        turned[...] = block.T
        for i in range(ring):
            to = slice(i * depth, (i + 1) * depth)
            for side_ref, side in zip(outs[:2], (1 - core, core)):
                first = pl.multiple_of((2 * i + side) * depth, 16)
                side_ref[to, span] = turned[pl.ds(first, depth), :]


def fold(core, blocks, ring, split=False):
    ranks = len(blocks)
    rows, width = blocks[0].shape
    length = ranks * rows
    whole = lambda shape: pl.BlockSpec(shape, lambda i: (0, 0))
    shapes = [(length, width)] + ([(width // 2, length)] * 2 if split else [(width, length)])
    return pl.pallas_call(
        functools.partial(fold_kernel, ranks, ring, rows, split),
        grid=(1,),
        in_specs=[pl.BlockSpec(memory_space=pltpu.SMEM)] + [whole((rows, width))] * ranks,
        out_specs=[whole(shape) for shape in shapes],
        out_shape=[jax.ShapeDtypeStruct(shape, LOW) for shape in shapes],
        scratch_shapes=[pltpu.VMEM((width, rows), LOW)] if split else [],
        compiler_params=pltpu.CompilerParams(vmem_limit_bytes=40 * 2**20),
        cost_estimate=FREE,
        name="fold",
    )(core, *blocks)


def place_kernel(ring, depth, at_ref, *refs):
    blocks = refs[: 2 * ring]
    full_ref, sems = refs[2 * ring :]
    stage, core = at_ref[0], at_ref[1]
    copies = []
    for hop in range(ring):
        owner = lax.rem(stage - hop + ring, ring)
        for half, side in enumerate((core, 1 - core)):
            first = pl.multiple_of((owner * 2 + side) * depth, 16)
            copies.append(
                pltpu.make_async_copy(
                    blocks[2 * hop + half], full_ref.at[pl.ds(first, depth)], sems.at[2 * hop + half]
                )
            )
    for copy in copies:
        copy.start()
    for copy in copies:
        copy.wait()


def place(at, blocks, ring):
    depth, cols = blocks[0].shape
    return pl.pallas_call(
        functools.partial(place_kernel, ring, depth),
        in_specs=[pl.BlockSpec(memory_space=pltpu.SMEM)]
        + [pl.BlockSpec(memory_space=pl.ANY)] * (2 * ring),
        grid=(1,),
        out_specs=pl.BlockSpec((2 * ring * depth, cols), lambda i: (0, 0)),
        out_shape=jax.ShapeDtypeStruct((2 * ring * depth, cols), LOW),
        scratch_shapes=[pltpu.SemaphoreType.DMA((2 * ring,))],
        compiler_params=pltpu.CompilerParams(vmem_limit_bytes=24 * 2**20),
        cost_estimate=FREE,
        name="place",
    )(at, *blocks)


def product_kernel(tiles, left_ref, *refs):
    for k, right in enumerate(refs[:-1]):

        @pl.when(pl.program_id(0) // tiles == k)
        def _(right=right):
            refs[-1][...] = jnp.dot(
                left_ref[...], right[...], preferred_element_type=F32
            ).astype(LOW)


def product(left, rights):
    depth, length = left.shape
    cols = rights[0].shape[1]
    tile = 256 if cols % 256 == 0 else 128
    tiles = cols // tile
    return pl.pallas_call(
        functools.partial(product_kernel, tiles),
        grid=(tiles * len(rights),),
        in_specs=[pl.BlockSpec((depth, length), lambda i: (0, 0))]
        + [
            pl.BlockSpec((length, tile), lambda i, k=k: (0, jnp.clip(i - k * tiles, 0, tiles - 1)))
            for k in range(len(rights))
        ],
        out_specs=pl.BlockSpec((depth, tile), lambda i: (0, i)),
        out_shape=jax.ShapeDtypeStruct((depth, cols * len(rights)), LOW),
        compiler_params=pltpu.CompilerParams(vmem_limit_bytes=40 * 2**20),
        cost_estimate=FREE,
        name="product",
    )(left, *rights)


def attn_products_kernel(*refs):
    lefts, rights, out_ref = refs[:2], refs[2:4], refs[4]
    first = 0
    for left, right in zip(lefts, rights):
        cols = right.shape[1]
        out_ref[:, first : first + cols] = jnp.dot(
            left[...], right[...], preferred_element_type=F32
        ).astype(LOW)
        first += cols


def attn_products(lefts, rights):
    depth = lefts[0].shape[0]
    tiles = 4
    part = lambda a: pl.BlockSpec((depth // tiles, a.shape[1]), lambda i: (i, 0))
    whole = lambda a: pl.BlockSpec(a.shape, lambda i: (0, 0))
    shape = jax.ShapeDtypeStruct((depth, sum(a.shape[1] for a in rights)), LOW)
    return pl.pallas_call(
        attn_products_kernel,
        grid=(tiles,),
        in_specs=[part(a) for a in lefts] + [whole(a) for a in rights],
        out_specs=part(shape),
        out_shape=shape,
        compiler_params=pltpu.CompilerParams(vmem_limit_bytes=40 * 2**20),
        cost_estimate=FREE,
        name="attn_products",
    )(*lefts, *rights)


def back_parts_kernel(rows, count, *refs):
    total = sum(kdot(refs[k][...], refs[count + k][0], NT) for k in range(count))
    for j, out_ref in enumerate(refs[2 * count :]):
        out_ref[...] = total[j * rows : (j + 1) * rows].astype(LOW)


def back_parts(lefts, weights, which, ranks):
    length, cols = lefts[0].shape
    width = weights.shape[1]
    rows = length // ranks
    tile = 256
    return pl.pallas_call(
        functools.partial(back_parts_kernel, rows, len(lefts)),
        grid=(width // tile,),
        in_specs=[pl.BlockSpec((length, cols), lambda i: (0, 0))] * len(lefts)
        + [pl.BlockSpec((1, tile, cols), lambda i, k=k: (k, i, 0)) for k in which],
        out_specs=[pl.BlockSpec((rows, tile), lambda i: (0, i))] * ranks,
        out_shape=[jax.ShapeDtypeStruct((rows, width), LOW)] * ranks,
        compiler_params=pltpu.CompilerParams(vmem_limit_bytes=56 * 2**20),
        cost_estimate=FREE,
        name="back_parts",
    )(*lefts, *([weights] * len(which)))


def join_kernel(flows, at_ref, *refs):
    total = refs[flows][...].astype(F32) + refs[flows + 1][...].astype(F32)
    if flows:
        total = total + refs[0][...].astype(F32)
    refs[-1][...] = total.astype(refs[-1].dtype)


def join(owner, flow, near, other, ring, dtype):
    depth, cols = near.shape[0] // ring, near.shape[1]
    flows = [] if flow is None else [flow]
    half = cols // 2 if cols % 256 == 0 else cols
    row = pl.BlockSpec((depth, half), lambda i, at: (0, i))
    chosen = pl.BlockSpec((depth, half), lambda i, at: (at[0], i))
    return pl.pallas_call(
        functools.partial(join_kernel, len(flows)),
        grid_spec=pltpu.PrefetchScalarGridSpec(
            num_scalar_prefetch=1,
            grid=(cols // half,),
            in_specs=[row] * len(flows) + [chosen] * 2,
            out_specs=row,
        ),
        out_shape=jax.ShapeDtypeStruct((depth, cols), dtype),
        compiler_params=pltpu.CompilerParams(vmem_limit_bytes=56 * 2**20),
        cost_estimate=FREE,
        name="join",
    )(owner.astype(jnp.int32).reshape(1), *flows, near, other)


def last_join_kernel(at_ref, flow_ref, near_ref, other_ref, *out_refs):
    total = flow_ref[...].astype(F32) + near_ref[...].astype(F32) + other_ref[...].astype(F32)
    width = total.shape[1] // len(out_refs)
    for k, out_ref in enumerate(out_refs):
        cols = out_ref.shape[1]
        out_ref[...] = total[:, k * width : k * width + cols]


def last_join(owner, flow, near, other, ring, cols, count):
    depth, wide = near.shape[0] // ring, near.shape[1]
    chosen = pl.BlockSpec((depth, wide), lambda i, at: (at[0], 0))
    return pl.pallas_call(
        last_join_kernel,
        grid_spec=pltpu.PrefetchScalarGridSpec(
            num_scalar_prefetch=1,
            grid=(1,),
            in_specs=[pl.BlockSpec((depth, wide), lambda i, at: (0, 0)), chosen, chosen],
            out_specs=[pl.BlockSpec((depth, cols), lambda i, at: (0, 0))] * count,
        ),
        out_shape=[jax.ShapeDtypeStruct((depth, cols), F32)] * count,
        compiler_params=pltpu.CompilerParams(vmem_limit_bytes=56 * 2**20),
        cost_estimate=FREE,
        name="last_join",
    )(owner.astype(jnp.int32).reshape(1), flow, near, other)


def cut_kernel(widths, grads_ref, *out_refs):
    first = 0
    for cols, out_ref in zip(widths[:-1], out_refs):
        out_ref[...] = grads_ref[:, first : first + cols].astype(F32)
        first += cols
    out_refs[-1][...] = grads_ref[:, first : first + widths[-1]].astype(F32).T


def cut_grads(grads, widths):
    depth = grads.shape[0]
    whole = lambda shape: pl.BlockSpec(shape, lambda i: (0, 0))
    shapes = [(depth, cols) for cols in widths[:-1]] + [(widths[-1], depth)]
    return pl.pallas_call(
        functools.partial(cut_kernel, widths),
        grid=(1,),
        in_specs=[whole(grads.shape)],
        out_specs=[whole(shape) for shape in shapes],
        out_shape=[jax.ShapeDtypeStruct(shape, F32) for shape in shapes],
        compiler_params=pltpu.CompilerParams(vmem_limit_bytes=24 * 2**20),
        cost_estimate=FREE,
        name="cut_grads",
    )(grads)


def sum_kernel(count, base_ref, *refs):
    total = base_ref[...].astype(F32)
    arrived = refs[0][...].astype(F32)
    for ref in refs[1:count]:
        arrived = arrived + ref[...].astype(F32)
    total = total + arrived
    refs[-1 if len(refs) == count + 1 else -2][...] = total
    if len(refs) > count + 1:
        gain_ref = refs[count]
        inverse = lax.rsqrt(jnp.mean(total * total, axis=-1, keepdims=True) + EPSILON)
        refs[-1][...] = (total * inverse * gain_ref[...]).astype(LOW)


def sum_up(base, parts, gain=None):
    rows, width = base.shape
    step = rows // 2
    by_row = pl.BlockSpec((step, width), lambda i: (i, 0))
    gains = [] if gain is None else [gain.reshape(1, -1)]
    outs = [jax.ShapeDtypeStruct((rows, width), F32)]
    if gains:
        outs.append(jax.ShapeDtypeStruct((rows, width), LOW))
    return pl.pallas_call(
        functools.partial(sum_kernel, len(parts)),
        grid=(2,),
        in_specs=[by_row] * (1 + len(parts)) + [pl.BlockSpec((1, width), lambda i: (0, 0))] * len(gains),
        out_specs=[by_row] * len(outs),
        out_shape=outs,
        compiler_params=pltpu.CompilerParams(vmem_limit_bytes=56 * 2**20),
        cost_estimate=FREE,
        name="sum_up",
    )(base, *parts, *gains)


def norm_back_kernel(count, value_ref, gain_ref, rest_ref, *refs):
    parts, outs = refs[:count], refs[count:]
    value = value_ref[...].astype(F32)
    grad = parts[0][...].astype(F32)
    for ref in parts[1:]:
        grad = grad + ref[...].astype(F32)
    inverse = lax.rsqrt(jnp.mean(value * value, axis=-1, keepdims=True) + EPSILON)
    hat = value * inverse
    scaled = grad * gain_ref[...]
    inner = jnp.mean(scaled * hat, axis=-1, keepdims=True)
    total = rest_ref[...].astype(F32) + (scaled - hat * inner) * inverse
    outs[0][...] = total
    if len(outs) > 1:
        outs[1][...] = total.astype(LOW)

        @pl.when(pl.program_id(0) == 0)
        def _():
            outs[2][...] = jnp.zeros_like(outs[2])

        outs[2][...] += jnp.sum(grad * hat, axis=0, keepdims=True)


def norm_back_sum(value, gain, rest, parts, more):
    rows, width = value.shape
    step = rows // 2
    by_row = pl.BlockSpec((step, width), lambda i: (i, 0))
    fixed = pl.BlockSpec((1, width), lambda i: (0, 0))
    shapes = [jax.ShapeDtypeStruct((rows, width), F32)]
    if more:
        shapes += [jax.ShapeDtypeStruct((rows, width), LOW), jax.ShapeDtypeStruct((1, width), F32)]
    return pl.pallas_call(
        functools.partial(norm_back_kernel, len(parts)),
        grid=(2,),
        in_specs=[by_row, fixed, by_row] + [by_row] * len(parts),
        out_specs=[by_row, by_row, fixed][: len(shapes)],
        out_shape=shapes,
        compiler_params=pltpu.CompilerParams(vmem_limit_bytes=56 * 2**20),
        cost_estimate=FREE,
        name="norm_back_sum",
    )(value, gain.reshape(1, -1), rest, *parts)


def rows_product_kernel(left_ref, right_ref, out_ref):
    out_ref[...] = jnp.dot(left_ref[...], right_ref[0], preferred_element_type=F32).astype(LOW)


def rows_product(left, right, ranks):
    length, depth = left.shape
    rows = length // ranks
    return pl.pallas_call(
        rows_product_kernel,
        grid=(ranks,),
        in_specs=[
            pl.BlockSpec((rows, depth), lambda i: (i, 0)),
            pl.BlockSpec((1,) + right.shape[1:], lambda i: (0, 0, 0)),
        ],
        out_specs=pl.BlockSpec((rows, right.shape[2]), lambda i: (i, 0)),
        out_shape=jax.ShapeDtypeStruct((length, right.shape[2]), LOW),
        compiler_params=pltpu.CompilerParams(vmem_limit_bytes=24 * 2**20),
        cost_estimate=FREE,
        name="rows_product",
    )(left, right)


def gain_parts_kernel(normed_ref, gain_ref, two_ref, heads_ref, *refs):
    parts, out_ref = refs[:-1], refs[-1]
    rows, width = parts[0].shape
    total = jnp.zeros((1, width), F32)
    for j, ref in enumerate(parts):
        block = normed_ref[j * rows : (j + 1) * rows, :].astype(F32)
        total = total + jnp.sum(block * ref[...].astype(F32), axis=0, keepdims=True)
    out_ref[:, :width] = total / gain_ref[...]
    out_ref[:, width : 2 * width] = two_ref[...]
    out_ref[:, 2 * width :] = heads_ref[...]


def gain_parts(normed, gain, parts, two, heads):
    args = [normed, gain.reshape(1, -1), two, heads, *parts]
    whole = lambda a: pl.BlockSpec(a.shape, lambda i: (0, 0))
    shape = jax.ShapeDtypeStruct((1, 2 * normed.shape[1] + heads.shape[1]), F32)
    return pl.pallas_call(
        gain_parts_kernel,
        grid=(1,),
        in_specs=[whole(a) for a in args],
        out_specs=whole(shape),
        out_shape=shape,
        compiler_params=pltpu.CompilerParams(vmem_limit_bytes=56 * 2**20),
        cost_estimate=FREE,
        name="gain_parts",
    )(*args)


def group_mean(values):
    width = values.shape[1]
    part = 2 * HEAD_SIZE
    left = lax.broadcasted_iota(jnp.int32, (part, part), 0) // HEAD_SIZE
    right = lax.broadcasted_iota(jnp.int32, (part, part), 1) // HEAD_SIZE
    spread = jnp.where(left == right, 1.0 / HEAD_SIZE, 0.0).astype(F32)
    pieces = []
    for first in range(0, width, part):
        size = min(part, width - first)
        pieces.append(
            lax.dot_general(
                values[:, first : first + size],
                spread[:size, :size],
                NN,
                precision=lax.Precision.HIGHEST,
                preferred_element_type=F32,
            )
        )
    return jnp.concatenate(pieces, axis=1) if len(pieces) > 1 else pieces[0]


def across(table, width):
    part = table.shape[1]
    if width < part:
        return table[:, :width]
    return jnp.concatenate([table] * (width // part) + ([table[:, : width % part]] if width % part else []), axis=1)


def partner(values):
    width = values.shape[1]
    half = HEAD_SIZE // 2
    lane = lax.broadcasted_iota(jnp.int32, values.shape, 1) % HEAD_SIZE
    return jnp.where(lane < half, pltpu.roll(values, width - half, 1), pltpu.roll(values, half, 1))


def prepare_kernel(q_cols, kv_cols, x_ref, w_ref, cos_ref, sin_ref, gain_ref, q_ref, k_ref, v_ref, raw_ref):
    product = jnp.dot(x_ref[...], w_ref[...], preferred_element_type=F32)
    for first, cols, to in ((0, q_cols, q_ref), (q_cols, kv_cols, k_ref)):
        raw = product[:, first : first + cols]
        scaled = raw * lax.rsqrt(group_mean(raw * raw) + EPSILON) * gain_ref[:, first : first + cols]
        cos = across(cos_ref[...], cols)
        sin = across(sin_ref[...], cols)
        to[...] = (scaled * cos + partner(scaled) * sin).astype(LOW)
        raw_ref[:, first : first + cols] = raw
    v_ref[...] = product[:, q_cols + kv_cols :].astype(LOW)


def prepare(normed, weight, cosine, sine, gains, q_cols, kv_cols, ranks):
    length, width = normed.shape
    rows = length // ranks
    at_row = lambda i: (i, 0)
    fixed = lambda i: (0, 0)
    return pl.pallas_call(
        functools.partial(prepare_kernel, q_cols, kv_cols),
        grid=(ranks,),
        in_specs=[
            pl.BlockSpec((rows, width), at_row),
            pl.BlockSpec(weight.shape, fixed),
            pl.BlockSpec((rows, cosine.shape[1]), at_row),
            pl.BlockSpec((rows, cosine.shape[1]), at_row),
            pl.BlockSpec((1, q_cols + kv_cols), fixed),
        ],
        out_specs=[
            pl.BlockSpec((rows, q_cols), at_row),
            pl.BlockSpec((rows, kv_cols), at_row),
            pl.BlockSpec((rows, kv_cols), at_row),
            pl.BlockSpec((rows, q_cols + kv_cols), at_row),
        ],
        out_shape=[
            jax.ShapeDtypeStruct((length, q_cols), LOW),
            jax.ShapeDtypeStruct((length, kv_cols), LOW),
            jax.ShapeDtypeStruct((length, kv_cols), LOW),
            jax.ShapeDtypeStruct((length, q_cols + kv_cols), F32),
        ],
        compiler_params=pltpu.CompilerParams(vmem_limit_bytes=40 * 2**20),
        cost_estimate=FREE,
        name="prepare",
    )(normed, weight, cosine, sine, gains)


def prepare_back_kernel(
    q_cols, kv_cols, dq_ref, dk_ref, dv_ref, raw_ref, cos_ref, sin_ref, gain_ref, out_ref, gain_grad_ref
):
    @pl.when(pl.program_id(0) == 0)
    def _():
        gain_grad_ref[...] = jnp.zeros_like(gain_grad_ref)

    for first, cols, grad_ref in ((0, q_cols, dq_ref), (q_cols, kv_cols, dk_ref)):
        span = slice(first, first + cols)
        grad = grad_ref[...]
        turned = grad * across(cos_ref[...], cols) - partner(grad) * across(sin_ref[...], cols)
        raw = raw_ref[:, span]
        inverse = lax.rsqrt(group_mean(raw * raw) + EPSILON)
        hat = raw * inverse
        gain_grad_ref[:, span] += jnp.sum(turned * hat, axis=0, keepdims=True)
        scaled = turned * gain_ref[:, span]
        out_ref[:, span] = ((scaled - hat * group_mean(scaled * hat)) * inverse).astype(LOW)
    out_ref[:, q_cols + kv_cols :] = dv_ref[...].astype(LOW)


def prepare_back(d_queries, d_keys, d_values, raw, cosine, sine, gains, ranks):
    length, q_cols = d_queries.shape
    kv_cols = d_keys.shape[1]
    rows = length // ranks
    at_row = lambda i: (i, 0)
    fixed = lambda i: (0, 0)
    return pl.pallas_call(
        functools.partial(prepare_back_kernel, q_cols, kv_cols),
        grid=(ranks,),
        in_specs=[
            pl.BlockSpec((rows, q_cols), at_row),
            pl.BlockSpec((rows, kv_cols), at_row),
            pl.BlockSpec((rows, kv_cols), at_row),
            pl.BlockSpec((rows, q_cols + kv_cols), at_row),
            pl.BlockSpec((rows, cosine.shape[1]), at_row),
            pl.BlockSpec((rows, cosine.shape[1]), at_row),
            pl.BlockSpec((1, q_cols + kv_cols), fixed),
        ],
        out_specs=[
            pl.BlockSpec((rows, q_cols + 2 * kv_cols), at_row),
            pl.BlockSpec((1, q_cols + kv_cols), fixed),
        ],
        out_shape=[
            jax.ShapeDtypeStruct((length, q_cols + 2 * kv_cols), LOW),
            jax.ShapeDtypeStruct((1, q_cols + kv_cols), F32),
        ],
        compiler_params=pltpu.CompilerParams(vmem_limit_bytes=56 * 2**20),
        cost_estimate=FREE,
        name="prepare_back",
    )(d_queries, d_keys, d_values, raw, cosine, sine, gains)


def shards(
    dp_size,
    ranks,
    tokens,
    segments,
    attn_gain,
    w_query,
    key_weight,
    value_weight,
    query_gain,
    key_gain,
    w_out,
    ffn_gain,
    w_gate,
    w_up,
    w_down,
    cotangent,
):
    ring = dp_size // 2
    index = lax.axis_index("dp")
    stage = index // 2
    core = index % 2
    me = lax.axis_index("tensor")
    swap_pairs = [(i, i ^ 1) for i in range(dp_size)]
    ring_pairs = [(i, (i + 2) % dp_size) for i in range(dp_size)]
    heads = KEY_VALUE_HEADS // ranks
    rows = tokens.shape[0]
    length = segments.shape[0]
    q_cols = w_query.shape[1]
    kv_cols = key_weight.shape[1]

    hidden_cols = w_gate.shape[1]
    hidden_pad = -hidden_cols % 128

    def widen(weight):
        return jnp.pad(weight, ((0, 0), (0, hidden_pad)))

    def swap(v):
        return lax.ppermute(v, "dp", swap_pairs)

    def onward(v):
        return lax.ppermute(v, "dp", ring_pairs)

    core_array = core.astype(jnp.int32).reshape(1)
    at = jnp.stack([stage, core]).astype(jnp.int32)

    def hop(label, block):
        with jax.named_scope(label):
            return onward(block)

    def owner_after(count):
        return lax.rem(stage - 1 - count + 2 * ring, ring)

    def spread(label, block):
        with jax.named_scope(label):
            return [block] + [
                lax.ppermute(block, "tensor", [(i, i ^ j) for i in range(ranks)])
                for j in range(1, ranks)
            ]

    def send_parts(label, parts):
        with jax.named_scope(label):
            return [
                lax.ppermute(parts[j], "tensor", [(i, i ^ j) for i in range(ranks)])
                for j in range(1, ranks)
            ]

    def add_up(own, arrived):
        total = own.astype(F32)
        for piece in arrived:
            total = total + piece.astype(F32)
        return total

    def cut(matrix):
        return [matrix[j * rows : (j + 1) * rows] for j in range(ranks)]

    def tie(value, *others):
        return lax.optimization_barrier((value,) + others)[0]

    tokens_wide = tokens.astype(F32)
    normed_own = norm_rows(tokens_wide, attn_gain).astype(LOW)
    normed_one = spread("one_spread", normed_own)
    wide = hidden_cols + hidden_pad
    ffn_full = lax.all_gather(
        jnp.stack([widen(w_down.T), widen(w_gate), widen(w_up)]), "dp", axis=1, tiled=True
    )
    gate_full, up_full = ffn_full[1], ffn_full[2]
    qkv_blocks = [jnp.concatenate([w_query, key_weight, value_weight], axis=1)]
    for count in range(1, ring):
        qkv_blocks.append(hop(f"qkv_hop{count}", qkv_blocks[-1]))
    out_blocks = [w_out.T]
    for count in range(1, ring):
        out_flow = hop(f"out_hop{count}", out_blocks[-1])
        if count < ring - 1:
            out_blocks.append(tie(out_flow, qkv_blocks[count + 1]))

    def complete(blocks):
        return place(at, [b for block in blocks for b in (block, swap(block))], ring)

    grad_blocks = spread("cot_spread", tie(cotangent, *normed_one))
    first_start = jnp.sum((segments < 1).astype(jnp.int32))
    second_start = jnp.sum((segments < 2).astype(jnp.int32))
    ids = jnp.arange(length, dtype=jnp.int32).reshape(ranks, rows)
    begins = jnp.where(segments == 0, 0, jnp.where(segments == 1, first_start, second_start))
    begins = begins.astype(jnp.int32).reshape(ranks, rows)
    order = [me ^ j for j in range(ranks)]
    bounds = jnp.stack([lax.dynamic_index_in_dim(begins, o, 0, keepdims=False) for o in order])
    here = jnp.stack([lax.dynamic_index_in_dim(ids, o, 0, keepdims=False) for o in order])
    positions = (here - bounds).reshape(length).astype(F32)
    bounds = bounds.reshape(ranks, 1, rows)
    half = HEAD_SIZE // 2
    freqs = ROTARY_BASE ** (-2.0 * jnp.arange(half, dtype=F32) / HEAD_SIZE)
    angles = positions[:, None] * jnp.concatenate([freqs] * 4)[None, :]
    signs = jnp.concatenate([-jnp.ones(half, F32), jnp.ones(half, F32)] * 2)
    cosine = jnp.cos(angles)
    sine = jnp.sin(angles) * signs[None, :]
    head_gains = jnp.concatenate(
        [query_gain] * (q_cols // HEAD_SIZE) + [key_gain] * (kv_cols // HEAD_SIZE)
    ).reshape(1, -1)

    normed_all, normed_one_t = fold(core_array, normed_one, ring)
    w_qkv = complete(qkv_blocks)
    query_low, key_low, value_low, raw = prepare(
        normed_all, w_qkv, cosine, sine, head_gains, q_cols, kv_cols, ranks
    )
    me_array = me.astype(jnp.int32).reshape(1)
    attended, lse = attend(me_array, query_low, key_low, value_low, bounds, ranks, heads)

    attended_go = tie(attended, *grad_blocks)
    out_blocks.append(tie(out_flow, attended))
    out_t = complete(out_blocks)
    attn_parts = back_parts([attended_go], out_t[None], (0,), ranks)
    attn_arrived = send_parts("attn_sum", attn_parts)
    grad_all, grad_t = fold(core_array, [tie(grad_blocks[0], *attn_parts)] + grad_blocks[1:], ring)
    attn_arrived[0] = tie(attn_arrived[0], grad_all)
    hidden, normed_two_own = sum_up(tokens, [attn_parts[0]] + attn_arrived, ffn_gain)
    normed_two = spread("two_spread", normed_two_own)
    d_activation = rows_product(grad_all, ffn_full, ranks)
    normed_two[-1] = tie(normed_two[-1], d_activation)
    normed_two_all, *normed_two_pair = fold(core_array, normed_two, ring, True)

    gating = mm(normed_two_all, gate_full).astype(LOW).astype(F32)
    lifted = mm(normed_two_all, up_full)
    gate_sig = jax.nn.sigmoid(gating)
    silu = gating * gate_sig
    activation = (silu * lifted).astype(LOW)
    d_act_wide = d_activation.astype(F32)
    d_gating = (d_act_wide * lifted * gate_sig * (1.0 + gating * (1.0 - gate_sig))).astype(LOW)
    d_lifted = (d_act_wide * silu).astype(LOW)

    last = ring - 1

    def advance(label, flow, near, other, count):
        if count == last:
            return join(owner_after(count), flow, near, other, ring, F32), None
        block = join(owner_after(count), flow, near, other, ring, LOW)
        return block, hop(f"{label}_hop{count + 1}", block)

    def several(label, block, flow, near, other, first, end, *after):
        for count in range(first, end):
            block, flow = advance(label, tie(flow, *after), near, other, count)
        return block, flow

    down_full_grad = product(grad_t, [activation])
    down_grad = lax.psum_scatter(down_full_grad, "dp", scatter_dimension=0, tiled=True)
    two_parts = back_parts([tie(d_gating, down_full_grad), d_lifted], ffn_full, (1, 2), ranks)
    two_arrived = send_parts("two_sum", two_parts)
    both_far = product(normed_two_pair[0], [tie(d_gating, *two_parts), d_lifted])
    both_near = product(normed_two_pair[1], [tie(d_gating, both_far), d_lifted])
    *two_arrived, both_far, both_near = lax.optimization_barrier((*two_arrived, both_far, both_near))
    both_other = swap(both_far)
    d_hidden, d_hidden_low, ffn_gain_part = norm_back_sum(
        hidden, ffn_gain, cotangent, [two_parts[0]] + two_arrived, True
    )
    hidden_grad = spread("dh_spread", d_hidden_low)
    both_block, both_flow = advance("both_grad", None, tie(both_near, d_hidden_low), both_other, 0)
    ffn_parts = back_parts([tie(activation, d_hidden_low)], ffn_full, (0,), ranks)
    hidden_grad[1] = tie(hidden_grad[1], *ffn_parts)
    both_block, both_flow = several(
        "both_grad", both_block, both_flow, both_near, both_other, 1, last - 1, hidden_grad[1]
    )
    hidden_grad[-1] = tie(hidden_grad[-1], both_block)
    hidden_grad_all, hidden_grad_t = fold(core_array, hidden_grad, ring)
    ffn_go = lax.optimization_barrier(tuple(ffn_parts) + tuple(hidden_grad))[:ranks]
    ffn_arrived = send_parts("ffn_sum", ffn_go)
    d_attended = rows_product(hidden_grad_all, out_t[None], ranks)
    d_queries, d_keys, d_values = attend_back(
        me_array, query_low, key_low, value_low, bounds, attended, d_attended, lse, ranks, heads
    )
    d_raw, head_gain_parts = prepare_back(
        d_queries, d_keys, d_values, raw, cosine, sine, head_gains, ranks
    )
    both_block, both_flow = advance(
        "both_grad", tie(both_flow, *ffn_arrived), both_near, both_other, last - 1
    )
    one_parts = back_parts([tie(d_raw, both_block, *ffn_arrived)], w_qkv[None], (0,), ranks)
    one_arrived = send_parts("one_sum", one_parts)
    attn_full_grad = attn_products([normed_one_t, hidden_grad_t], [tie(d_raw, *one_parts), attended])
    attn_grad = lax.psum_scatter(
        tie(attn_full_grad, down_grad), "dp", scatter_dimension=0, tiled=True)
    gains = gain_parts(
        tie(normed_all, attn_full_grad), attn_gain, one_parts, ffn_gain_part, head_gain_parts
    )
    (output,) = sum_up(tie(hidden, gains), [ffn_parts[0]] + ffn_arrived)

    def exchange_sum(own, axis, offsets, size):
        pieces = [own] + [lax.ppermute(own, axis, [(i, i ^ j) for i in range(size)]) for j in offsets]
        while len(pieces) > 1:
            pieces = [a + b for a, b in zip(pieces[::2], pieces[1::2])]
        return pieces[0]

    total = exchange_sum(gains, "tensor", range(1, ranks), ranks)
    one_arrived[-1] = tie(one_arrived[-1], output, total)
    (tokens_grad,) = norm_back_sum(tokens, attn_gain, d_hidden, [one_parts[0]] + one_arrived, False)
    gate_grad, lift_grad = last_join(
        owner_after(last), tie(both_flow, tokens_grad), both_near, both_other, ring, hidden_cols, 2
    )
    query_grad, key_grad, value_grad, out_grad = cut_grads(
        attn_grad, (q_cols, kv_cols, kv_cols, q_cols)
    )
    down_grad = down_grad[:, :hidden_cols].astype(F32)

    total = tie(total, gate_grad, tokens_grad)
    total = exchange_sum(total, "dp", range(1, 2), dp_size)
    total = exchange_sum(total, "dp", range(2, dp_size, 2), dp_size)
    total = total.reshape(-1)
    a, b = attn_gain.shape[0], 2 * attn_gain.shape[0]
    query_gain_grad = jnp.sum(total[b : b + q_cols].reshape(-1, HEAD_SIZE), axis=0)
    key_gain_grad = jnp.sum(total[b + q_cols :].reshape(-1, HEAD_SIZE), axis=0)
    return (
        output,
        tokens_grad,
        total[:a],
        query_grad,
        key_grad,
        value_grad,
        query_gain_grad,
        key_gain_grad,
        out_grad,
        total[a:b],
        gate_grad,
        lift_grad,
        down_grad.T,
    )


def solution(mesh):
    in_specs = (
        P(("dp", "tensor"), None),
        P("dp"),
        P(),
        P("dp", "tensor"),
        P("dp", "tensor"),
        P("dp", "tensor"),
        P(),
        P(),
        P("tensor", "dp"),
        P(),
        P("dp", "tensor"),
        P("dp", "tensor"),
        P("tensor", "dp"),
        P(("dp", "tensor"), None),
    )
    out_specs = (
        P(("dp", "tensor"), None),
        P(("dp", "tensor"), None),
        P(),
        P("dp", "tensor"),
        P("dp", "tensor"),
        P("dp", "tensor"),
        P(),
        P(),
        P("tensor", "dp"),
        P(),
        P("dp", "tensor"),
        P("dp", "tensor"),
        P("tensor", "dp"),
    )
    body = functools.partial(shards, mesh.shape["dp"], mesh.shape["tensor"])
    return jax.shard_map(body, mesh=mesh, in_specs=in_specs, out_specs=out_specs, check_vma=False)
```

```python
import functools

import jax
import jax.numpy as jnp
from jax import lax
from jax.experimental import pallas as pl
from jax.experimental.pallas import tpu as pltpu
from jax.sharding import PartitionSpec as P

QUERY_HEADS = 24
KEY_VALUE_HEADS = 8
HEAD_SIZE = 64
GROUP = QUERY_HEADS // KEY_VALUE_HEADS
EPSILON = 1e-05
ROTARY_BASE = 1000000.0
NEGATIVE_FILL = -1e30
F32 = jnp.float32
LOW = jnp.bfloat16
SCALE = HEAD_SIZE ** (-0.5)
FREE = pl.CostEstimate(flops=0, bytes_accessed=0, transcendentals=0)


def norm_rows(values_in, gain):
    return (
        values_in
        * lax.rsqrt(jnp.mean(values_in * values_in, axis=-1, keepdims=True) + EPSILON)
        * gain
    )


def norm_back(values, gain, grad):
    inverse = lax.rsqrt(jnp.mean(values * values, axis=-1, keepdims=True) + EPSILON)
    hat = values * inverse
    scaled = grad * gain
    inner = jnp.mean(scaled * hat, axis=-1, keepdims=True)
    return (scaled - hat * inner) * inverse, jnp.sum(grad * hat, axis=0)


def mm(left, right):
    return jnp.dot(left, right, preferred_element_type=F32)


def cross_rows(left, right):
    return lax.dot_general(left, right, (((1,), (1,)), ((), ())), preferred_element_type=F32)


def cross_cols(left, right):
    return lax.dot_general(left, right, (((0,), (0,)), ((), ())), preferred_element_type=F32)


NT = (((1,), (1,)), ((), ()))
NN = (((1,), (0,)), ((), ()))
TN = (((0,), (0,)), ((), ()))


def kdot(left, right, dims):
    return lax.dot_general(left, right, dims, preferred_element_type=F32)


def stack_heads(block, head):
    first = head * GROUP * HEAD_SIZE
    return jnp.concatenate(
        [block[:, first + g * HEAD_SIZE : first + (g + 1) * HEAD_SIZE] for g in range(GROUP)], axis=0
    )


def attend_kernel(heads, rows, me_ref, q_ref, k_ref, v_ref, lo_ref, out_ref, lse_ref):
    me = me_ref[0]
    block = pl.program_id(0) ^ me
    low_bound = jnp.concatenate([lo_ref[0]] * GROUP, axis=1)
    row_ids = block * rows + lax.broadcasted_iota(jnp.int32, (1, rows), 1)
    row_ids = jnp.concatenate([row_ids] * GROUP, axis=1)
    width = GROUP * rows
    queries = q_ref[...] * SCALE
    pieces = []
    for head in range(heads):
        q3 = stack_heads(queries, head)
        cols = slice(head * HEAD_SIZE, (head + 1) * HEAD_SIZE)

        def step(other, carry, q3=q3, cols=cols):
            peak, total, acc = carry
            first = pl.multiple_of((other ^ me) * rows, rows)
            keys = k_ref[pl.ds(first, rows), cols]
            vals = v_ref[pl.ds(first, rows), cols]
            ids = other * rows + lax.broadcasted_iota(jnp.int32, (rows, 1), 0)
            scores = kdot(keys, q3, NT)
            scores = jnp.where((ids <= row_ids) & (ids >= low_bound), scores, NEGATIVE_FILL)
            higher = jnp.maximum(peak, jnp.max(scores, axis=0, keepdims=True))
            fade = jnp.exp(peak - higher)
            exps = jnp.exp(scores - higher)
            total = total * fade + jnp.sum(exps, axis=0, keepdims=True)
            acc = acc * fade + kdot(vals, exps.astype(LOW), TN)
            return higher, total, acc

        start = (
            jnp.full((1, width), NEGATIVE_FILL, F32),
            jnp.zeros((1, width), F32),
            jnp.zeros((HEAD_SIZE, width), F32),
        )
        start = step(block, start)
        peak, total, acc = lax.fori_loop(0, block, step, start)
        acc = acc / total
        lse_ref[0, head : head + 1, :] = peak + jnp.log(total)
        pieces += [acc[:, g * rows : (g + 1) * rows] for g in range(GROUP)]
    out_ref[...] = jnp.concatenate(pieces, axis=0).T.astype(LOW)


def attend_back_kernel(
    heads, rows, me_ref, q_ref, k_ref, v_ref, lo_ref, o_ref, do_ref, lse_ref, dq_ref, dk_ref, dv_ref
):
    me = me_ref[0]

    @pl.when(pl.program_id(0) == 0)
    def _():
        dk_ref[...] = jnp.zeros_like(dk_ref)
        dv_ref[...] = jnp.zeros_like(dv_ref)

    block = pl.program_id(0) ^ me
    low_bound = jnp.concatenate([lo_ref[0]] * GROUP, axis=1)
    row_ids = block * rows + lax.broadcasted_iota(jnp.int32, (1, rows), 1)
    row_ids = jnp.concatenate([row_ids] * GROUP, axis=1)
    width = GROUP * rows
    queries = q_ref[...] * SCALE
    grads = do_ref[...]
    product = (grads.astype(F32) * o_ref[...].astype(F32)).T
    pieces = []
    for head in range(heads):
        q3 = stack_heads(queries, head)
        do3 = stack_heads(grads, head)
        cols = slice(head * HEAD_SIZE, (head + 1) * HEAD_SIZE)
        first_row = head * GROUP * HEAD_SIZE
        inner = jnp.concatenate(
            [
                jnp.sum(
                    product[first_row + g * HEAD_SIZE : first_row + (g + 1) * HEAD_SIZE],
                    axis=0,
                    keepdims=True,
                )
                for g in range(GROUP)
            ],
            axis=1,
        )
        lse = lse_ref[0, head : head + 1, :]

        def step(other, acc, q3=q3, do3=do3, cols=cols, inner=inner, lse=lse):
            first = pl.multiple_of((other ^ me) * rows, rows)
            place = pl.ds(first, rows)
            keys = k_ref[place, cols]
            vals = v_ref[place, cols]
            ids = other * rows + lax.broadcasted_iota(jnp.int32, (rows, 1), 0)
            scores = kdot(keys, q3, NT)
            scores = jnp.where((ids <= row_ids) & (ids >= low_bound), scores, NEGATIVE_FILL)
            probs = jnp.exp(scores - lse)
            d_probs = kdot(vals, do3, NT)
            d_scores = (probs * (d_probs - inner)).astype(LOW)
            dk_ref[place, cols] += kdot(d_scores, q3, NN)
            dv_ref[place, cols] += kdot(probs.astype(LOW), do3, NN)
            return acc + kdot(keys, d_scores, TN)

        acc = lax.fori_loop(0, block + 1, step, jnp.zeros((HEAD_SIZE, width), F32))
        pieces += [acc[:, g * rows : (g + 1) * rows] for g in range(GROUP)]
    dq_ref[...] = jnp.concatenate(pieces, axis=0).T * SCALE


def attention_specs(ranks, rows, heads):
    length = ranks * rows
    q_spec = pl.BlockSpec((rows, heads * GROUP * HEAD_SIZE), lambda i, me: (i, 0))
    kv_spec = pl.BlockSpec((length, heads * HEAD_SIZE), lambda i, me: (0, 0))
    lo_spec = pl.BlockSpec((1, 1, rows), lambda i, me: (i, 0, 0))
    lse_spec = pl.BlockSpec((1, heads, GROUP * rows), lambda i, me: (i, 0, 0))
    return q_spec, kv_spec, lo_spec, lse_spec


def attend(me, queries, keys, values, bounds, ranks, heads):
    length = queries.shape[0]
    rows = length // ranks
    q_spec, kv_spec, lo_spec, lse_spec = attention_specs(ranks, rows, heads)
    return pl.pallas_call(
        functools.partial(attend_kernel, heads, rows),
        grid_spec=pltpu.PrefetchScalarGridSpec(
            num_scalar_prefetch=1,
            grid=(ranks,),
            in_specs=[q_spec, kv_spec, kv_spec, lo_spec],
            out_specs=[q_spec, lse_spec],
        ),
        out_shape=[
            jax.ShapeDtypeStruct(queries.shape, LOW),
            jax.ShapeDtypeStruct((ranks, heads, GROUP * rows), F32),
        ],
        compiler_params=pltpu.CompilerParams(vmem_limit_bytes=48 * 2**20),
        cost_estimate=pl.CostEstimate(
            flops=16 * length * length * heads * GROUP * HEAD_SIZE,
            bytes_accessed=32 * 2**20,
            transcendentals=length * length * heads * GROUP,
        ),
        name="attend",
    )(me, queries, keys, values, bounds)


def attend_back(me, queries, keys, values, bounds, attended, d_attended, lse, ranks, heads):
    length = queries.shape[0]
    rows = length // ranks
    q_spec, kv_spec, lo_spec, lse_spec = attention_specs(ranks, rows, heads)
    return pl.pallas_call(
        functools.partial(attend_back_kernel, heads, rows),
        grid_spec=pltpu.PrefetchScalarGridSpec(
            num_scalar_prefetch=1,
            grid=(ranks,),
            in_specs=[q_spec, kv_spec, kv_spec, lo_spec, q_spec, q_spec, lse_spec],
            out_specs=[q_spec, kv_spec, kv_spec],
        ),
        out_shape=[
            jax.ShapeDtypeStruct(queries.shape, F32),
            jax.ShapeDtypeStruct(keys.shape, F32),
            jax.ShapeDtypeStruct(keys.shape, F32),
        ],
        compiler_params=pltpu.CompilerParams(vmem_limit_bytes=48 * 2**20),
        cost_estimate=FREE,
        name="attend_back",
    )(me, queries, keys, values, bounds, attended, d_attended, lse)


def fold_kernel(ranks, ring, rows, core_ref, *refs):
    blocks, (all_ref, turned_ref), split = refs[:ranks], refs[ranks : ranks + 2], refs[ranks + 2 :]
    core = core_ref[0]
    depth = turned_ref.shape[0] // (2 * ring)
    for j in range(ranks):
        block = blocks[j][...]
        span = slice(j * rows, (j + 1) * rows)
        all_ref[span, :] = block
        turned_ref[:, span] = block.T
        if split:
            for i in range(ring):
                to = slice(i * depth, (i + 1) * depth)
                for side_ref, side in zip(split, (1 - core, core)):
                    first = pl.multiple_of((2 * i + side) * depth, 16)
                    side_ref[to, span] = turned_ref[pl.ds(first, depth), span]


def fold(core, blocks, ring, split=False):
    ranks = len(blocks)
    rows, width = blocks[0].shape
    length = ranks * rows
    whole = lambda shape: pl.BlockSpec(shape, lambda i: (0, 0))
    shapes = [(length, width), (width, length)] + ([(width // 2, length)] * 2 if split else [])
    return pl.pallas_call(
        functools.partial(fold_kernel, ranks, ring, rows),
        grid=(1,),
        in_specs=[pl.BlockSpec(memory_space=pltpu.SMEM)] + [whole((rows, width))] * ranks,
        out_specs=[whole(shape) for shape in shapes],
        out_shape=[jax.ShapeDtypeStruct(shape, LOW) for shape in shapes],
        compiler_params=pltpu.CompilerParams(vmem_limit_bytes=40 * 2**20),
        cost_estimate=FREE,
        name="fold",
    )(core, *blocks)


def place_kernel(ring, depth, at_ref, *refs):
    blocks = refs[: 2 * ring]
    full_ref, sems = refs[2 * ring :]
    stage, core = at_ref[0], at_ref[1]
    copies = []
    for hop in range(ring):
        owner = lax.rem(stage - hop + ring, ring)
        for half, side in enumerate((core, 1 - core)):
            first = pl.multiple_of((owner * 2 + side) * depth, 16)
            copies.append(
                pltpu.make_async_copy(
                    blocks[2 * hop + half], full_ref.at[pl.ds(first, depth)], sems.at[2 * hop + half]
                )
            )
    for copy in copies:
        copy.start()
    for copy in copies:
        copy.wait()


def place(at, blocks, ring):
    depth, cols = blocks[0].shape
    return pl.pallas_call(
        functools.partial(place_kernel, ring, depth),
        in_specs=[pl.BlockSpec(memory_space=pltpu.SMEM)]
        + [pl.BlockSpec(memory_space=pl.ANY)] * (2 * ring),
        grid=(1,),
        out_specs=pl.BlockSpec((2 * ring * depth, cols), lambda i: (0, 0)),
        out_shape=jax.ShapeDtypeStruct((2 * ring * depth, cols), LOW),
        scratch_shapes=[pltpu.SemaphoreType.DMA((2 * ring,))],
        compiler_params=pltpu.CompilerParams(vmem_limit_bytes=24 * 2**20),
        cost_estimate=FREE,
        name="place",
    )(at, *blocks)


def product_kernel(tiles, left_ref, *refs):
    for k, right in enumerate(refs[:-1]):

        @pl.when(pl.program_id(0) // tiles == k)
        def _(right=right):
            refs[-1][...] = jnp.dot(
                left_ref[...], right[...], preferred_element_type=F32
            ).astype(LOW)


def product(left, rights):
    depth, length = left.shape
    cols = rights[0].shape[1]
    tile = 256 if cols % 256 == 0 else 128
    tiles = cols // tile
    return pl.pallas_call(
        functools.partial(product_kernel, tiles),
        grid=(tiles * len(rights),),
        in_specs=[pl.BlockSpec((depth, length), lambda i: (0, 0))]
        + [
            pl.BlockSpec((length, tile), lambda i, k=k: (0, jnp.clip(i - k * tiles, 0, tiles - 1)))
            for k in range(len(rights))
        ],
        out_specs=pl.BlockSpec((depth, tile), lambda i: (0, i)),
        out_shape=jax.ShapeDtypeStruct((depth, cols * len(rights)), LOW),
        compiler_params=pltpu.CompilerParams(vmem_limit_bytes=40 * 2**20),
        cost_estimate=FREE,
        name="product",
    )(left, *rights)


def attn_products_kernel(*refs):
    lefts, rights, out_ref = refs[:2], refs[2:4], refs[4]
    first = 0
    for left, right in zip(lefts, rights):
        cols = right.shape[1]
        out_ref[:, first : first + cols] = jnp.dot(
            left[...], right[...], preferred_element_type=F32
        ).astype(LOW)
        first += cols


def attn_products(lefts, rights):
    depth = lefts[0].shape[0]
    tiles = 4
    part = lambda a: pl.BlockSpec((depth // tiles, a.shape[1]), lambda i: (i, 0))
    whole = lambda a: pl.BlockSpec(a.shape, lambda i: (0, 0))
    shape = jax.ShapeDtypeStruct((depth, sum(a.shape[1] for a in rights)), LOW)
    return pl.pallas_call(
        attn_products_kernel,
        grid=(tiles,),
        in_specs=[part(a) for a in lefts] + [whole(a) for a in rights],
        out_specs=part(shape),
        out_shape=shape,
        compiler_params=pltpu.CompilerParams(vmem_limit_bytes=40 * 2**20),
        cost_estimate=FREE,
        name="attn_products",
    )(*lefts, *rights)


def back_parts_kernel(rows, count, *refs):
    total = sum(kdot(refs[k][...], refs[count + k][0], NT) for k in range(count))
    for j, out_ref in enumerate(refs[2 * count :]):
        out_ref[...] = total[j * rows : (j + 1) * rows].astype(LOW)


def back_parts(lefts, weights, which, ranks):
    length, cols = lefts[0].shape
    width = weights.shape[1]
    rows = length // ranks
    tile = 256
    return pl.pallas_call(
        functools.partial(back_parts_kernel, rows, len(lefts)),
        grid=(width // tile,),
        in_specs=[pl.BlockSpec((length, cols), lambda i: (0, 0))] * len(lefts)
        + [pl.BlockSpec((1, tile, cols), lambda i, k=k: (k, i, 0)) for k in which],
        out_specs=[pl.BlockSpec((rows, tile), lambda i: (0, i))] * ranks,
        out_shape=[jax.ShapeDtypeStruct((rows, width), LOW)] * ranks,
        compiler_params=pltpu.CompilerParams(vmem_limit_bytes=48 * 2**20),
        cost_estimate=FREE,
        name="back_parts",
    )(*lefts, *([weights] * len(which)))


def join_kernel(flows, at_ref, *refs):
    total = refs[flows][...].astype(F32) + refs[flows + 1][...].astype(F32)
    if flows:
        total = total + refs[0][...].astype(F32)
    refs[-1][...] = total.astype(refs[-1].dtype)


def join(owner, flow, near, other, ring, dtype):
    depth, cols = near.shape[0] // ring, near.shape[1]
    flows = [] if flow is None else [flow]
    half = cols // 2 if cols % 256 == 0 else cols
    row = pl.BlockSpec((depth, half), lambda i, at: (0, i))
    chosen = pl.BlockSpec((depth, half), lambda i, at: (at[0], i))
    return pl.pallas_call(
        functools.partial(join_kernel, len(flows)),
        grid_spec=pltpu.PrefetchScalarGridSpec(
            num_scalar_prefetch=1,
            grid=(cols // half,),
            in_specs=[row] * len(flows) + [chosen] * 2,
            out_specs=row,
        ),
        out_shape=jax.ShapeDtypeStruct((depth, cols), dtype),
        compiler_params=pltpu.CompilerParams(vmem_limit_bytes=24 * 2**20),
        cost_estimate=FREE,
        name="join",
    )(owner.astype(jnp.int32).reshape(1), *flows, near, other)


def last_join_kernel(at_ref, flow_ref, near_ref, other_ref, *out_refs):
    total = flow_ref[...].astype(F32) + near_ref[...].astype(F32) + other_ref[...].astype(F32)
    width = total.shape[1] // len(out_refs)
    for k, out_ref in enumerate(out_refs):
        cols = out_ref.shape[1]
        out_ref[...] = total[:, k * width : k * width + cols]


def last_join(owner, flow, near, other, ring, cols, count):
    depth, wide = near.shape[0] // ring, near.shape[1]
    chosen = pl.BlockSpec((depth, wide), lambda i, at: (at[0], 0))
    return pl.pallas_call(
        last_join_kernel,
        grid_spec=pltpu.PrefetchScalarGridSpec(
            num_scalar_prefetch=1,
            grid=(1,),
            in_specs=[pl.BlockSpec((depth, wide), lambda i, at: (0, 0)), chosen, chosen],
            out_specs=[pl.BlockSpec((depth, cols), lambda i, at: (0, 0))] * count,
        ),
        out_shape=[jax.ShapeDtypeStruct((depth, cols), F32)] * count,
        compiler_params=pltpu.CompilerParams(vmem_limit_bytes=56 * 2**20),
        cost_estimate=FREE,
        name="last_join",
    )(owner.astype(jnp.int32).reshape(1), flow, near, other)


def cut_kernel(widths, grads_ref, *out_refs):
    first = 0
    for cols, out_ref in zip(widths[:-1], out_refs):
        out_ref[...] = grads_ref[:, first : first + cols].astype(F32)
        first += cols
    out_refs[-1][...] = grads_ref[:, first : first + widths[-1]].astype(F32).T


def cut_grads(grads, widths):
    depth = grads.shape[0]
    whole = lambda shape: pl.BlockSpec(shape, lambda i: (0, 0))
    shapes = [(depth, cols) for cols in widths[:-1]] + [(widths[-1], depth)]
    return pl.pallas_call(
        functools.partial(cut_kernel, widths),
        grid=(1,),
        in_specs=[whole(grads.shape)],
        out_specs=[whole(shape) for shape in shapes],
        out_shape=[jax.ShapeDtypeStruct(shape, F32) for shape in shapes],
        compiler_params=pltpu.CompilerParams(vmem_limit_bytes=24 * 2**20),
        cost_estimate=FREE,
        name="cut_grads",
    )(grads)


def sum_kernel(count, base_ref, *refs):
    total = base_ref[...].astype(F32)
    arrived = refs[0][...].astype(F32)
    for ref in refs[1:count]:
        arrived = arrived + ref[...].astype(F32)
    total = total + arrived
    refs[-1 if len(refs) == count + 1 else -2][...] = total
    if len(refs) > count + 1:
        gain_ref = refs[count]
        inverse = lax.rsqrt(jnp.mean(total * total, axis=-1, keepdims=True) + EPSILON)
        refs[-1][...] = (total * inverse * gain_ref[...]).astype(LOW)


def sum_up(base, parts, gain=None):
    rows, width = base.shape
    step = rows // 2
    by_row = pl.BlockSpec((step, width), lambda i: (i, 0))
    gains = [] if gain is None else [gain.reshape(1, -1)]
    outs = [jax.ShapeDtypeStruct((rows, width), F32)]
    if gains:
        outs.append(jax.ShapeDtypeStruct((rows, width), LOW))
    return pl.pallas_call(
        functools.partial(sum_kernel, len(parts)),
        grid=(2,),
        in_specs=[by_row] * (1 + len(parts)) + [pl.BlockSpec((1, width), lambda i: (0, 0))] * len(gains),
        out_specs=[by_row] * len(outs),
        out_shape=outs,
        compiler_params=pltpu.CompilerParams(vmem_limit_bytes=56 * 2**20),
        cost_estimate=FREE,
        name="sum_up",
    )(base, *parts, *gains)


def norm_back_kernel(count, value_ref, gain_ref, rest_ref, *refs):
    parts, outs = refs[:count], refs[count:]
    value = value_ref[...].astype(F32)
    grad = parts[0][...].astype(F32)
    for ref in parts[1:]:
        grad = grad + ref[...].astype(F32)
    inverse = lax.rsqrt(jnp.mean(value * value, axis=-1, keepdims=True) + EPSILON)
    hat = value * inverse
    scaled = grad * gain_ref[...]
    inner = jnp.mean(scaled * hat, axis=-1, keepdims=True)
    total = rest_ref[...].astype(F32) + (scaled - hat * inner) * inverse
    outs[0][...] = total
    if len(outs) > 1:
        outs[1][...] = total.astype(LOW)

        @pl.when(pl.program_id(0) == 0)
        def _():
            outs[2][...] = jnp.zeros_like(outs[2])

        outs[2][...] += jnp.sum(grad * hat, axis=0, keepdims=True)


def norm_back_sum(value, gain, rest, parts, more):
    rows, width = value.shape
    step = rows // 2
    by_row = pl.BlockSpec((step, width), lambda i: (i, 0))
    fixed = pl.BlockSpec((1, width), lambda i: (0, 0))
    shapes = [jax.ShapeDtypeStruct((rows, width), F32)]
    if more:
        shapes += [jax.ShapeDtypeStruct((rows, width), LOW), jax.ShapeDtypeStruct((1, width), F32)]
    return pl.pallas_call(
        functools.partial(norm_back_kernel, len(parts)),
        grid=(2,),
        in_specs=[by_row, fixed, by_row] + [by_row] * len(parts),
        out_specs=[by_row, by_row, fixed][: len(shapes)],
        out_shape=shapes,
        compiler_params=pltpu.CompilerParams(vmem_limit_bytes=56 * 2**20),
        cost_estimate=FREE,
        name="norm_back_sum",
    )(value, gain.reshape(1, -1), rest, *parts)


def rows_product_kernel(left_ref, right_ref, out_ref):
    out_ref[...] = jnp.dot(left_ref[...], right_ref[0], preferred_element_type=F32).astype(LOW)


def rows_product(left, right, ranks):
    length, depth = left.shape
    rows = length // ranks
    return pl.pallas_call(
        rows_product_kernel,
        grid=(ranks,),
        in_specs=[
            pl.BlockSpec((rows, depth), lambda i: (i, 0)),
            pl.BlockSpec((1,) + right.shape[1:], lambda i: (0, 0, 0)),
        ],
        out_specs=pl.BlockSpec((rows, right.shape[2]), lambda i: (i, 0)),
        out_shape=jax.ShapeDtypeStruct((length, right.shape[2]), LOW),
        compiler_params=pltpu.CompilerParams(vmem_limit_bytes=24 * 2**20),
        cost_estimate=FREE,
        name="rows_product",
    )(left, right)


def gain_parts_kernel(normed_ref, gain_ref, two_ref, heads_ref, *refs):
    parts, out_ref = refs[:-1], refs[-1]
    rows, width = parts[0].shape
    total = jnp.zeros((1, width), F32)
    for j, ref in enumerate(parts):
        block = normed_ref[j * rows : (j + 1) * rows, :].astype(F32)
        total = total + jnp.sum(block * ref[...].astype(F32), axis=0, keepdims=True)
    out_ref[:, :width] = total / gain_ref[...]
    out_ref[:, width : 2 * width] = two_ref[...]
    out_ref[:, 2 * width :] = heads_ref[...]


def gain_parts(normed, gain, parts, two, heads):
    args = [normed, gain.reshape(1, -1), two, heads, *parts]
    whole = lambda a: pl.BlockSpec(a.shape, lambda i: (0, 0))
    shape = jax.ShapeDtypeStruct((1, 2 * normed.shape[1] + heads.shape[1]), F32)
    return pl.pallas_call(
        gain_parts_kernel,
        grid=(1,),
        in_specs=[whole(a) for a in args],
        out_specs=whole(shape),
        out_shape=shape,
        compiler_params=pltpu.CompilerParams(vmem_limit_bytes=56 * 2**20),
        cost_estimate=FREE,
        name="gain_parts",
    )(*args)


def group_mean(values):
    width = values.shape[1]
    part = 2 * HEAD_SIZE
    left = lax.broadcasted_iota(jnp.int32, (part, part), 0) // HEAD_SIZE
    right = lax.broadcasted_iota(jnp.int32, (part, part), 1) // HEAD_SIZE
    spread = jnp.where(left == right, 1.0 / HEAD_SIZE, 0.0).astype(F32)
    pieces = []
    for first in range(0, width, part):
        size = min(part, width - first)
        pieces.append(
            lax.dot_general(
                values[:, first : first + size],
                spread[:size, :size],
                NN,
                precision=lax.Precision.HIGHEST,
                preferred_element_type=F32,
            )
        )
    return jnp.concatenate(pieces, axis=1) if len(pieces) > 1 else pieces[0]


def across(table, width):
    part = table.shape[1]
    if width < part:
        return table[:, :width]
    return jnp.concatenate([table] * (width // part) + ([table[:, : width % part]] if width % part else []), axis=1)


def partner(values):
    width = values.shape[1]
    half = HEAD_SIZE // 2
    lane = lax.broadcasted_iota(jnp.int32, values.shape, 1) % HEAD_SIZE
    return jnp.where(lane < half, pltpu.roll(values, width - half, 1), pltpu.roll(values, half, 1))


def prepare_kernel(q_cols, kv_cols, x_ref, w_ref, cos_ref, sin_ref, gain_ref, q_ref, k_ref, v_ref, raw_ref):
    product = jnp.dot(x_ref[...], w_ref[...], preferred_element_type=F32)
    for first, cols, to in ((0, q_cols, q_ref), (q_cols, kv_cols, k_ref)):
        raw = product[:, first : first + cols]
        scaled = raw * lax.rsqrt(group_mean(raw * raw) + EPSILON) * gain_ref[:, first : first + cols]
        cos = across(cos_ref[...], cols)
        sin = across(sin_ref[...], cols)
        to[...] = (scaled * cos + partner(scaled) * sin).astype(LOW)
        raw_ref[:, first : first + cols] = raw
    v_ref[...] = product[:, q_cols + kv_cols :].astype(LOW)


def prepare(normed, weight, cosine, sine, gains, q_cols, kv_cols, ranks):
    length, width = normed.shape
    rows = length // ranks
    at_row = lambda i: (i, 0)
    fixed = lambda i: (0, 0)
    return pl.pallas_call(
        functools.partial(prepare_kernel, q_cols, kv_cols),
        grid=(ranks,),
        in_specs=[
            pl.BlockSpec((rows, width), at_row),
            pl.BlockSpec(weight.shape, fixed),
            pl.BlockSpec((rows, cosine.shape[1]), at_row),
            pl.BlockSpec((rows, cosine.shape[1]), at_row),
            pl.BlockSpec((1, q_cols + kv_cols), fixed),
        ],
        out_specs=[
            pl.BlockSpec((rows, q_cols), at_row),
            pl.BlockSpec((rows, kv_cols), at_row),
            pl.BlockSpec((rows, kv_cols), at_row),
            pl.BlockSpec((rows, q_cols + kv_cols), at_row),
        ],
        out_shape=[
            jax.ShapeDtypeStruct((length, q_cols), LOW),
            jax.ShapeDtypeStruct((length, kv_cols), LOW),
            jax.ShapeDtypeStruct((length, kv_cols), LOW),
            jax.ShapeDtypeStruct((length, q_cols + kv_cols), F32),
        ],
        compiler_params=pltpu.CompilerParams(vmem_limit_bytes=40 * 2**20),
        cost_estimate=FREE,
        name="prepare",
    )(normed, weight, cosine, sine, gains)


def prepare_back_kernel(
    q_cols, kv_cols, dq_ref, dk_ref, dv_ref, raw_ref, cos_ref, sin_ref, gain_ref, out_ref, gain_grad_ref
):
    @pl.when(pl.program_id(0) == 0)
    def _():
        gain_grad_ref[...] = jnp.zeros_like(gain_grad_ref)

    for first, cols, grad_ref in ((0, q_cols, dq_ref), (q_cols, kv_cols, dk_ref)):
        span = slice(first, first + cols)
        grad = grad_ref[...]
        turned = grad * across(cos_ref[...], cols) - partner(grad) * across(sin_ref[...], cols)
        raw = raw_ref[:, span]
        inverse = lax.rsqrt(group_mean(raw * raw) + EPSILON)
        hat = raw * inverse
        gain_grad_ref[:, span] += jnp.sum(turned * hat, axis=0, keepdims=True)
        scaled = turned * gain_ref[:, span]
        out_ref[:, span] = ((scaled - hat * group_mean(scaled * hat)) * inverse).astype(LOW)
    out_ref[:, q_cols + kv_cols :] = dv_ref[...].astype(LOW)


def prepare_back(d_queries, d_keys, d_values, raw, cosine, sine, gains, ranks):
    length, q_cols = d_queries.shape
    kv_cols = d_keys.shape[1]
    rows = length // ranks
    at_row = lambda i: (i, 0)
    fixed = lambda i: (0, 0)
    return pl.pallas_call(
        functools.partial(prepare_back_kernel, q_cols, kv_cols),
        grid=(ranks,),
        in_specs=[
            pl.BlockSpec((rows, q_cols), at_row),
            pl.BlockSpec((rows, kv_cols), at_row),
            pl.BlockSpec((rows, kv_cols), at_row),
            pl.BlockSpec((rows, q_cols + kv_cols), at_row),
            pl.BlockSpec((rows, cosine.shape[1]), at_row),
            pl.BlockSpec((rows, cosine.shape[1]), at_row),
            pl.BlockSpec((1, q_cols + kv_cols), fixed),
        ],
        out_specs=[
            pl.BlockSpec((rows, q_cols + 2 * kv_cols), at_row),
            pl.BlockSpec((1, q_cols + kv_cols), fixed),
        ],
        out_shape=[
            jax.ShapeDtypeStruct((length, q_cols + 2 * kv_cols), LOW),
            jax.ShapeDtypeStruct((1, q_cols + kv_cols), F32),
        ],
        compiler_params=pltpu.CompilerParams(vmem_limit_bytes=56 * 2**20),
        cost_estimate=FREE,
        name="prepare_back",
    )(d_queries, d_keys, d_values, raw, cosine, sine, gains)


def shards(
    dp_size,
    ranks,
    tokens,
    segments,
    attn_gain,
    w_query,
    key_weight,
    value_weight,
    query_gain,
    key_gain,
    w_out,
    ffn_gain,
    w_gate,
    w_up,
    w_down,
    cotangent,
):
    ring = dp_size // 2
    index = lax.axis_index("dp")
    stage = index // 2
    core = index % 2
    me = lax.axis_index("tensor")
    swap_pairs = [(i, i ^ 1) for i in range(dp_size)]
    ring_pairs = [(i, (i + 2) % dp_size) for i in range(dp_size)]
    heads = KEY_VALUE_HEADS // ranks
    rows = tokens.shape[0]
    length = segments.shape[0]
    q_cols = w_query.shape[1]
    kv_cols = key_weight.shape[1]

    hidden_cols = w_gate.shape[1]
    hidden_pad = -hidden_cols % 128

    def widen(weight):
        return jnp.pad(weight, ((0, 0), (0, hidden_pad)))

    def swap(v):
        return lax.ppermute(v, "dp", swap_pairs)

    def onward(v):
        return lax.ppermute(v, "dp", ring_pairs)

    core_array = core.astype(jnp.int32).reshape(1)
    at = jnp.stack([stage, core]).astype(jnp.int32)

    def hop(label, block):
        with jax.named_scope(label):
            return onward(block)

    def owner_after(count):
        return lax.rem(stage - 1 - count + 2 * ring, ring)

    def spread(label, block):
        with jax.named_scope(label):
            return [block] + [
                lax.ppermute(block, "tensor", [(i, i ^ j) for i in range(ranks)])
                for j in range(1, ranks)
            ]

    def send_parts(label, parts):
        with jax.named_scope(label):
            return [
                lax.ppermute(parts[j], "tensor", [(i, i ^ j) for i in range(ranks)])
                for j in range(1, ranks)
            ]

    def add_up(own, arrived):
        total = own.astype(F32)
        for piece in arrived:
            total = total + piece.astype(F32)
        return total

    def cut(matrix):
        return [matrix[j * rows : (j + 1) * rows] for j in range(ranks)]

    def tie(value, *others):
        return lax.optimization_barrier((value,) + others)[0]

    tokens_wide = tokens.astype(F32)
    normed_own = norm_rows(tokens_wide, attn_gain).astype(LOW)
    normed_one = spread("one_spread", normed_own)
    wide = hidden_cols + hidden_pad
    qkv_blocks = [jnp.concatenate([w_query, key_weight, value_weight], axis=1)]
    for count in range(1, ring):
        qkv_blocks.append(hop(f"qkv_hop{count}", qkv_blocks[-1]))
    ffn_full = lax.all_gather(
        tie(jnp.stack([widen(w_down.T), widen(w_gate), widen(w_up)]), qkv_blocks[2]),
        "dp",
        axis=1,
        tiled=True,
    )
    gate_full, up_full = ffn_full[1], ffn_full[2]
    grad_blocks = spread("cot_spread", tie(cotangent, *normed_one))
    first_start = jnp.sum((segments < 1).astype(jnp.int32))
    second_start = jnp.sum((segments < 2).astype(jnp.int32))
    ids = jnp.arange(length, dtype=jnp.int32).reshape(ranks, rows)
    begins = jnp.where(segments == 0, 0, jnp.where(segments == 1, first_start, second_start))
    begins = begins.astype(jnp.int32).reshape(ranks, rows)
    order = [me ^ j for j in range(ranks)]
    bounds = jnp.stack([lax.dynamic_index_in_dim(begins, o, 0, keepdims=False) for o in order])
    here = jnp.stack([lax.dynamic_index_in_dim(ids, o, 0, keepdims=False) for o in order])
    positions = (here - bounds).reshape(length).astype(F32)
    bounds = bounds.reshape(ranks, 1, rows)
    half = HEAD_SIZE // 2
    freqs = ROTARY_BASE ** (-2.0 * jnp.arange(half, dtype=F32) / HEAD_SIZE)
    angles = positions[:, None] * jnp.concatenate([freqs] * 4)[None, :]
    signs = jnp.concatenate([-jnp.ones(half, F32), jnp.ones(half, F32)] * 2)
    cosine = jnp.cos(angles)
    sine = jnp.sin(angles) * signs[None, :]
    head_gains = jnp.concatenate(
        [query_gain] * (q_cols // HEAD_SIZE) + [key_gain] * (kv_cols // HEAD_SIZE)
    ).reshape(1, -1)

    out_blocks = [w_out.T]
    normed_all, normed_one_t = fold(core_array, normed_one, ring)
    for count in range(1, ring):
        out_flow = hop(f"out_hop{count}", out_blocks[-1])
        if count < ring - 1:
            before = (cosine, sine, head_gains, bounds) if count == 1 else (normed_all,)
            out_blocks.append(tie(out_flow, qkv_blocks[count + 1], *before))

    def complete(blocks):
        return place(at, [b for block in blocks for b in (block, swap(block))], ring)

    w_qkv = complete(qkv_blocks)
    query_low, key_low, value_low, raw = prepare(
        normed_all, w_qkv, cosine, sine, head_gains, q_cols, kv_cols, ranks
    )
    me_array = me.astype(jnp.int32).reshape(1)
    attended, lse = attend(me_array, query_low, key_low, value_low, bounds, ranks, heads)

    attended_go = tie(attended, *grad_blocks)
    out_blocks.append(tie(out_flow, attended))
    out_t = complete(out_blocks)
    attn_parts = back_parts([attended_go], out_t[None], (0,), ranks)
    attn_arrived = send_parts("attn_sum", attn_parts)
    grad_all, grad_t = fold(core_array, [tie(grad_blocks[0], *attn_parts)] + grad_blocks[1:], ring)
    attn_arrived[0] = tie(attn_arrived[0], grad_all)
    hidden, normed_two_own = sum_up(tokens, [attn_parts[0]] + attn_arrived, ffn_gain)
    normed_two = spread("two_spread", normed_two_own)
    d_activation = rows_product(grad_all, ffn_full, ranks)
    normed_two[-1] = tie(normed_two[-1], d_activation)
    normed_two_all, normed_two_t, *normed_two_pair = fold(core_array, normed_two, ring, True)

    gating = mm(normed_two_all, gate_full).astype(LOW).astype(F32)
    lifted = mm(normed_two_all, up_full)
    gate_sig = jax.nn.sigmoid(gating)
    silu = gating * gate_sig
    activation = (silu * lifted).astype(LOW)
    d_act_wide = d_activation.astype(F32)
    d_gating = (d_act_wide * lifted * gate_sig * (1.0 + gating * (1.0 - gate_sig))).astype(LOW)
    d_lifted = (d_act_wide * silu).astype(LOW)

    last = ring - 1

    def advance(label, flow, near, other, count):
        if count == last:
            return join(owner_after(count), flow, near, other, ring, F32), None
        block = join(owner_after(count), flow, near, other, ring, LOW)
        return block, hop(f"{label}_hop{count + 1}", block)

    def several(label, block, flow, near, other, first, end, *after):
        for count in range(first, end):
            block, flow = advance(label, tie(flow, *after), near, other, count)
        return block, flow

    down_full_grad = product(grad_t, [activation])
    down_grad = lax.psum_scatter(down_full_grad, "dp", scatter_dimension=0, tiled=True)
    two_parts = back_parts([tie(d_gating, down_full_grad), d_lifted], ffn_full, (1, 2), ranks)
    two_arrived = send_parts("two_sum", two_parts)
    gate_far = product(normed_two_pair[0], [tie(d_gating, *two_parts)])
    gate_near = product(normed_two_pair[1], [tie(d_gating, gate_far)])
    lift_full_grad = product(normed_two_t, [tie(d_lifted, gate_near)])
    *two_arrived, gate_far, gate_near, lift_full_grad = lax.optimization_barrier(
        (*two_arrived, gate_far, gate_near, lift_full_grad)
    )
    gate_other = swap(gate_far)
    d_hidden, d_hidden_low, ffn_gain_part = norm_back_sum(
        hidden, ffn_gain, cotangent, [two_parts[0]] + two_arrived, True
    )
    hidden_grad = spread("dh_spread", d_hidden_low)
    lift_grad = lax.psum_scatter(
        tie(lift_full_grad, down_grad, d_hidden_low), "dp", scatter_dimension=0, tiled=True
    )
    gate_block, gate_flow = advance("gate_grad", None, tie(gate_near, d_hidden_low), gate_other, 0)
    ffn_parts = back_parts([tie(activation, d_hidden_low)], ffn_full, (0,), ranks)
    hidden_grad[1] = tie(hidden_grad[1], *ffn_parts)
    gate_block, gate_flow = several(
        "gate_grad", gate_block, gate_flow, gate_near, gate_other, 1, last - 1, hidden_grad[1]
    )
    hidden_grad[-1] = tie(hidden_grad[-1], gate_block)
    hidden_grad_all, hidden_grad_t = fold(core_array, hidden_grad, ring)
    ffn_go = lax.optimization_barrier(tuple(ffn_parts) + tuple(hidden_grad))[:ranks]
    ffn_arrived = send_parts("ffn_sum", ffn_go)
    d_attended = rows_product(hidden_grad_all, out_t[None], ranks)
    d_queries, d_keys, d_values = attend_back(
        me_array, query_low, key_low, value_low, bounds, attended, d_attended, lse, ranks, heads
    )
    d_raw, head_gain_parts = prepare_back(
        d_queries, d_keys, d_values, raw, cosine, sine, head_gains, ranks
    )
    gate_block, gate_flow = advance(
        "gate_grad", tie(gate_flow, *ffn_arrived), gate_near, gate_other, last - 1
    )
    one_parts = back_parts([tie(d_raw, gate_block, *ffn_arrived)], w_qkv[None], (0,), ranks)
    one_arrived = send_parts("one_sum", one_parts)
    attn_full_grad = attn_products([normed_one_t, hidden_grad_t], [tie(d_raw, *one_parts), attended])
    attn_grad = lax.psum_scatter(
        tie(attn_full_grad, lift_grad), "dp", scatter_dimension=0, tiled=True)
    gains = gain_parts(
        tie(normed_all, attn_full_grad), attn_gain, one_parts, ffn_gain_part, head_gain_parts
    )
    (output,) = sum_up(tie(hidden, gains), [ffn_parts[0]] + ffn_arrived)

    def exchange_sum(own, axis, offsets, size):
        pieces = [own] + [lax.ppermute(own, axis, [(i, i ^ j) for i in range(size)]) for j in offsets]
        while len(pieces) > 1:
            pieces = [a + b for a, b in zip(pieces[::2], pieces[1::2])]
        return pieces[0]

    (gate_grad,) = last_join(
        owner_after(last), tie(gate_flow, output), gate_near, gate_other, ring, hidden_cols, 1
    )
    one_arrived[-1] = tie(one_arrived[-1], output, gains, gate_grad)
    (tokens_grad,) = norm_back_sum(tokens, attn_gain, d_hidden, [one_parts[0]] + one_arrived, False)
    lift_grad = lift_grad[:, :hidden_cols].astype(F32)
    query_grad, key_grad, value_grad, out_grad = cut_grads(
        attn_grad, (q_cols, kv_cols, kv_cols, q_cols)
    )
    down_grad = down_grad[:, :hidden_cols].astype(F32)

    total = exchange_sum(tie(gains, tokens_grad), "tensor", range(1, ranks), ranks)
    total = exchange_sum(total, "dp", range(1, 2), dp_size)
    total = exchange_sum(total, "dp", range(2, dp_size, 2), dp_size)
    total = total.reshape(-1)
    a, b = attn_gain.shape[0], 2 * attn_gain.shape[0]
    query_gain_grad = jnp.sum(total[b : b + q_cols].reshape(-1, HEAD_SIZE), axis=0)
    key_gain_grad = jnp.sum(total[b + q_cols :].reshape(-1, HEAD_SIZE), axis=0)
    return (
        output,
        tokens_grad,
        total[:a],
        query_grad,
        key_grad,
        value_grad,
        query_gain_grad,
        key_gain_grad,
        out_grad,
        total[a:b],
        gate_grad,
        lift_grad,
        down_grad.T,
    )


def solution(mesh):
    in_specs = (
        P(("dp", "tensor"), None),
        P("dp"),
        P(),
        P("dp", "tensor"),
        P("dp", "tensor"),
        P("dp", "tensor"),
        P(),
        P(),
        P("tensor", "dp"),
        P(),
        P("dp", "tensor"),
        P("dp", "tensor"),
        P("tensor", "dp"),
        P(("dp", "tensor"), None),
    )
    out_specs = (
        P(("dp", "tensor"), None),
        P(("dp", "tensor"), None),
        P(),
        P("dp", "tensor"),
        P("dp", "tensor"),
        P("dp", "tensor"),
        P(),
        P(),
        P("tensor", "dp"),
        P(),
        P("dp", "tensor"),
        P("dp", "tensor"),
        P("tensor", "dp"),
    )
    body = functools.partial(shards, mesh.shape["dp"], mesh.shape["tensor"])
    return jax.shard_map(body, mesh=mesh, in_specs=in_specs, out_specs=out_specs, check_vma=False)
```

```python
import functools

import jax
import jax.numpy as jnp
from jax import lax
from jax.experimental import pallas as pl
from jax.experimental.pallas import tpu as pltpu
from jax.sharding import PartitionSpec as P

QUERY_HEADS = 24
KEY_VALUE_HEADS = 8
HEAD_SIZE = 64
GROUP = QUERY_HEADS // KEY_VALUE_HEADS
EPSILON = 1e-05
ROTARY_BASE = 1000000.0
NEGATIVE_FILL = -1e30
F32 = jnp.float32
LOW = jnp.bfloat16
SCALE = HEAD_SIZE ** (-0.5)
FREE = pl.CostEstimate(flops=0, bytes_accessed=0, transcendentals=0)


def norm_rows(values_in, gain):
    return (
        values_in
        * lax.rsqrt(jnp.mean(values_in * values_in, axis=-1, keepdims=True) + EPSILON)
        * gain
    )


def norm_back(values, gain, grad):
    inverse = lax.rsqrt(jnp.mean(values * values, axis=-1, keepdims=True) + EPSILON)
    hat = values * inverse
    scaled = grad * gain
    inner = jnp.mean(scaled * hat, axis=-1, keepdims=True)
    return (scaled - hat * inner) * inverse, jnp.sum(grad * hat, axis=0)


def mm(left, right):
    return jnp.dot(left, right, preferred_element_type=F32)


def cross_rows(left, right):
    return lax.dot_general(left, right, (((1,), (1,)), ((), ())), preferred_element_type=F32)


def cross_cols(left, right):
    return lax.dot_general(left, right, (((0,), (0,)), ((), ())), preferred_element_type=F32)


NT = (((1,), (1,)), ((), ()))
NN = (((1,), (0,)), ((), ()))
TN = (((0,), (0,)), ((), ()))


def kdot(left, right, dims):
    return lax.dot_general(left, right, dims, preferred_element_type=F32)


def stack_heads(block, head):
    first = head * GROUP * HEAD_SIZE
    return jnp.concatenate(
        [block[:, first + g * HEAD_SIZE : first + (g + 1) * HEAD_SIZE] for g in range(GROUP)], axis=0
    )


def attend_kernel(heads, rows, me_ref, q_ref, k_ref, v_ref, lo_ref, out_ref, lse_ref):
    me = me_ref[0]
    block = pl.program_id(0) ^ me
    low_bound = jnp.concatenate([lo_ref[0]] * GROUP, axis=1)
    row_ids = block * rows + lax.broadcasted_iota(jnp.int32, (1, rows), 1)
    row_ids = jnp.concatenate([row_ids] * GROUP, axis=1)
    width = GROUP * rows
    queries = q_ref[...] * SCALE
    pieces = []
    for head in range(heads):
        q3 = stack_heads(queries, head)
        cols = slice(head * HEAD_SIZE, (head + 1) * HEAD_SIZE)

        def step(other, carry, q3=q3, cols=cols):
            peak, total, acc = carry
            first = pl.multiple_of((other ^ me) * rows, rows)
            keys = k_ref[pl.ds(first, rows), cols]
            vals = v_ref[pl.ds(first, rows), cols]
            ids = other * rows + lax.broadcasted_iota(jnp.int32, (rows, 1), 0)
            scores = kdot(keys, q3, NT)
            scores = jnp.where((ids <= row_ids) & (ids >= low_bound), scores, NEGATIVE_FILL)
            higher = jnp.maximum(peak, jnp.max(scores, axis=0, keepdims=True))
            fade = jnp.exp(peak - higher)
            exps = jnp.exp(scores - higher)
            total = total * fade + jnp.sum(exps, axis=0, keepdims=True)
            acc = acc * fade + kdot(vals, exps.astype(LOW), TN)
            return higher, total, acc

        start = (
            jnp.full((1, width), NEGATIVE_FILL, F32),
            jnp.zeros((1, width), F32),
            jnp.zeros((HEAD_SIZE, width), F32),
        )
        start = step(block, start)
        peak, total, acc = lax.fori_loop(0, block, step, start)
        acc = acc / total
        lse_ref[0, head : head + 1, :] = peak + jnp.log(total)
        pieces += [acc[:, g * rows : (g + 1) * rows] for g in range(GROUP)]
    out_ref[...] = jnp.concatenate(pieces, axis=0).T.astype(LOW)


def attend_back_kernel(
    heads, rows, me_ref, q_ref, k_ref, v_ref, lo_ref, o_ref, do_ref, lse_ref, dq_ref, dk_ref, dv_ref
):
    me = me_ref[0]

    @pl.when(pl.program_id(0) == 0)
    def _():
        dk_ref[...] = jnp.zeros_like(dk_ref)
        dv_ref[...] = jnp.zeros_like(dv_ref)

    block = pl.program_id(0) ^ me
    low_bound = jnp.concatenate([lo_ref[0]] * GROUP, axis=1)
    row_ids = block * rows + lax.broadcasted_iota(jnp.int32, (1, rows), 1)
    row_ids = jnp.concatenate([row_ids] * GROUP, axis=1)
    width = GROUP * rows
    queries = q_ref[...] * SCALE
    grads = do_ref[...]
    product = (grads.astype(F32) * o_ref[...].astype(F32)).T
    pieces = []
    for head in range(heads):
        q3 = stack_heads(queries, head)
        do3 = stack_heads(grads, head)
        cols = slice(head * HEAD_SIZE, (head + 1) * HEAD_SIZE)
        first_row = head * GROUP * HEAD_SIZE
        inner = jnp.concatenate(
            [
                jnp.sum(
                    product[first_row + g * HEAD_SIZE : first_row + (g + 1) * HEAD_SIZE],
                    axis=0,
                    keepdims=True,
                )
                for g in range(GROUP)
            ],
            axis=1,
        )
        lse = lse_ref[0, head : head + 1, :]

        def step(other, acc, q3=q3, do3=do3, cols=cols, inner=inner, lse=lse):
            first = pl.multiple_of((other ^ me) * rows, rows)
            place = pl.ds(first, rows)
            keys = k_ref[place, cols]
            vals = v_ref[place, cols]
            ids = other * rows + lax.broadcasted_iota(jnp.int32, (rows, 1), 0)
            scores = kdot(keys, q3, NT)
            scores = jnp.where((ids <= row_ids) & (ids >= low_bound), scores, NEGATIVE_FILL)
            probs = jnp.exp(scores - lse)
            d_probs = kdot(vals, do3, NT)
            d_scores = (probs * (d_probs - inner)).astype(LOW)
            dk_ref[place, cols] += kdot(d_scores, q3, NN)
            dv_ref[place, cols] += kdot(probs.astype(LOW), do3, NN)
            return acc + kdot(keys, d_scores, TN)

        acc = lax.fori_loop(0, block + 1, step, jnp.zeros((HEAD_SIZE, width), F32))
        pieces += [acc[:, g * rows : (g + 1) * rows] for g in range(GROUP)]
    dq_ref[...] = jnp.concatenate(pieces, axis=0).T * SCALE


def attention_specs(ranks, rows, heads):
    length = ranks * rows
    q_spec = pl.BlockSpec((rows, heads * GROUP * HEAD_SIZE), lambda i, me: (i, 0))
    kv_spec = pl.BlockSpec((length, heads * HEAD_SIZE), lambda i, me: (0, 0))
    lo_spec = pl.BlockSpec((1, 1, rows), lambda i, me: (i, 0, 0))
    lse_spec = pl.BlockSpec((1, heads, GROUP * rows), lambda i, me: (i, 0, 0))
    return q_spec, kv_spec, lo_spec, lse_spec


def attend(me, queries, keys, values, bounds, ranks, heads):
    length = queries.shape[0]
    rows = length // ranks
    q_spec, kv_spec, lo_spec, lse_spec = attention_specs(ranks, rows, heads)
    return pl.pallas_call(
        functools.partial(attend_kernel, heads, rows),
        grid_spec=pltpu.PrefetchScalarGridSpec(
            num_scalar_prefetch=1,
            grid=(ranks,),
            in_specs=[q_spec, kv_spec, kv_spec, lo_spec],
            out_specs=[q_spec, lse_spec],
        ),
        out_shape=[
            jax.ShapeDtypeStruct(queries.shape, LOW),
            jax.ShapeDtypeStruct((ranks, heads, GROUP * rows), F32),
        ],
        compiler_params=pltpu.CompilerParams(vmem_limit_bytes=48 * 2**20),
        cost_estimate=pl.CostEstimate(
            flops=16 * length * length * heads * GROUP * HEAD_SIZE,
            bytes_accessed=32 * 2**20,
            transcendentals=length * length * heads * GROUP,
        ),
        name="attend",
    )(me, queries, keys, values, bounds)


def attend_back(me, queries, keys, values, bounds, attended, d_attended, lse, ranks, heads):
    length = queries.shape[0]
    rows = length // ranks
    q_spec, kv_spec, lo_spec, lse_spec = attention_specs(ranks, rows, heads)
    return pl.pallas_call(
        functools.partial(attend_back_kernel, heads, rows),
        grid_spec=pltpu.PrefetchScalarGridSpec(
            num_scalar_prefetch=1,
            grid=(ranks,),
            in_specs=[q_spec, kv_spec, kv_spec, lo_spec, q_spec, q_spec, lse_spec],
            out_specs=[q_spec, kv_spec, kv_spec],
        ),
        out_shape=[
            jax.ShapeDtypeStruct(queries.shape, F32),
            jax.ShapeDtypeStruct(keys.shape, F32),
            jax.ShapeDtypeStruct(keys.shape, F32),
        ],
        compiler_params=pltpu.CompilerParams(vmem_limit_bytes=48 * 2**20),
        cost_estimate=FREE,
        name="attend_back",
    )(me, queries, keys, values, bounds, attended, d_attended, lse)


def fold_kernel(ranks, ring, rows, core_ref, *refs):
    blocks, (all_ref, turned_ref), split = refs[:ranks], refs[ranks : ranks + 2], refs[ranks + 2 :]
    core = core_ref[0]
    depth = turned_ref.shape[0] // (2 * ring)
    for j in range(ranks):
        block = blocks[j][...]
        span = slice(j * rows, (j + 1) * rows)
        all_ref[span, :] = block
        turned_ref[:, span] = block.T
        if split:
            for i in range(ring):
                to = slice(i * depth, (i + 1) * depth)
                for side_ref, side in zip(split, (1 - core, core)):
                    first = pl.multiple_of((2 * i + side) * depth, 16)
                    side_ref[to, span] = turned_ref[pl.ds(first, depth), span]


def fold(core, blocks, ring, split=False):
    ranks = len(blocks)
    rows, width = blocks[0].shape
    length = ranks * rows
    whole = lambda shape: pl.BlockSpec(shape, lambda i: (0, 0))
    shapes = [(length, width), (width, length)] + ([(width // 2, length)] * 2 if split else [])
    return pl.pallas_call(
        functools.partial(fold_kernel, ranks, ring, rows),
        grid=(1,),
        in_specs=[pl.BlockSpec(memory_space=pltpu.SMEM)] + [whole((rows, width))] * ranks,
        out_specs=[whole(shape) for shape in shapes],
        out_shape=[jax.ShapeDtypeStruct(shape, LOW) for shape in shapes],
        compiler_params=pltpu.CompilerParams(vmem_limit_bytes=40 * 2**20),
        cost_estimate=FREE,
        name="fold",
    )(core, *blocks)


def place_kernel(ring, depth, at_ref, *refs):
    blocks = refs[: 2 * ring]
    full_ref, sems = refs[2 * ring :]
    stage, core = at_ref[0], at_ref[1]
    copies = []
    for hop in range(ring):
        owner = lax.rem(stage - hop + ring, ring)
        for half, side in enumerate((core, 1 - core)):
            first = pl.multiple_of((owner * 2 + side) * depth, 16)
            copies.append(
                pltpu.make_async_copy(
                    blocks[2 * hop + half], full_ref.at[pl.ds(first, depth)], sems.at[2 * hop + half]
                )
            )
    for copy in copies:
        copy.start()
    for copy in copies:
        copy.wait()


def place(at, blocks, ring):
    depth, cols = blocks[0].shape
    return pl.pallas_call(
        functools.partial(place_kernel, ring, depth),
        in_specs=[pl.BlockSpec(memory_space=pltpu.SMEM)]
        + [pl.BlockSpec(memory_space=pl.ANY)] * (2 * ring),
        grid=(1,),
        out_specs=pl.BlockSpec((2 * ring * depth, cols), lambda i: (0, 0)),
        out_shape=jax.ShapeDtypeStruct((2 * ring * depth, cols), LOW),
        scratch_shapes=[pltpu.SemaphoreType.DMA((2 * ring,))],
        compiler_params=pltpu.CompilerParams(vmem_limit_bytes=24 * 2**20),
        cost_estimate=FREE,
        name="place",
    )(at, *blocks)


def product_kernel(tiles, left_ref, *refs):
    for k, right in enumerate(refs[:-1]):

        @pl.when(pl.program_id(0) // tiles == k)
        def _(right=right):
            refs[-1][...] = jnp.dot(
                left_ref[...], right[...], preferred_element_type=F32
            ).astype(LOW)


def product(left, rights):
    depth, length = left.shape
    cols = rights[0].shape[1]
    tile = 256 if cols % 256 == 0 else 128
    tiles = cols // tile
    return pl.pallas_call(
        functools.partial(product_kernel, tiles),
        grid=(tiles * len(rights),),
        in_specs=[pl.BlockSpec((depth, length), lambda i: (0, 0))]
        + [
            pl.BlockSpec((length, tile), lambda i, k=k: (0, jnp.clip(i - k * tiles, 0, tiles - 1)))
            for k in range(len(rights))
        ],
        out_specs=pl.BlockSpec((depth, tile), lambda i: (0, i)),
        out_shape=jax.ShapeDtypeStruct((depth, cols * len(rights)), LOW),
        compiler_params=pltpu.CompilerParams(vmem_limit_bytes=56 * 2**20),
        cost_estimate=FREE,
        name="product",
    )(left, *rights)


def attn_products_kernel(*refs):
    lefts, rights, out_ref = refs[:2], refs[2:4], refs[4]
    first = 0
    for left, right in zip(lefts, rights):
        cols = right.shape[1]
        out_ref[:, first : first + cols] = jnp.dot(
            left[...], right[...], preferred_element_type=F32
        ).astype(LOW)
        first += cols


def attn_products(lefts, rights):
    depth = lefts[0].shape[0]
    tiles = 4
    part = lambda a: pl.BlockSpec((depth // tiles, a.shape[1]), lambda i: (i, 0))
    whole = lambda a: pl.BlockSpec(a.shape, lambda i: (0, 0))
    shape = jax.ShapeDtypeStruct((depth, sum(a.shape[1] for a in rights)), LOW)
    return pl.pallas_call(
        attn_products_kernel,
        grid=(tiles,),
        in_specs=[part(a) for a in lefts] + [whole(a) for a in rights],
        out_specs=part(shape),
        out_shape=shape,
        compiler_params=pltpu.CompilerParams(vmem_limit_bytes=40 * 2**20),
        cost_estimate=FREE,
        name="attn_products",
    )(*lefts, *rights)


def back_parts_kernel(rows, count, *refs):
    total = sum(kdot(refs[k][...], refs[count + k][0], NT) for k in range(count))
    for j, out_ref in enumerate(refs[2 * count :]):
        out_ref[...] = total[j * rows : (j + 1) * rows].astype(LOW)


def back_parts(lefts, weights, which, ranks):
    length, cols = lefts[0].shape
    width = weights.shape[1]
    rows = length // ranks
    tile = 256
    return pl.pallas_call(
        functools.partial(back_parts_kernel, rows, len(lefts)),
        grid=(width // tile,),
        in_specs=[pl.BlockSpec((length, cols), lambda i: (0, 0))] * len(lefts)
        + [pl.BlockSpec((1, tile, cols), lambda i, k=k: (k, i, 0)) for k in which],
        out_specs=[pl.BlockSpec((rows, tile), lambda i: (0, i))] * ranks,
        out_shape=[jax.ShapeDtypeStruct((rows, width), LOW)] * ranks,
        compiler_params=pltpu.CompilerParams(vmem_limit_bytes=48 * 2**20),
        cost_estimate=FREE,
        name="back_parts",
    )(*lefts, *([weights] * len(which)))


def join_kernel(flows, at_ref, *refs):
    total = refs[flows][...].astype(F32) + refs[flows + 1][...].astype(F32)
    if flows:
        total = total + refs[0][...].astype(F32)
    refs[-1][...] = total.astype(refs[-1].dtype)


def join(owner, flow, near, other, ring, dtype):
    depth, cols = near.shape[0] // ring, near.shape[1]
    flows = [] if flow is None else [flow]
    half = cols // 2 if cols % 256 == 0 else cols
    row = pl.BlockSpec((depth, half), lambda i, at: (0, i))
    chosen = pl.BlockSpec((depth, half), lambda i, at: (at[0], i))
    return pl.pallas_call(
        functools.partial(join_kernel, len(flows)),
        grid_spec=pltpu.PrefetchScalarGridSpec(
            num_scalar_prefetch=1,
            grid=(cols // half,),
            in_specs=[row] * len(flows) + [chosen] * 2,
            out_specs=row,
        ),
        out_shape=jax.ShapeDtypeStruct((depth, cols), dtype),
        compiler_params=pltpu.CompilerParams(vmem_limit_bytes=24 * 2**20),
        cost_estimate=FREE,
        name="join",
    )(owner.astype(jnp.int32).reshape(1), *flows, near, other)


def last_join_kernel(at_ref, flow_ref, near_ref, other_ref, *out_refs):
    total = flow_ref[...].astype(F32) + near_ref[...].astype(F32) + other_ref[...].astype(F32)
    width = total.shape[1] // len(out_refs)
    for k, out_ref in enumerate(out_refs):
        cols = out_ref.shape[1]
        out_ref[...] = total[:, k * width : k * width + cols]


def last_join(owner, flow, near, other, ring, cols, count):
    depth, wide = near.shape[0] // ring, near.shape[1]
    chosen = pl.BlockSpec((depth, wide), lambda i, at: (at[0], 0))
    return pl.pallas_call(
        last_join_kernel,
        grid_spec=pltpu.PrefetchScalarGridSpec(
            num_scalar_prefetch=1,
            grid=(1,),
            in_specs=[pl.BlockSpec((depth, wide), lambda i, at: (0, 0)), chosen, chosen],
            out_specs=[pl.BlockSpec((depth, cols), lambda i, at: (0, 0))] * count,
        ),
        out_shape=[jax.ShapeDtypeStruct((depth, cols), F32)] * count,
        compiler_params=pltpu.CompilerParams(vmem_limit_bytes=56 * 2**20),
        cost_estimate=FREE,
        name="last_join",
    )(owner.astype(jnp.int32).reshape(1), flow, near, other)


def cut_kernel(widths, grads_ref, *out_refs):
    first = 0
    for cols, out_ref in zip(widths[:-1], out_refs):
        out_ref[...] = grads_ref[:, first : first + cols].astype(F32)
        first += cols
    out_refs[-1][...] = grads_ref[:, first : first + widths[-1]].astype(F32).T


def cut_grads(grads, widths):
    depth = grads.shape[0]
    whole = lambda shape: pl.BlockSpec(shape, lambda i: (0, 0))
    shapes = [(depth, cols) for cols in widths[:-1]] + [(widths[-1], depth)]
    return pl.pallas_call(
        functools.partial(cut_kernel, widths),
        grid=(1,),
        in_specs=[whole(grads.shape)],
        out_specs=[whole(shape) for shape in shapes],
        out_shape=[jax.ShapeDtypeStruct(shape, F32) for shape in shapes],
        compiler_params=pltpu.CompilerParams(vmem_limit_bytes=24 * 2**20),
        cost_estimate=FREE,
        name="cut_grads",
    )(grads)


def sum_kernel(count, base_ref, *refs):
    total = base_ref[...].astype(F32)
    arrived = refs[0][...].astype(F32)
    for ref in refs[1:count]:
        arrived = arrived + ref[...].astype(F32)
    total = total + arrived
    refs[-1 if len(refs) == count + 1 else -2][...] = total
    if len(refs) > count + 1:
        gain_ref = refs[count]
        inverse = lax.rsqrt(jnp.mean(total * total, axis=-1, keepdims=True) + EPSILON)
        refs[-1][...] = (total * inverse * gain_ref[...]).astype(LOW)


def sum_up(base, parts, gain=None):
    rows, width = base.shape
    step = rows // 2
    by_row = pl.BlockSpec((step, width), lambda i: (i, 0))
    gains = [] if gain is None else [gain.reshape(1, -1)]
    outs = [jax.ShapeDtypeStruct((rows, width), F32)]
    if gains:
        outs.append(jax.ShapeDtypeStruct((rows, width), LOW))
    return pl.pallas_call(
        functools.partial(sum_kernel, len(parts)),
        grid=(2,),
        in_specs=[by_row] * (1 + len(parts)) + [pl.BlockSpec((1, width), lambda i: (0, 0))] * len(gains),
        out_specs=[by_row] * len(outs),
        out_shape=outs,
        compiler_params=pltpu.CompilerParams(vmem_limit_bytes=56 * 2**20),
        cost_estimate=FREE,
        name="sum_up",
    )(base, *parts, *gains)


def norm_back_kernel(count, value_ref, gain_ref, rest_ref, *refs):
    parts, outs = refs[:count], refs[count:]
    value = value_ref[...].astype(F32)
    grad = parts[0][...].astype(F32)
    for ref in parts[1:]:
        grad = grad + ref[...].astype(F32)
    inverse = lax.rsqrt(jnp.mean(value * value, axis=-1, keepdims=True) + EPSILON)
    hat = value * inverse
    scaled = grad * gain_ref[...]
    inner = jnp.mean(scaled * hat, axis=-1, keepdims=True)
    total = rest_ref[...].astype(F32) + (scaled - hat * inner) * inverse
    outs[0][...] = total
    if len(outs) > 1:
        outs[1][...] = total.astype(LOW)

        @pl.when(pl.program_id(0) == 0)
        def _():
            outs[2][...] = jnp.zeros_like(outs[2])

        outs[2][...] += jnp.sum(grad * hat, axis=0, keepdims=True)


def norm_back_sum(value, gain, rest, parts, more):
    rows, width = value.shape
    step = rows // 2
    by_row = pl.BlockSpec((step, width), lambda i: (i, 0))
    fixed = pl.BlockSpec((1, width), lambda i: (0, 0))
    shapes = [jax.ShapeDtypeStruct((rows, width), F32)]
    if more:
        shapes += [jax.ShapeDtypeStruct((rows, width), LOW), jax.ShapeDtypeStruct((1, width), F32)]
    return pl.pallas_call(
        functools.partial(norm_back_kernel, len(parts)),
        grid=(2,),
        in_specs=[by_row, fixed, by_row] + [by_row] * len(parts),
        out_specs=[by_row, by_row, fixed][: len(shapes)],
        out_shape=shapes,
        compiler_params=pltpu.CompilerParams(vmem_limit_bytes=56 * 2**20),
        cost_estimate=FREE,
        name="norm_back_sum",
    )(value, gain.reshape(1, -1), rest, *parts)


def rows_product_kernel(left_ref, right_ref, out_ref):
    out_ref[...] = jnp.dot(left_ref[...], right_ref[0], preferred_element_type=F32).astype(LOW)


def rows_product(left, right, ranks, grant):
    length, depth = left.shape
    rows = length // ranks
    return pl.pallas_call(
        rows_product_kernel,
        grid=(ranks,),
        in_specs=[
            pl.BlockSpec((rows, depth), lambda i: (i, 0)),
            pl.BlockSpec((1,) + right.shape[1:], lambda i: (0, 0, 0)),
        ],
        out_specs=pl.BlockSpec((rows, right.shape[2]), lambda i: (i, 0)),
        out_shape=jax.ShapeDtypeStruct((length, right.shape[2]), LOW),
        compiler_params=pltpu.CompilerParams(vmem_limit_bytes=grant * 2**20),
        cost_estimate=FREE,
        name="rows_product",
    )(left, right)


def gain_parts_kernel(normed_ref, gain_ref, two_ref, heads_ref, *refs):
    parts, out_ref = refs[:-1], refs[-1]
    rows, width = parts[0].shape
    total = jnp.zeros((1, width), F32)
    for j, ref in enumerate(parts):
        block = normed_ref[j * rows : (j + 1) * rows, :].astype(F32)
        total = total + jnp.sum(block * ref[...].astype(F32), axis=0, keepdims=True)
    out_ref[:, :width] = total / gain_ref[...]
    out_ref[:, width : 2 * width] = two_ref[...]
    out_ref[:, 2 * width :] = heads_ref[...]


def gain_parts(normed, gain, parts, two, heads):
    args = [normed, gain.reshape(1, -1), two, heads, *parts]
    whole = lambda a: pl.BlockSpec(a.shape, lambda i: (0, 0))
    shape = jax.ShapeDtypeStruct((1, 2 * normed.shape[1] + heads.shape[1]), F32)
    return pl.pallas_call(
        gain_parts_kernel,
        grid=(1,),
        in_specs=[whole(a) for a in args],
        out_specs=whole(shape),
        out_shape=shape,
        compiler_params=pltpu.CompilerParams(vmem_limit_bytes=56 * 2**20),
        cost_estimate=FREE,
        name="gain_parts",
    )(*args)


def group_mean(values):
    width = values.shape[1]
    part = 2 * HEAD_SIZE
    left = lax.broadcasted_iota(jnp.int32, (part, part), 0) // HEAD_SIZE
    right = lax.broadcasted_iota(jnp.int32, (part, part), 1) // HEAD_SIZE
    spread = jnp.where(left == right, 1.0 / HEAD_SIZE, 0.0).astype(F32)
    pieces = []
    for first in range(0, width, part):
        size = min(part, width - first)
        pieces.append(
            lax.dot_general(
                values[:, first : first + size],
                spread[:size, :size],
                NN,
                precision=lax.Precision.HIGHEST,
                preferred_element_type=F32,
            )
        )
    return jnp.concatenate(pieces, axis=1) if len(pieces) > 1 else pieces[0]


def across(table, width):
    part = table.shape[1]
    if width < part:
        return table[:, :width]
    return jnp.concatenate([table] * (width // part) + ([table[:, : width % part]] if width % part else []), axis=1)


def partner(values):
    width = values.shape[1]
    half = HEAD_SIZE // 2
    lane = lax.broadcasted_iota(jnp.int32, values.shape, 1) % HEAD_SIZE
    return jnp.where(lane < half, pltpu.roll(values, width - half, 1), pltpu.roll(values, half, 1))


def prepare_kernel(q_cols, kv_cols, x_ref, w_ref, cos_ref, sin_ref, gain_ref, q_ref, k_ref, v_ref, raw_ref):
    product = jnp.dot(x_ref[...], w_ref[...], preferred_element_type=F32)
    for first, cols, to in ((0, q_cols, q_ref), (q_cols, kv_cols, k_ref)):
        raw = product[:, first : first + cols]
        scaled = raw * lax.rsqrt(group_mean(raw * raw) + EPSILON) * gain_ref[:, first : first + cols]
        cos = across(cos_ref[...], cols)
        sin = across(sin_ref[...], cols)
        to[...] = (scaled * cos + partner(scaled) * sin).astype(LOW)
        raw_ref[:, first : first + cols] = raw
    v_ref[...] = product[:, q_cols + kv_cols :].astype(LOW)


def prepare(normed, weight, cosine, sine, gains, q_cols, kv_cols, ranks):
    length, width = normed.shape
    rows = length // ranks
    at_row = lambda i: (i, 0)
    fixed = lambda i: (0, 0)
    return pl.pallas_call(
        functools.partial(prepare_kernel, q_cols, kv_cols),
        grid=(ranks,),
        in_specs=[
            pl.BlockSpec((rows, width), at_row),
            pl.BlockSpec(weight.shape, fixed),
            pl.BlockSpec((rows, cosine.shape[1]), at_row),
            pl.BlockSpec((rows, cosine.shape[1]), at_row),
            pl.BlockSpec((1, q_cols + kv_cols), fixed),
        ],
        out_specs=[
            pl.BlockSpec((rows, q_cols), at_row),
            pl.BlockSpec((rows, kv_cols), at_row),
            pl.BlockSpec((rows, kv_cols), at_row),
            pl.BlockSpec((rows, q_cols + kv_cols), at_row),
        ],
        out_shape=[
            jax.ShapeDtypeStruct((length, q_cols), LOW),
            jax.ShapeDtypeStruct((length, kv_cols), LOW),
            jax.ShapeDtypeStruct((length, kv_cols), LOW),
            jax.ShapeDtypeStruct((length, q_cols + kv_cols), F32),
        ],
        compiler_params=pltpu.CompilerParams(vmem_limit_bytes=40 * 2**20),
        cost_estimate=FREE,
        name="prepare",
    )(normed, weight, cosine, sine, gains)


def prepare_back_kernel(
    q_cols, kv_cols, dq_ref, dk_ref, dv_ref, raw_ref, cos_ref, sin_ref, gain_ref, out_ref, gain_grad_ref
):
    @pl.when(pl.program_id(0) == 0)
    def _():
        gain_grad_ref[...] = jnp.zeros_like(gain_grad_ref)

    for first, cols, grad_ref in ((0, q_cols, dq_ref), (q_cols, kv_cols, dk_ref)):
        span = slice(first, first + cols)
        grad = grad_ref[...]
        turned = grad * across(cos_ref[...], cols) - partner(grad) * across(sin_ref[...], cols)
        raw = raw_ref[:, span]
        inverse = lax.rsqrt(group_mean(raw * raw) + EPSILON)
        hat = raw * inverse
        gain_grad_ref[:, span] += jnp.sum(turned * hat, axis=0, keepdims=True)
        scaled = turned * gain_ref[:, span]
        out_ref[:, span] = ((scaled - hat * group_mean(scaled * hat)) * inverse).astype(LOW)
    out_ref[:, q_cols + kv_cols :] = dv_ref[...].astype(LOW)


def prepare_back(d_queries, d_keys, d_values, raw, cosine, sine, gains, ranks):
    length, q_cols = d_queries.shape
    kv_cols = d_keys.shape[1]
    rows = length // ranks
    at_row = lambda i: (i, 0)
    fixed = lambda i: (0, 0)
    return pl.pallas_call(
        functools.partial(prepare_back_kernel, q_cols, kv_cols),
        grid=(ranks,),
        in_specs=[
            pl.BlockSpec((rows, q_cols), at_row),
            pl.BlockSpec((rows, kv_cols), at_row),
            pl.BlockSpec((rows, kv_cols), at_row),
            pl.BlockSpec((rows, q_cols + kv_cols), at_row),
            pl.BlockSpec((rows, cosine.shape[1]), at_row),
            pl.BlockSpec((rows, cosine.shape[1]), at_row),
            pl.BlockSpec((1, q_cols + kv_cols), fixed),
        ],
        out_specs=[
            pl.BlockSpec((rows, q_cols + 2 * kv_cols), at_row),
            pl.BlockSpec((1, q_cols + kv_cols), fixed),
        ],
        out_shape=[
            jax.ShapeDtypeStruct((length, q_cols + 2 * kv_cols), LOW),
            jax.ShapeDtypeStruct((1, q_cols + kv_cols), F32),
        ],
        compiler_params=pltpu.CompilerParams(vmem_limit_bytes=56 * 2**20),
        cost_estimate=FREE,
        name="prepare_back",
    )(d_queries, d_keys, d_values, raw, cosine, sine, gains)


def shards(
    dp_size,
    ranks,
    tokens,
    segments,
    attn_gain,
    w_query,
    key_weight,
    value_weight,
    query_gain,
    key_gain,
    w_out,
    ffn_gain,
    w_gate,
    w_up,
    w_down,
    cotangent,
):
    ring = dp_size // 2
    index = lax.axis_index("dp")
    stage = index // 2
    core = index % 2
    me = lax.axis_index("tensor")
    swap_pairs = [(i, i ^ 1) for i in range(dp_size)]
    ring_pairs = [(i, (i + 2) % dp_size) for i in range(dp_size)]
    heads = KEY_VALUE_HEADS // ranks
    rows = tokens.shape[0]
    length = segments.shape[0]
    q_cols = w_query.shape[1]
    kv_cols = key_weight.shape[1]

    hidden_cols = w_gate.shape[1]
    hidden_pad = -hidden_cols % 128

    def widen(weight):
        return jnp.pad(weight, ((0, 0), (0, hidden_pad)))

    def swap(v):
        return lax.ppermute(v, "dp", swap_pairs)

    def onward(v):
        return lax.ppermute(v, "dp", ring_pairs)

    core_array = core.astype(jnp.int32).reshape(1)
    at = jnp.stack([stage, core]).astype(jnp.int32)

    def hop(label, block):
        with jax.named_scope(label):
            return onward(block)

    def owner_after(count):
        return lax.rem(stage - 1 - count + 2 * ring, ring)

    def spread(label, block):
        with jax.named_scope(label):
            return [block] + [
                lax.ppermute(block, "tensor", [(i, i ^ j) for i in range(ranks)])
                for j in range(1, ranks)
            ]

    def send_parts(label, parts):
        with jax.named_scope(label):
            return [
                lax.ppermute(parts[j], "tensor", [(i, i ^ j) for i in range(ranks)])
                for j in range(1, ranks)
            ]

    def add_up(own, arrived):
        total = own.astype(F32)
        for piece in arrived:
            total = total + piece.astype(F32)
        return total

    def cut(matrix):
        return [matrix[j * rows : (j + 1) * rows] for j in range(ranks)]

    def tie(value, *others):
        return lax.optimization_barrier((value,) + others)[0]

    tokens_wide = tokens.astype(F32)
    normed_own = norm_rows(tokens_wide, attn_gain).astype(LOW)
    normed_one = spread("one_spread", normed_own)
    wide = hidden_cols + hidden_pad
    qkv_blocks = [jnp.concatenate([w_query, key_weight, value_weight], axis=1)]
    for count in range(1, ring):
        qkv_blocks.append(hop(f"qkv_hop{count}", qkv_blocks[-1]))
    ffn_full = lax.all_gather(
        tie(jnp.stack([widen(w_down.T), widen(w_gate), widen(w_up)]), qkv_blocks[2]),
        "dp",
        axis=1,
        tiled=True,
    )
    gate_full, up_full = ffn_full[1], ffn_full[2]
    grad_blocks = spread("cot_spread", tie(cotangent, *normed_one))
    first_start = jnp.sum((segments < 1).astype(jnp.int32))
    second_start = jnp.sum((segments < 2).astype(jnp.int32))
    ids = jnp.arange(length, dtype=jnp.int32).reshape(ranks, rows)
    begins = jnp.where(segments == 0, 0, jnp.where(segments == 1, first_start, second_start))
    begins = begins.astype(jnp.int32).reshape(ranks, rows)
    order = [me ^ j for j in range(ranks)]
    bounds = jnp.stack([lax.dynamic_index_in_dim(begins, o, 0, keepdims=False) for o in order])
    here = jnp.stack([lax.dynamic_index_in_dim(ids, o, 0, keepdims=False) for o in order])
    positions = (here - bounds).reshape(length).astype(F32)
    bounds = bounds.reshape(ranks, 1, rows)
    half = HEAD_SIZE // 2
    freqs = ROTARY_BASE ** (-2.0 * jnp.arange(half, dtype=F32) / HEAD_SIZE)
    angles = positions[:, None] * jnp.concatenate([freqs] * 4)[None, :]
    signs = jnp.concatenate([-jnp.ones(half, F32), jnp.ones(half, F32)] * 2)
    cosine = jnp.cos(angles)
    sine = jnp.sin(angles) * signs[None, :]
    head_gains = jnp.concatenate(
        [query_gain] * (q_cols // HEAD_SIZE) + [key_gain] * (kv_cols // HEAD_SIZE)
    ).reshape(1, -1)

    out_blocks = [w_out.T]
    normed_all, normed_one_t = fold(core_array, normed_one, ring)
    for count in range(1, ring):
        out_flow = hop(f"out_hop{count}", out_blocks[-1])
        if count < ring - 1:
            before = (cosine, sine, head_gains, bounds) if count == 1 else (normed_all,)
            out_blocks.append(tie(out_flow, qkv_blocks[count + 1], *before))

    def complete(blocks):
        return place(at, [b for block in blocks for b in (block, swap(block))], ring)

    w_qkv = complete(qkv_blocks)
    query_low, key_low, value_low, raw = prepare(
        normed_all, w_qkv, cosine, sine, head_gains, q_cols, kv_cols, ranks
    )
    me_array = me.astype(jnp.int32).reshape(1)
    attended, lse = attend(me_array, query_low, key_low, value_low, bounds, ranks, heads)

    attended_go = tie(attended, *grad_blocks)
    out_blocks.append(tie(out_flow, attended))
    out_t = complete(out_blocks)
    attn_parts = back_parts([attended_go], out_t[None], (0,), ranks)
    attn_arrived = send_parts("attn_sum", attn_parts)
    grad_all, grad_t = fold(core_array, [tie(grad_blocks[0], *attn_parts)] + grad_blocks[1:], ring)
    attn_arrived[0] = tie(attn_arrived[0], grad_all)
    hidden, normed_two_own = sum_up(tokens, [attn_parts[0]] + attn_arrived, ffn_gain)
    normed_two = spread("two_spread", normed_two_own)
    d_activation = rows_product(grad_all, ffn_full, ranks, 56)
    normed_two[-1] = tie(normed_two[-1], d_activation)
    normed_two_all, normed_two_t, *normed_two_pair = fold(core_array, normed_two, ring, True)

    gating = mm(normed_two_all, gate_full).astype(LOW).astype(F32)
    lifted = mm(normed_two_all, up_full)
    gate_sig = jax.nn.sigmoid(gating)
    silu = gating * gate_sig
    activation = (silu * lifted).astype(LOW)
    d_act_wide = d_activation.astype(F32)
    d_gating = (d_act_wide * lifted * gate_sig * (1.0 + gating * (1.0 - gate_sig))).astype(LOW)
    d_lifted = (d_act_wide * silu).astype(LOW)

    last = ring - 1

    def advance(label, flow, near, other, count):
        if count == last:
            return join(owner_after(count), flow, near, other, ring, F32), None
        block = join(owner_after(count), flow, near, other, ring, LOW)
        return block, hop(f"{label}_hop{count + 1}", block)

    def several(label, block, flow, near, other, first, end, *after):
        for count in range(first, end):
            block, flow = advance(label, tie(flow, *after), near, other, count)
        return block, flow

    down_full_grad = product(grad_t, [activation])
    down_grad = lax.psum_scatter(down_full_grad, "dp", scatter_dimension=0, tiled=True)
    two_parts = back_parts([tie(d_gating, down_full_grad), d_lifted], ffn_full, (1, 2), ranks)
    two_arrived = send_parts("two_sum", two_parts)
    gate_far = product(normed_two_pair[0], [tie(d_gating, *two_parts)])
    gate_near = product(normed_two_pair[1], [tie(d_gating, gate_far)])
    lift_full_grad = product(normed_two_t, [tie(d_lifted, gate_near)])
    *two_arrived, gate_far, gate_near, lift_full_grad = lax.optimization_barrier(
        (*two_arrived, gate_far, gate_near, lift_full_grad)
    )
    gate_other = swap(gate_far)
    d_hidden, d_hidden_low, ffn_gain_part = norm_back_sum(
        hidden, ffn_gain, cotangent, [two_parts[0]] + two_arrived, True
    )
    hidden_grad = spread("dh_spread", d_hidden_low)
    lift_grad = lax.psum_scatter(
        tie(lift_full_grad, down_grad, d_hidden_low), "dp", scatter_dimension=0, tiled=True
    )
    gate_block, gate_flow = advance("gate_grad", None, tie(gate_near, d_hidden_low), gate_other, 0)
    ffn_parts = back_parts([tie(activation, d_hidden_low)], ffn_full, (0,), ranks)
    hidden_grad[1] = tie(hidden_grad[1], *ffn_parts)
    gate_block, gate_flow = several(
        "gate_grad", gate_block, gate_flow, gate_near, gate_other, 1, last - 1, hidden_grad[1]
    )
    hidden_grad[-1] = tie(hidden_grad[-1], gate_block)
    hidden_grad_all, hidden_grad_t = fold(core_array, hidden_grad, ring)
    ffn_go = lax.optimization_barrier(tuple(ffn_parts) + tuple(hidden_grad))[:ranks]
    ffn_arrived = send_parts("ffn_sum", ffn_go)
    d_attended = rows_product(hidden_grad_all, out_t[None], ranks, 24)
    d_queries, d_keys, d_values = attend_back(
        me_array, query_low, key_low, value_low, bounds, attended, d_attended, lse, ranks, heads
    )
    d_raw, head_gain_parts = prepare_back(
        d_queries, d_keys, d_values, raw, cosine, sine, head_gains, ranks
    )
    gate_block, gate_flow = advance(
        "gate_grad", tie(gate_flow, *ffn_arrived), gate_near, gate_other, last - 1
    )
    one_parts = back_parts([tie(d_raw, gate_block, *ffn_arrived)], w_qkv[None], (0,), ranks)
    one_arrived = send_parts("one_sum", one_parts)
    attn_full_grad = attn_products([normed_one_t, hidden_grad_t], [tie(d_raw, *one_parts), attended])
    attn_grad = lax.psum_scatter(
        tie(attn_full_grad, lift_grad), "dp", scatter_dimension=0, tiled=True)
    gains = gain_parts(
        tie(normed_all, attn_full_grad), attn_gain, one_parts, ffn_gain_part, head_gain_parts
    )
    (output,) = sum_up(tie(hidden, gains), [ffn_parts[0]] + ffn_arrived)

    def exchange_sum(own, axis, offsets, size):
        pieces = [own] + [lax.ppermute(own, axis, [(i, i ^ j) for i in range(size)]) for j in offsets]
        while len(pieces) > 1:
            pieces = [a + b for a, b in zip(pieces[::2], pieces[1::2])]
        return pieces[0]

    gate_flow = tie(gate_flow, output, gains)
    (down_grad,) = cut_grads(tie(down_grad, output), (hidden_cols,))
    lift_grad = lift_grad[:, :hidden_cols].astype(F32)
    *one_arrived, gate_flow, total, down_grad, lift_grad = lax.optimization_barrier(
        (*one_arrived, gate_flow, gains, down_grad, lift_grad)
    )
    total = exchange_sum(total, "tensor", range(1, ranks), ranks)
    (gate_grad,) = last_join(
        owner_after(last), gate_flow, gate_near, gate_other, ring, hidden_cols, 1
    )
    (tokens_grad,) = norm_back_sum(tokens, attn_gain, d_hidden, [one_parts[0]] + one_arrived, False)
    query_grad, key_grad, value_grad, out_grad = cut_grads(
        attn_grad, (q_cols, kv_cols, kv_cols, q_cols)
    )

    total = tie(total, tokens_grad, gate_grad)
    total = exchange_sum(total, "dp", range(1, 2), dp_size)
    total = exchange_sum(total, "dp", range(2, dp_size, 2), dp_size)
    total = total.reshape(-1)
    a, b = attn_gain.shape[0], 2 * attn_gain.shape[0]
    query_gain_grad = jnp.sum(total[b : b + q_cols].reshape(-1, HEAD_SIZE), axis=0)
    key_gain_grad = jnp.sum(total[b + q_cols :].reshape(-1, HEAD_SIZE), axis=0)
    return (
        output,
        tokens_grad,
        total[:a],
        query_grad,
        key_grad,
        value_grad,
        query_gain_grad,
        key_gain_grad,
        out_grad,
        total[a:b],
        gate_grad,
        lift_grad,
        down_grad,
    )


def solution(mesh):
    in_specs = (
        P(("dp", "tensor"), None),
        P("dp"),
        P(),
        P("dp", "tensor"),
        P("dp", "tensor"),
        P("dp", "tensor"),
        P(),
        P(),
        P("tensor", "dp"),
        P(),
        P("dp", "tensor"),
        P("dp", "tensor"),
        P("tensor", "dp"),
        P(("dp", "tensor"), None),
    )
    out_specs = (
        P(("dp", "tensor"), None),
        P(("dp", "tensor"), None),
        P(),
        P("dp", "tensor"),
        P("dp", "tensor"),
        P("dp", "tensor"),
        P(),
        P(),
        P("tensor", "dp"),
        P(),
        P("dp", "tensor"),
        P("dp", "tensor"),
        P("tensor", "dp"),
    )
    body = functools.partial(shards, mesh.shape["dp"], mesh.shape["tensor"])
    return jax.shard_map(body, mesh=mesh, in_specs=in_specs, out_specs=out_specs, check_vma=False)
```

```python
import functools

import jax
import jax.numpy as jnp
from jax import lax
from jax.experimental import pallas as pl
from jax.experimental.pallas import tpu as pltpu
from jax.sharding import PartitionSpec as P

QUERY_HEADS = 24
KEY_VALUE_HEADS = 8
HEAD_SIZE = 64
GROUP = QUERY_HEADS // KEY_VALUE_HEADS
EPSILON = 1e-05
ROTARY_BASE = 1000000.0
NEGATIVE_FILL = -1e30
F32 = jnp.float32
LOW = jnp.bfloat16
SCALE = HEAD_SIZE ** (-0.5)
FREE = pl.CostEstimate(flops=0, bytes_accessed=0, transcendentals=0)


def norm_rows(values_in, gain):
    return (
        values_in
        * lax.rsqrt(jnp.mean(values_in * values_in, axis=-1, keepdims=True) + EPSILON)
        * gain
    )


def norm_back(values, gain, grad):
    inverse = lax.rsqrt(jnp.mean(values * values, axis=-1, keepdims=True) + EPSILON)
    hat = values * inverse
    scaled = grad * gain
    inner = jnp.mean(scaled * hat, axis=-1, keepdims=True)
    return (scaled - hat * inner) * inverse, jnp.sum(grad * hat, axis=0)


def mm(left, right):
    return jnp.dot(left, right, preferred_element_type=F32)


def cross_rows(left, right):
    return lax.dot_general(left, right, (((1,), (1,)), ((), ())), preferred_element_type=F32)


def cross_cols(left, right):
    return lax.dot_general(left, right, (((0,), (0,)), ((), ())), preferred_element_type=F32)


NT = (((1,), (1,)), ((), ()))
NN = (((1,), (0,)), ((), ()))
TN = (((0,), (0,)), ((), ()))


def kdot(left, right, dims):
    return lax.dot_general(left, right, dims, preferred_element_type=F32)


def stack_heads(block, head):
    first = head * GROUP * HEAD_SIZE
    return jnp.concatenate(
        [block[:, first + g * HEAD_SIZE : first + (g + 1) * HEAD_SIZE] for g in range(GROUP)], axis=0
    )


def attend_kernel(heads, rows, me_ref, q_ref, k_ref, v_ref, lo_ref, out_ref, lse_ref):
    me = me_ref[0]
    block = pl.program_id(0) ^ me
    low_bound = jnp.concatenate([lo_ref[0]] * GROUP, axis=1)
    row_ids = block * rows + lax.broadcasted_iota(jnp.int32, (1, rows), 1)
    row_ids = jnp.concatenate([row_ids] * GROUP, axis=1)
    width = GROUP * rows
    queries = q_ref[...] * SCALE
    pieces = []
    for head in range(heads):
        q3 = stack_heads(queries, head)
        cols = slice(head * HEAD_SIZE, (head + 1) * HEAD_SIZE)

        def step(other, carry, q3=q3, cols=cols):
            peak, total, acc = carry
            first = pl.multiple_of((other ^ me) * rows, rows)
            keys = k_ref[pl.ds(first, rows), cols]
            vals = v_ref[pl.ds(first, rows), cols]
            ids = other * rows + lax.broadcasted_iota(jnp.int32, (rows, 1), 0)
            scores = kdot(keys, q3, NT)
            scores = jnp.where((ids <= row_ids) & (ids >= low_bound), scores, NEGATIVE_FILL)
            higher = jnp.maximum(peak, jnp.max(scores, axis=0, keepdims=True))
            fade = jnp.exp(peak - higher)
            exps = jnp.exp(scores - higher)
            total = total * fade + jnp.sum(exps, axis=0, keepdims=True)
            acc = acc * fade + kdot(vals, exps.astype(LOW), TN)
            return higher, total, acc

        start = (
            jnp.full((1, width), NEGATIVE_FILL, F32),
            jnp.zeros((1, width), F32),
            jnp.zeros((HEAD_SIZE, width), F32),
        )
        start = step(block, start)
        peak, total, acc = lax.fori_loop(0, block, step, start)
        acc = acc / total
        lse_ref[0, head : head + 1, :] = peak + jnp.log(total)
        pieces += [acc[:, g * rows : (g + 1) * rows] for g in range(GROUP)]
    out_ref[...] = jnp.concatenate(pieces, axis=0).T.astype(LOW)


def attend_back_kernel(
    heads, rows, me_ref, q_ref, k_ref, v_ref, lo_ref, o_ref, do_ref, lse_ref, dq_ref, dk_ref, dv_ref
):
    me = me_ref[0]

    @pl.when(pl.program_id(0) == 0)
    def _():
        dk_ref[...] = jnp.zeros_like(dk_ref)
        dv_ref[...] = jnp.zeros_like(dv_ref)

    block = pl.program_id(0) ^ me
    low_bound = jnp.concatenate([lo_ref[0]] * GROUP, axis=1)
    row_ids = block * rows + lax.broadcasted_iota(jnp.int32, (1, rows), 1)
    row_ids = jnp.concatenate([row_ids] * GROUP, axis=1)
    width = GROUP * rows
    queries = q_ref[...] * SCALE
    grads = do_ref[...]
    product = (grads.astype(F32) * o_ref[...].astype(F32)).T
    pieces = []
    for head in range(heads):
        q3 = stack_heads(queries, head)
        do3 = stack_heads(grads, head)
        cols = slice(head * HEAD_SIZE, (head + 1) * HEAD_SIZE)
        first_row = head * GROUP * HEAD_SIZE
        inner = jnp.concatenate(
            [
                jnp.sum(
                    product[first_row + g * HEAD_SIZE : first_row + (g + 1) * HEAD_SIZE],
                    axis=0,
                    keepdims=True,
                )
                for g in range(GROUP)
            ],
            axis=1,
        )
        lse = lse_ref[0, head : head + 1, :]

        def step(other, acc, q3=q3, do3=do3, cols=cols, inner=inner, lse=lse, own=False):
            first = pl.multiple_of((other ^ me) * rows, rows)
            place = pl.ds(first, rows)
            keys = k_ref[place, cols]
            vals = v_ref[place, cols]
            ids = other * rows + lax.broadcasted_iota(jnp.int32, (rows, 1), 0)
            scores = kdot(keys, q3, NT)
            allowed = ids >= low_bound
            if own:
                allowed = allowed & (ids <= row_ids)
            scores = jnp.where(allowed, scores, NEGATIVE_FILL)
            probs = jnp.exp(scores - lse)
            d_probs = kdot(vals, do3, NT)
            d_scores = (probs * (d_probs - inner)).astype(LOW)
            dk_ref[place, cols] += kdot(d_scores, q3, NN)
            dv_ref[place, cols] += kdot(probs.astype(LOW), do3, NN)
            return acc + kdot(keys, d_scores, TN)

        acc = step(block, jnp.zeros((HEAD_SIZE, width), F32), own=True)
        acc = lax.fori_loop(0, block, step, acc)
        pieces += [acc[:, g * rows : (g + 1) * rows] for g in range(GROUP)]
    dq_ref[...] = jnp.concatenate(pieces, axis=0).T * SCALE


def attention_specs(ranks, rows, heads):
    length = ranks * rows
    q_spec = pl.BlockSpec((rows, heads * GROUP * HEAD_SIZE), lambda i, me: (i, 0))
    kv_spec = pl.BlockSpec((length, heads * HEAD_SIZE), lambda i, me: (0, 0))
    lo_spec = pl.BlockSpec((1, 1, rows), lambda i, me: (i, 0, 0))
    lse_spec = pl.BlockSpec((1, heads, GROUP * rows), lambda i, me: (i, 0, 0))
    return q_spec, kv_spec, lo_spec, lse_spec


def attend(me, queries, keys, values, bounds, ranks, heads):
    length = queries.shape[0]
    rows = length // ranks
    q_spec, kv_spec, lo_spec, lse_spec = attention_specs(ranks, rows, heads)
    return pl.pallas_call(
        functools.partial(attend_kernel, heads, rows),
        grid_spec=pltpu.PrefetchScalarGridSpec(
            num_scalar_prefetch=1,
            grid=(ranks,),
            in_specs=[q_spec, kv_spec, kv_spec, lo_spec],
            out_specs=[q_spec, lse_spec],
        ),
        out_shape=[
            jax.ShapeDtypeStruct(queries.shape, LOW),
            jax.ShapeDtypeStruct((ranks, heads, GROUP * rows), F32),
        ],
        compiler_params=pltpu.CompilerParams(vmem_limit_bytes=48 * 2**20),
        cost_estimate=pl.CostEstimate(
            flops=16 * length * length * heads * GROUP * HEAD_SIZE,
            bytes_accessed=32 * 2**20,
            transcendentals=length * length * heads * GROUP,
        ),
        name="attend",
    )(me, queries, keys, values, bounds)


def attend_back(me, queries, keys, values, bounds, attended, d_attended, lse, ranks, heads):
    length = queries.shape[0]
    rows = length // ranks
    q_spec, kv_spec, lo_spec, lse_spec = attention_specs(ranks, rows, heads)
    return pl.pallas_call(
        functools.partial(attend_back_kernel, heads, rows),
        grid_spec=pltpu.PrefetchScalarGridSpec(
            num_scalar_prefetch=1,
            grid=(ranks,),
            in_specs=[q_spec, kv_spec, kv_spec, lo_spec, q_spec, q_spec, lse_spec],
            out_specs=[q_spec, kv_spec, kv_spec],
        ),
        out_shape=[
            jax.ShapeDtypeStruct(queries.shape, F32),
            jax.ShapeDtypeStruct(keys.shape, F32),
            jax.ShapeDtypeStruct(keys.shape, F32),
        ],
        compiler_params=pltpu.CompilerParams(vmem_limit_bytes=48 * 2**20),
        cost_estimate=FREE,
        name="attend_back",
    )(me, queries, keys, values, bounds, attended, d_attended, lse)


def fold_kernel(ranks, ring, rows, core_ref, *refs):
    blocks, (all_ref, turned_ref), split = refs[:ranks], refs[ranks : ranks + 2], refs[ranks + 2 :]
    core = core_ref[0]
    depth = turned_ref.shape[0] // (2 * ring)
    for j in range(ranks):
        block = blocks[j][...]
        span = slice(j * rows, (j + 1) * rows)
        all_ref[span, :] = block
        turned_ref[:, span] = block.T
        if split:
            for i in range(ring):
                to = slice(i * depth, (i + 1) * depth)
                for side_ref, side in zip(split, (1 - core, core)):
                    first = pl.multiple_of((2 * i + side) * depth, 16)
                    side_ref[to, span] = turned_ref[pl.ds(first, depth), span]


def fold(core, blocks, ring, split=False):
    ranks = len(blocks)
    rows, width = blocks[0].shape
    length = ranks * rows
    whole = lambda shape: pl.BlockSpec(shape, lambda i: (0, 0))
    shapes = [(length, width), (width, length)] + ([(width // 2, length)] * 2 if split else [])
    return pl.pallas_call(
        functools.partial(fold_kernel, ranks, ring, rows),
        grid=(1,),
        in_specs=[pl.BlockSpec(memory_space=pltpu.SMEM)] + [whole((rows, width))] * ranks,
        out_specs=[whole(shape) for shape in shapes],
        out_shape=[jax.ShapeDtypeStruct(shape, LOW) for shape in shapes],
        compiler_params=pltpu.CompilerParams(vmem_limit_bytes=40 * 2**20),
        cost_estimate=FREE,
        name="fold",
    )(core, *blocks)


def place_kernel(ring, depth, at_ref, *refs):
    blocks = refs[: 2 * ring]
    full_ref, sems = refs[2 * ring :]
    stage, core = at_ref[0], at_ref[1]
    copies = []
    for hop in range(ring):
        owner = lax.rem(stage - hop + ring, ring)
        for half, side in enumerate((core, 1 - core)):
            first = pl.multiple_of((owner * 2 + side) * depth, 16)
            copies.append(
                pltpu.make_async_copy(
                    blocks[2 * hop + half], full_ref.at[pl.ds(first, depth)], sems.at[2 * hop + half]
                )
            )
    for copy in copies:
        copy.start()
    for copy in copies:
        copy.wait()


def place(at, blocks, ring):
    depth, cols = blocks[0].shape
    return pl.pallas_call(
        functools.partial(place_kernel, ring, depth),
        in_specs=[pl.BlockSpec(memory_space=pltpu.SMEM)]
        + [pl.BlockSpec(memory_space=pl.ANY)] * (2 * ring),
        grid=(1,),
        out_specs=pl.BlockSpec((2 * ring * depth, cols), lambda i: (0, 0)),
        out_shape=jax.ShapeDtypeStruct((2 * ring * depth, cols), LOW),
        scratch_shapes=[pltpu.SemaphoreType.DMA((2 * ring,))],
        compiler_params=pltpu.CompilerParams(vmem_limit_bytes=24 * 2**20),
        cost_estimate=FREE,
        name="place",
    )(at, *blocks)


def product_kernel(tiles, left_ref, *refs):
    for k, right in enumerate(refs[:-1]):

        @pl.when(pl.program_id(0) // tiles == k)
        def _(right=right):
            refs[-1][...] = jnp.dot(
                left_ref[...], right[...], preferred_element_type=F32
            ).astype(LOW)


def product(left, rights):
    depth, length = left.shape
    cols = rights[0].shape[1]
    tile = 256 if cols % 256 == 0 else 128
    tiles = cols // tile
    return pl.pallas_call(
        functools.partial(product_kernel, tiles),
        grid=(tiles * len(rights),),
        in_specs=[pl.BlockSpec((depth, length), lambda i: (0, 0))]
        + [
            pl.BlockSpec((length, tile), lambda i, k=k: (0, jnp.clip(i - k * tiles, 0, tiles - 1)))
            for k in range(len(rights))
        ],
        out_specs=pl.BlockSpec((depth, tile), lambda i: (0, i)),
        out_shape=jax.ShapeDtypeStruct((depth, cols * len(rights)), LOW),
        compiler_params=pltpu.CompilerParams(vmem_limit_bytes=56 * 2**20),
        cost_estimate=FREE,
        name="product",
    )(left, *rights)


def attn_products_kernel(*refs):
    lefts, rights, out_ref = refs[:2], refs[2:4], refs[4]
    first = 0
    for left, right in zip(lefts, rights):
        cols = right.shape[1]
        out_ref[:, first : first + cols] = jnp.dot(
            left[...], right[...], preferred_element_type=F32
        ).astype(LOW)
        first += cols


def attn_products(lefts, rights):
    depth = lefts[0].shape[0]
    tiles = 4
    part = lambda a: pl.BlockSpec((depth // tiles, a.shape[1]), lambda i: (i, 0))
    whole = lambda a: pl.BlockSpec(a.shape, lambda i: (0, 0))
    shape = jax.ShapeDtypeStruct((depth, sum(a.shape[1] for a in rights)), LOW)
    return pl.pallas_call(
        attn_products_kernel,
        grid=(tiles,),
        in_specs=[part(a) for a in lefts] + [whole(a) for a in rights],
        out_specs=part(shape),
        out_shape=shape,
        compiler_params=pltpu.CompilerParams(vmem_limit_bytes=40 * 2**20),
        cost_estimate=FREE,
        name="attn_products",
    )(*lefts, *rights)


def back_parts_kernel(rows, count, *refs):
    total = sum(kdot(refs[k][...], refs[count + k][0], NT) for k in range(count))
    for j, out_ref in enumerate(refs[2 * count :]):
        out_ref[...] = total[j * rows : (j + 1) * rows].astype(LOW)


def back_parts(lefts, weights, which, ranks):
    length, cols = lefts[0].shape
    width = weights.shape[1]
    rows = length // ranks
    tile = 512
    return pl.pallas_call(
        functools.partial(back_parts_kernel, rows, len(lefts)),
        grid=(width // tile,),
        in_specs=[pl.BlockSpec((length, cols), lambda i: (0, 0))] * len(lefts)
        + [pl.BlockSpec((1, tile, cols), lambda i, k=k: (k, i, 0)) for k in which],
        out_specs=[pl.BlockSpec((rows, tile), lambda i: (0, i))] * ranks,
        out_shape=[jax.ShapeDtypeStruct((rows, width), LOW)] * ranks,
        compiler_params=pltpu.CompilerParams(vmem_limit_bytes=48 * 2**20),
        cost_estimate=FREE,
        name="back_parts",
    )(*lefts, *([weights] * len(which)))


def join_kernel(flows, at_ref, *refs):
    total = refs[flows][...].astype(F32) + refs[flows + 1][...].astype(F32)
    if flows:
        total = total + refs[0][...].astype(F32)
    refs[-1][...] = total.astype(refs[-1].dtype)


def join(owner, flow, near, other, ring, dtype):
    depth, cols = near.shape[0] // ring, near.shape[1]
    flows = [] if flow is None else [flow]
    half = cols // 2 if cols % 256 == 0 else cols
    row = pl.BlockSpec((depth, half), lambda i, at: (0, i))
    chosen = pl.BlockSpec((depth, half), lambda i, at: (at[0], i))
    return pl.pallas_call(
        functools.partial(join_kernel, len(flows)),
        grid_spec=pltpu.PrefetchScalarGridSpec(
            num_scalar_prefetch=1,
            grid=(cols // half,),
            in_specs=[row] * len(flows) + [chosen] * 2,
            out_specs=row,
        ),
        out_shape=jax.ShapeDtypeStruct((depth, cols), dtype),
        compiler_params=pltpu.CompilerParams(vmem_limit_bytes=24 * 2**20),
        cost_estimate=FREE,
        name="join",
    )(owner.astype(jnp.int32).reshape(1), *flows, near, other)


def last_join_kernel(at_ref, flow_ref, near_ref, other_ref, *out_refs):
    total = flow_ref[...].astype(F32) + near_ref[...].astype(F32) + other_ref[...].astype(F32)
    width = total.shape[1] // len(out_refs)
    for k, out_ref in enumerate(out_refs):
        cols = out_ref.shape[1]
        out_ref[...] = total[:, k * width : k * width + cols]


def last_join(owner, flow, near, other, ring, cols, count):
    depth, wide = near.shape[0] // ring, near.shape[1]
    chosen = pl.BlockSpec((depth, wide), lambda i, at: (at[0], 0))
    return pl.pallas_call(
        last_join_kernel,
        grid_spec=pltpu.PrefetchScalarGridSpec(
            num_scalar_prefetch=1,
            grid=(1,),
            in_specs=[pl.BlockSpec((depth, wide), lambda i, at: (0, 0)), chosen, chosen],
            out_specs=[pl.BlockSpec((depth, cols), lambda i, at: (0, 0))] * count,
        ),
        out_shape=[jax.ShapeDtypeStruct((depth, cols), F32)] * count,
        compiler_params=pltpu.CompilerParams(vmem_limit_bytes=56 * 2**20),
        cost_estimate=FREE,
        name="last_join",
    )(owner.astype(jnp.int32).reshape(1), flow, near, other)


def cut_kernel(widths, grads_ref, *out_refs):
    first = 0
    for cols, out_ref in zip(widths[:-1], out_refs):
        out_ref[...] = grads_ref[:, first : first + cols].astype(F32)
        first += cols
    out_refs[-1][...] = grads_ref[:, first : first + widths[-1]].astype(F32).T


def cut_grads(grads, widths):
    depth = grads.shape[0]
    whole = lambda shape: pl.BlockSpec(shape, lambda i: (0, 0))
    shapes = [(depth, cols) for cols in widths[:-1]] + [(widths[-1], depth)]
    return pl.pallas_call(
        functools.partial(cut_kernel, widths),
        grid=(1,),
        in_specs=[whole(grads.shape)],
        out_specs=[whole(shape) for shape in shapes],
        out_shape=[jax.ShapeDtypeStruct(shape, F32) for shape in shapes],
        compiler_params=pltpu.CompilerParams(vmem_limit_bytes=24 * 2**20),
        cost_estimate=FREE,
        name="cut_grads",
    )(grads)


def sum_kernel(count, base_ref, *refs):
    total = base_ref[...].astype(F32)
    arrived = refs[0][...].astype(F32)
    for ref in refs[1:count]:
        arrived = arrived + ref[...].astype(F32)
    total = total + arrived
    refs[-1 if len(refs) == count + 1 else -2][...] = total
    if len(refs) > count + 1:
        gain_ref = refs[count]
        inverse = lax.rsqrt(jnp.mean(total * total, axis=-1, keepdims=True) + EPSILON)
        refs[-1][...] = (total * inverse * gain_ref[...]).astype(LOW)


def sum_up(base, parts, gain=None):
    rows, width = base.shape
    step = rows // 2
    by_row = pl.BlockSpec((step, width), lambda i: (i, 0))
    gains = [] if gain is None else [gain.reshape(1, -1)]
    outs = [jax.ShapeDtypeStruct((rows, width), F32)]
    if gains:
        outs.append(jax.ShapeDtypeStruct((rows, width), LOW))
    return pl.pallas_call(
        functools.partial(sum_kernel, len(parts)),
        grid=(2,),
        in_specs=[by_row] * (1 + len(parts)) + [pl.BlockSpec((1, width), lambda i: (0, 0))] * len(gains),
        out_specs=[by_row] * len(outs),
        out_shape=outs,
        compiler_params=pltpu.CompilerParams(vmem_limit_bytes=56 * 2**20),
        cost_estimate=FREE,
        name="sum_up",
    )(base, *parts, *gains)


def norm_back_kernel(count, value_ref, gain_ref, rest_ref, *refs):
    parts, outs = refs[:count], refs[count:]
    value = value_ref[...].astype(F32)
    grad = parts[0][...].astype(F32)
    for ref in parts[1:]:
        grad = grad + ref[...].astype(F32)
    inverse = lax.rsqrt(jnp.mean(value * value, axis=-1, keepdims=True) + EPSILON)
    hat = value * inverse
    scaled = grad * gain_ref[...]
    inner = jnp.mean(scaled * hat, axis=-1, keepdims=True)
    total = rest_ref[...].astype(F32) + (scaled - hat * inner) * inverse
    outs[0][...] = total
    if len(outs) > 1:
        outs[1][...] = total.astype(LOW)

        @pl.when(pl.program_id(0) == 0)
        def _():
            outs[2][...] = jnp.zeros_like(outs[2])

        outs[2][...] += jnp.sum(grad * hat, axis=0, keepdims=True)


def norm_back_sum(value, gain, rest, parts, more):
    rows, width = value.shape
    step = rows // 2
    by_row = pl.BlockSpec((step, width), lambda i: (i, 0))
    fixed = pl.BlockSpec((1, width), lambda i: (0, 0))
    shapes = [jax.ShapeDtypeStruct((rows, width), F32)]
    if more:
        shapes += [jax.ShapeDtypeStruct((rows, width), LOW), jax.ShapeDtypeStruct((1, width), F32)]
    return pl.pallas_call(
        functools.partial(norm_back_kernel, len(parts)),
        grid=(2,),
        in_specs=[by_row, fixed, by_row] + [by_row] * len(parts),
        out_specs=[by_row, by_row, fixed][: len(shapes)],
        out_shape=shapes,
        compiler_params=pltpu.CompilerParams(vmem_limit_bytes=56 * 2**20),
        cost_estimate=FREE,
        name="norm_back_sum",
    )(value, gain.reshape(1, -1), rest, *parts)


def rows_product_kernel(left_ref, right_ref, out_ref):
    out_ref[...] = jnp.dot(left_ref[...], right_ref[0], preferred_element_type=F32).astype(LOW)


def rows_product(left, right, ranks, grant):
    length, depth = left.shape
    rows = length // ranks
    return pl.pallas_call(
        rows_product_kernel,
        grid=(ranks,),
        in_specs=[
            pl.BlockSpec((rows, depth), lambda i: (i, 0)),
            pl.BlockSpec((1,) + right.shape[1:], lambda i: (0, 0, 0)),
        ],
        out_specs=pl.BlockSpec((rows, right.shape[2]), lambda i: (i, 0)),
        out_shape=jax.ShapeDtypeStruct((length, right.shape[2]), LOW),
        compiler_params=pltpu.CompilerParams(vmem_limit_bytes=grant * 2**20),
        cost_estimate=FREE,
        name="rows_product",
    )(left, right)


def gain_parts_kernel(normed_ref, gain_ref, two_ref, heads_ref, *refs):
    parts, out_ref = refs[:-1], refs[-1]
    rows, width = parts[0].shape
    total = jnp.zeros((1, width), F32)
    for j, ref in enumerate(parts):
        block = normed_ref[j * rows : (j + 1) * rows, :].astype(F32)
        total = total + jnp.sum(block * ref[...].astype(F32), axis=0, keepdims=True)
    out_ref[:, :width] = total / gain_ref[...]
    out_ref[:, width : 2 * width] = two_ref[...]
    out_ref[:, 2 * width :] = heads_ref[...]


def gain_parts(normed, gain, parts, two, heads):
    args = [normed, gain.reshape(1, -1), two, heads, *parts]
    whole = lambda a: pl.BlockSpec(a.shape, lambda i: (0, 0))
    shape = jax.ShapeDtypeStruct((1, 2 * normed.shape[1] + heads.shape[1]), F32)
    return pl.pallas_call(
        gain_parts_kernel,
        grid=(1,),
        in_specs=[whole(a) for a in args],
        out_specs=whole(shape),
        out_shape=shape,
        compiler_params=pltpu.CompilerParams(vmem_limit_bytes=56 * 2**20),
        cost_estimate=FREE,
        name="gain_parts",
    )(*args)


def group_mean(values):
    width = values.shape[1]
    part = 2 * HEAD_SIZE
    left = lax.broadcasted_iota(jnp.int32, (part, part), 0) // HEAD_SIZE
    right = lax.broadcasted_iota(jnp.int32, (part, part), 1) // HEAD_SIZE
    spread = jnp.where(left == right, 1.0 / HEAD_SIZE, 0.0).astype(F32)
    pieces = []
    for first in range(0, width, part):
        size = min(part, width - first)
        pieces.append(
            lax.dot_general(
                values[:, first : first + size],
                spread[:size, :size],
                NN,
                precision=lax.Precision.HIGHEST,
                preferred_element_type=F32,
            )
        )
    return jnp.concatenate(pieces, axis=1) if len(pieces) > 1 else pieces[0]


def across(table, width):
    part = table.shape[1]
    if width < part:
        return table[:, :width]
    return jnp.concatenate([table] * (width // part) + ([table[:, : width % part]] if width % part else []), axis=1)


def partner(values):
    width = values.shape[1]
    half = HEAD_SIZE // 2
    lane = lax.broadcasted_iota(jnp.int32, values.shape, 1) % HEAD_SIZE
    return jnp.where(lane < half, pltpu.roll(values, width - half, 1), pltpu.roll(values, half, 1))


def prepare_kernel(q_cols, kv_cols, x_ref, w_ref, cos_ref, sin_ref, gain_ref, q_ref, k_ref, v_ref, raw_ref):
    product = jnp.dot(x_ref[...], w_ref[...], preferred_element_type=F32)
    for first, cols, to in ((0, q_cols, q_ref), (q_cols, kv_cols, k_ref)):
        raw = product[:, first : first + cols]
        scaled = raw * lax.rsqrt(group_mean(raw * raw) + EPSILON) * gain_ref[:, first : first + cols]
        cos = across(cos_ref[...], cols)
        sin = across(sin_ref[...], cols)
        to[...] = (scaled * cos + partner(scaled) * sin).astype(LOW)
        raw_ref[:, first : first + cols] = raw
    v_ref[...] = product[:, q_cols + kv_cols :].astype(LOW)


def prepare(normed, weight, cosine, sine, gains, q_cols, kv_cols, ranks):
    length, width = normed.shape
    rows = length // ranks
    at_row = lambda i: (i, 0)
    fixed = lambda i: (0, 0)
    return pl.pallas_call(
        functools.partial(prepare_kernel, q_cols, kv_cols),
        grid=(ranks,),
        in_specs=[
            pl.BlockSpec((rows, width), at_row),
            pl.BlockSpec(weight.shape, fixed),
            pl.BlockSpec((rows, cosine.shape[1]), at_row),
            pl.BlockSpec((rows, cosine.shape[1]), at_row),
            pl.BlockSpec((1, q_cols + kv_cols), fixed),
        ],
        out_specs=[
            pl.BlockSpec((rows, q_cols), at_row),
            pl.BlockSpec((rows, kv_cols), at_row),
            pl.BlockSpec((rows, kv_cols), at_row),
            pl.BlockSpec((rows, q_cols + kv_cols), at_row),
        ],
        out_shape=[
            jax.ShapeDtypeStruct((length, q_cols), LOW),
            jax.ShapeDtypeStruct((length, kv_cols), LOW),
            jax.ShapeDtypeStruct((length, kv_cols), LOW),
            jax.ShapeDtypeStruct((length, q_cols + kv_cols), F32),
        ],
        compiler_params=pltpu.CompilerParams(vmem_limit_bytes=40 * 2**20),
        cost_estimate=FREE,
        name="prepare",
    )(normed, weight, cosine, sine, gains)


def prepare_back_kernel(
    q_cols, kv_cols, dq_ref, dk_ref, dv_ref, raw_ref, cos_ref, sin_ref, gain_ref, out_ref, gain_grad_ref
):
    @pl.when(pl.program_id(0) == 0)
    def _():
        gain_grad_ref[...] = jnp.zeros_like(gain_grad_ref)

    for first, cols, grad_ref in ((0, q_cols, dq_ref), (q_cols, kv_cols, dk_ref)):
        span = slice(first, first + cols)
        grad = grad_ref[...]
        turned = grad * across(cos_ref[...], cols) - partner(grad) * across(sin_ref[...], cols)
        raw = raw_ref[:, span]
        inverse = lax.rsqrt(group_mean(raw * raw) + EPSILON)
        hat = raw * inverse
        gain_grad_ref[:, span] += jnp.sum(turned * hat, axis=0, keepdims=True)
        scaled = turned * gain_ref[:, span]
        out_ref[:, span] = ((scaled - hat * group_mean(scaled * hat)) * inverse).astype(LOW)
    out_ref[:, q_cols + kv_cols :] = dv_ref[...].astype(LOW)


def prepare_back(d_queries, d_keys, d_values, raw, cosine, sine, gains, ranks):
    length, q_cols = d_queries.shape
    kv_cols = d_keys.shape[1]
    rows = length // ranks
    at_row = lambda i: (i, 0)
    fixed = lambda i: (0, 0)
    return pl.pallas_call(
        functools.partial(prepare_back_kernel, q_cols, kv_cols),
        grid=(ranks,),
        in_specs=[
            pl.BlockSpec((rows, q_cols), at_row),
            pl.BlockSpec((rows, kv_cols), at_row),
            pl.BlockSpec((rows, kv_cols), at_row),
            pl.BlockSpec((rows, q_cols + kv_cols), at_row),
            pl.BlockSpec((rows, cosine.shape[1]), at_row),
            pl.BlockSpec((rows, cosine.shape[1]), at_row),
            pl.BlockSpec((1, q_cols + kv_cols), fixed),
        ],
        out_specs=[
            pl.BlockSpec((rows, q_cols + 2 * kv_cols), at_row),
            pl.BlockSpec((1, q_cols + kv_cols), fixed),
        ],
        out_shape=[
            jax.ShapeDtypeStruct((length, q_cols + 2 * kv_cols), LOW),
            jax.ShapeDtypeStruct((1, q_cols + kv_cols), F32),
        ],
        compiler_params=pltpu.CompilerParams(vmem_limit_bytes=56 * 2**20),
        cost_estimate=FREE,
        name="prepare_back",
    )(d_queries, d_keys, d_values, raw, cosine, sine, gains)


def shards(
    dp_size,
    ranks,
    tokens,
    segments,
    attn_gain,
    w_query,
    key_weight,
    value_weight,
    query_gain,
    key_gain,
    w_out,
    ffn_gain,
    w_gate,
    w_up,
    w_down,
    cotangent,
):
    ring = dp_size // 2
    index = lax.axis_index("dp")
    stage = index // 2
    core = index % 2
    me = lax.axis_index("tensor")
    swap_pairs = [(i, i ^ 1) for i in range(dp_size)]
    ring_pairs = [(i, (i + 2) % dp_size) for i in range(dp_size)]
    heads = KEY_VALUE_HEADS // ranks
    rows = tokens.shape[0]
    length = segments.shape[0]
    q_cols = w_query.shape[1]
    kv_cols = key_weight.shape[1]

    hidden_cols = w_gate.shape[1]
    hidden_pad = -hidden_cols % 128

    def widen(weight):
        return jnp.pad(weight, ((0, 0), (0, hidden_pad)))

    def swap(v):
        return lax.ppermute(v, "dp", swap_pairs)

    def onward(v):
        return lax.ppermute(v, "dp", ring_pairs)

    core_array = core.astype(jnp.int32).reshape(1)
    at = jnp.stack([stage, core]).astype(jnp.int32)

    def hop(label, block):
        with jax.named_scope(label):
            return onward(block)

    def owner_after(count):
        return lax.rem(stage - 1 - count + 2 * ring, ring)

    def spread(label, block):
        with jax.named_scope(label):
            return [block] + [
                lax.ppermute(block, "tensor", [(i, i ^ j) for i in range(ranks)])
                for j in range(1, ranks)
            ]

    def send_parts(label, parts):
        with jax.named_scope(label):
            return [
                lax.ppermute(parts[j], "tensor", [(i, i ^ j) for i in range(ranks)])
                for j in range(1, ranks)
            ]

    def add_up(own, arrived):
        total = own.astype(F32)
        for piece in arrived:
            total = total + piece.astype(F32)
        return total

    def cut(matrix):
        return [matrix[j * rows : (j + 1) * rows] for j in range(ranks)]

    def tie(value, *others):
        return lax.optimization_barrier((value,) + others)[0]

    tokens_wide = tokens.astype(F32)
    normed_own = norm_rows(tokens_wide, attn_gain).astype(LOW)
    normed_one = spread("one_spread", normed_own)
    wide = hidden_cols + hidden_pad
    qkv_blocks = [jnp.concatenate([w_query, key_weight, value_weight], axis=1)]
    for count in range(1, ring):
        qkv_blocks.append(hop(f"qkv_hop{count}", qkv_blocks[-1]))
    ffn_full = lax.all_gather(
        tie(jnp.stack([widen(w_down.T), widen(w_gate), widen(w_up)]), qkv_blocks[2]),
        "dp",
        axis=1,
        tiled=True,
    )
    gate_full, up_full = ffn_full[1], ffn_full[2]
    grad_blocks = spread("cot_spread", tie(cotangent, *normed_one))
    first_start = jnp.sum((segments < 1).astype(jnp.int32))
    second_start = jnp.sum((segments < 2).astype(jnp.int32))
    ids = jnp.arange(length, dtype=jnp.int32).reshape(ranks, rows)
    begins = jnp.where(segments == 0, 0, jnp.where(segments == 1, first_start, second_start))
    begins = begins.astype(jnp.int32).reshape(ranks, rows)
    order = [me ^ j for j in range(ranks)]
    bounds = jnp.stack([lax.dynamic_index_in_dim(begins, o, 0, keepdims=False) for o in order])
    here = jnp.stack([lax.dynamic_index_in_dim(ids, o, 0, keepdims=False) for o in order])
    positions = (here - bounds).reshape(length).astype(F32)
    bounds = bounds.reshape(ranks, 1, rows)
    half = HEAD_SIZE // 2
    freqs = ROTARY_BASE ** (-2.0 * jnp.arange(half, dtype=F32) / HEAD_SIZE)
    angles = positions[:, None] * jnp.concatenate([freqs] * 4)[None, :]
    signs = jnp.concatenate([-jnp.ones(half, F32), jnp.ones(half, F32)] * 2)
    cosine = jnp.cos(angles)
    sine = jnp.sin(angles) * signs[None, :]
    head_gains = jnp.concatenate(
        [query_gain] * (q_cols // HEAD_SIZE) + [key_gain] * (kv_cols // HEAD_SIZE)
    ).reshape(1, -1)

    out_blocks = [w_out.T]
    normed_all, normed_one_t = fold(core_array, normed_one, ring)
    for count in range(1, ring):
        out_flow = hop(f"out_hop{count}", out_blocks[-1])
        if count < ring - 1:
            before = (cosine, sine, head_gains, bounds) if count == 1 else (normed_all,)
            out_blocks.append(tie(out_flow, qkv_blocks[count + 1], *before))

    def complete(blocks):
        return place(at, [b for block in blocks for b in (block, swap(block))], ring)

    w_qkv = complete(qkv_blocks)
    query_low, key_low, value_low, raw = prepare(
        normed_all, w_qkv, cosine, sine, head_gains, q_cols, kv_cols, ranks
    )
    me_array = me.astype(jnp.int32).reshape(1)
    attended, lse = attend(me_array, query_low, key_low, value_low, bounds, ranks, heads)

    attended_go = tie(attended, *grad_blocks)
    out_blocks.append(tie(out_flow, attended))
    out_t = complete(out_blocks)
    attn_parts = back_parts([attended_go], out_t[None], (0,), ranks)
    attn_arrived = send_parts("attn_sum", attn_parts)
    grad_all, grad_t = fold(core_array, [tie(grad_blocks[0], *attn_parts)] + grad_blocks[1:], ring)
    attn_arrived[0] = tie(attn_arrived[0], grad_all)
    hidden, normed_two_own = sum_up(tokens, [attn_parts[0]] + attn_arrived, ffn_gain)
    normed_two = spread("two_spread", normed_two_own)
    d_activation = rows_product(grad_all, ffn_full, ranks, 56)
    normed_two[-1] = tie(normed_two[-1], d_activation)
    normed_two_all, normed_two_t, *normed_two_pair = fold(core_array, normed_two, ring, True)

    gating = mm(normed_two_all, gate_full).astype(LOW).astype(F32)
    lifted = mm(normed_two_all, up_full)
    gate_sig = jax.nn.sigmoid(gating)
    silu = gating * gate_sig
    activation = (silu * lifted).astype(LOW)
    d_act_wide = d_activation.astype(F32)
    d_gating = (d_act_wide * lifted * gate_sig * (1.0 + gating * (1.0 - gate_sig))).astype(LOW)
    d_lifted = (d_act_wide * silu).astype(LOW)

    last = ring - 1

    def advance(label, flow, near, other, count):
        if count == last:
            return join(owner_after(count), flow, near, other, ring, F32), None
        block = join(owner_after(count), flow, near, other, ring, LOW)
        return block, hop(f"{label}_hop{count + 1}", block)

    def several(label, block, flow, near, other, first, end, *after):
        for count in range(first, end):
            block, flow = advance(label, tie(flow, *after), near, other, count)
        return block, flow

    down_full_grad = product(grad_t, [activation])
    down_grad = lax.psum_scatter(down_full_grad, "dp", scatter_dimension=0, tiled=True)
    two_parts = back_parts([tie(d_gating, down_full_grad), d_lifted], ffn_full, (1, 2), ranks)
    two_arrived = send_parts("two_sum", two_parts)
    gate_far = product(normed_two_pair[0], [tie(d_gating, *two_parts)])
    gate_near = product(normed_two_pair[1], [tie(d_gating, gate_far)])
    lift_full_grad = product(normed_two_t, [tie(d_lifted, gate_near)])
    *two_arrived, gate_far, gate_near, lift_full_grad = lax.optimization_barrier(
        (*two_arrived, gate_far, gate_near, lift_full_grad)
    )
    gate_other = swap(gate_far)
    d_hidden, d_hidden_low, ffn_gain_part = norm_back_sum(
        hidden, ffn_gain, cotangent, [two_parts[0]] + two_arrived, True
    )
    hidden_grad = spread("dh_spread", d_hidden_low)
    lift_grad = lax.psum_scatter(
        tie(lift_full_grad, down_grad, d_hidden_low), "dp", scatter_dimension=0, tiled=True
    )
    gate_block, gate_flow = advance("gate_grad", None, tie(gate_near, d_hidden_low), gate_other, 0)
    ffn_parts = back_parts([tie(activation, d_hidden_low)], ffn_full, (0,), ranks)
    hidden_grad[1] = tie(hidden_grad[1], *ffn_parts)
    gate_block, gate_flow = several(
        "gate_grad", gate_block, gate_flow, gate_near, gate_other, 1, last - 1, hidden_grad[1]
    )
    hidden_grad[-1] = tie(hidden_grad[-1], gate_block)
    hidden_grad_all, hidden_grad_t = fold(core_array, hidden_grad, ring)
    ffn_go = lax.optimization_barrier(tuple(ffn_parts) + tuple(hidden_grad))[:ranks]
    ffn_arrived = send_parts("ffn_sum", ffn_go)
    d_attended = rows_product(hidden_grad_all, out_t[None], ranks, 24)
    d_queries, d_keys, d_values = attend_back(
        me_array, query_low, key_low, value_low, bounds, attended, d_attended, lse, ranks, heads
    )
    d_raw, head_gain_parts = prepare_back(
        d_queries, d_keys, d_values, raw, cosine, sine, head_gains, ranks
    )
    gate_block, gate_flow = advance(
        "gate_grad", tie(gate_flow, *ffn_arrived), gate_near, gate_other, last - 1
    )
    one_parts = back_parts([tie(d_raw, gate_block, *ffn_arrived)], w_qkv[None], (0,), ranks)
    one_arrived = send_parts("one_sum", one_parts)
    attn_full_grad = attn_products([normed_one_t, hidden_grad_t], [tie(d_raw, *one_parts), attended])
    attn_grad = lax.psum_scatter(
        tie(attn_full_grad, lift_grad), "dp", scatter_dimension=0, tiled=True)
    gains = gain_parts(
        tie(normed_all, attn_full_grad), attn_gain, one_parts, ffn_gain_part, head_gain_parts
    )
    (output,) = sum_up(tie(hidden, gains), [ffn_parts[0]] + ffn_arrived)

    def exchange_sum(own, axis, offsets, size):
        pieces = [own] + [lax.ppermute(own, axis, [(i, i ^ j) for i in range(size)]) for j in offsets]
        while len(pieces) > 1:
            pieces = [a + b for a, b in zip(pieces[::2], pieces[1::2])]
        return pieces[0]

    gate_flow = tie(gate_flow, output, gains)
    (down_grad,) = cut_grads(tie(down_grad, output), (hidden_cols,))
    lift_grad = lift_grad[:, :hidden_cols].astype(F32)
    *one_arrived, gate_flow, total, down_grad, lift_grad = lax.optimization_barrier(
        (*one_arrived, gate_flow, gains, down_grad, lift_grad)
    )
    total = exchange_sum(total, "tensor", range(1, ranks), ranks)
    (gate_grad,) = last_join(
        owner_after(last), gate_flow, gate_near, gate_other, ring, hidden_cols, 1
    )
    (tokens_grad,) = norm_back_sum(tokens, attn_gain, d_hidden, [one_parts[0]] + one_arrived, False)
    query_grad, key_grad, value_grad, out_grad = cut_grads(
        attn_grad, (q_cols, kv_cols, kv_cols, q_cols)
    )

    total = tie(total, tokens_grad, gate_grad)
    total = exchange_sum(total, "dp", range(1, 2), dp_size)
    total = exchange_sum(total, "dp", range(2, dp_size, 2), dp_size)
    total = total.reshape(-1)
    a, b = attn_gain.shape[0], 2 * attn_gain.shape[0]
    query_gain_grad = jnp.sum(total[b : b + q_cols].reshape(-1, HEAD_SIZE), axis=0)
    key_gain_grad = jnp.sum(total[b + q_cols :].reshape(-1, HEAD_SIZE), axis=0)
    return (
        output,
        tokens_grad,
        total[:a],
        query_grad,
        key_grad,
        value_grad,
        query_gain_grad,
        key_gain_grad,
        out_grad,
        total[a:b],
        gate_grad,
        lift_grad,
        down_grad,
    )


def solution(mesh):
    in_specs = (
        P(("dp", "tensor"), None),
        P("dp"),
        P(),
        P("dp", "tensor"),
        P("dp", "tensor"),
        P("dp", "tensor"),
        P(),
        P(),
        P("tensor", "dp"),
        P(),
        P("dp", "tensor"),
        P("dp", "tensor"),
        P("tensor", "dp"),
        P(("dp", "tensor"), None),
    )
    out_specs = (
        P(("dp", "tensor"), None),
        P(("dp", "tensor"), None),
        P(),
        P("dp", "tensor"),
        P("dp", "tensor"),
        P("dp", "tensor"),
        P(),
        P(),
        P("tensor", "dp"),
        P(),
        P("dp", "tensor"),
        P("dp", "tensor"),
        P("tensor", "dp"),
    )
    body = functools.partial(shards, mesh.shape["dp"], mesh.shape["tensor"])
    return jax.shard_map(body, mesh=mesh, in_specs=in_specs, out_specs=out_specs, check_vma=False)
```

```python
import functools

import jax
import jax.numpy as jnp
from jax import lax
from jax.experimental import pallas as pl
from jax.experimental.pallas import tpu as pltpu
from jax.sharding import PartitionSpec as P

QUERY_HEADS = 24
KEY_VALUE_HEADS = 8
HEAD_SIZE = 64
GROUP = QUERY_HEADS // KEY_VALUE_HEADS
EPSILON = 1e-05
ROTARY_BASE = 1000000.0
NEGATIVE_FILL = -1e30
F32 = jnp.float32
LOW = jnp.bfloat16
SCALE = HEAD_SIZE ** (-0.5)
FREE = pl.CostEstimate(flops=0, bytes_accessed=0, transcendentals=0)


def norm_rows(values_in, gain):
    return (
        values_in
        * lax.rsqrt(jnp.mean(values_in * values_in, axis=-1, keepdims=True) + EPSILON)
        * gain
    )


def norm_back(values, gain, grad):
    inverse = lax.rsqrt(jnp.mean(values * values, axis=-1, keepdims=True) + EPSILON)
    hat = values * inverse
    scaled = grad * gain
    inner = jnp.mean(scaled * hat, axis=-1, keepdims=True)
    return (scaled - hat * inner) * inverse, jnp.sum(grad * hat, axis=0)


def mm(left, right):
    return jnp.dot(left, right, preferred_element_type=F32)


def cross_rows(left, right):
    return lax.dot_general(left, right, (((1,), (1,)), ((), ())), preferred_element_type=F32)


def cross_cols(left, right):
    return lax.dot_general(left, right, (((0,), (0,)), ((), ())), preferred_element_type=F32)


NT = (((1,), (1,)), ((), ()))
NN = (((1,), (0,)), ((), ()))
TN = (((0,), (0,)), ((), ()))


def kdot(left, right, dims):
    return lax.dot_general(left, right, dims, preferred_element_type=F32)


def stack_heads(block, head):
    first = head * GROUP * HEAD_SIZE
    return jnp.concatenate(
        [block[:, first + g * HEAD_SIZE : first + (g + 1) * HEAD_SIZE] for g in range(GROUP)], axis=0
    )


def attend_kernel(heads, rows, me_ref, q_ref, k_ref, v_ref, lo_ref, out_ref, lse_ref):
    me = me_ref[0]
    block = pl.program_id(0) ^ me
    low_bound = jnp.concatenate([lo_ref[0]] * GROUP, axis=1)
    row_ids = block * rows + lax.broadcasted_iota(jnp.int32, (1, rows), 1)
    row_ids = jnp.concatenate([row_ids] * GROUP, axis=1)
    width = GROUP * rows
    queries = q_ref[...] * SCALE
    pieces = []
    for head in range(heads):
        q3 = stack_heads(queries, head)
        cols = slice(head * HEAD_SIZE, (head + 1) * HEAD_SIZE)

        def step(other, carry, q3=q3, cols=cols):
            peak, total, acc = carry
            first = pl.multiple_of((other ^ me) * rows, rows)
            keys = k_ref[pl.ds(first, rows), cols]
            vals = v_ref[pl.ds(first, rows), cols]
            ids = other * rows + lax.broadcasted_iota(jnp.int32, (rows, 1), 0)
            scores = kdot(keys, q3, NT)
            scores = jnp.where((ids <= row_ids) & (ids >= low_bound), scores, NEGATIVE_FILL)
            higher = jnp.maximum(peak, jnp.max(scores, axis=0, keepdims=True))
            fade = jnp.exp(peak - higher)
            exps = jnp.exp(scores - higher)
            total = total * fade + jnp.sum(exps, axis=0, keepdims=True)
            acc = acc * fade + kdot(vals, exps.astype(LOW), TN)
            return higher, total, acc

        start = (
            jnp.full((1, width), NEGATIVE_FILL, F32),
            jnp.zeros((1, width), F32),
            jnp.zeros((HEAD_SIZE, width), F32),
        )
        start = step(block, start)
        peak, total, acc = lax.fori_loop(0, block, step, start)
        acc = acc / total
        lse_ref[0, head : head + 1, :] = peak + jnp.log(total)
        pieces += [acc[:, g * rows : (g + 1) * rows] for g in range(GROUP)]
    out_ref[...] = jnp.concatenate(pieces, axis=0).T.astype(LOW)


def attend_back_kernel(
    heads, rows, me_ref, q_ref, k_ref, v_ref, lo_ref, o_ref, do_ref, lse_ref, dq_ref, dk_ref, dv_ref
):
    me = me_ref[0]

    @pl.when(pl.program_id(0) == 0)
    def _():
        dk_ref[...] = jnp.zeros_like(dk_ref)
        dv_ref[...] = jnp.zeros_like(dv_ref)

    block = pl.program_id(0) ^ me
    low_bound = jnp.concatenate([lo_ref[0]] * GROUP, axis=1)
    row_ids = block * rows + lax.broadcasted_iota(jnp.int32, (1, rows), 1)
    row_ids = jnp.concatenate([row_ids] * GROUP, axis=1)
    width = GROUP * rows
    queries = q_ref[...] * SCALE
    grads = do_ref[...]
    product = (grads.astype(F32) * o_ref[...].astype(F32)).T
    pieces = []
    for head in range(heads):
        q3 = stack_heads(queries, head)
        do3 = stack_heads(grads, head)
        cols = slice(head * HEAD_SIZE, (head + 1) * HEAD_SIZE)
        first_row = head * GROUP * HEAD_SIZE
        inner = jnp.concatenate(
            [
                jnp.sum(
                    product[first_row + g * HEAD_SIZE : first_row + (g + 1) * HEAD_SIZE],
                    axis=0,
                    keepdims=True,
                )
                for g in range(GROUP)
            ],
            axis=1,
        )
        lse = lse_ref[0, head : head + 1, :]

        def step(other, acc, q3=q3, do3=do3, cols=cols, inner=inner, lse=lse, own=False):
            first = pl.multiple_of((other ^ me) * rows, rows)
            place = pl.ds(first, rows)
            keys = k_ref[place, cols]
            vals = v_ref[place, cols]
            ids = other * rows + lax.broadcasted_iota(jnp.int32, (rows, 1), 0)
            scores = kdot(keys, q3, NT)
            allowed = ids >= low_bound
            if own:
                allowed = allowed & (ids <= row_ids)
            scores = jnp.where(allowed, scores, NEGATIVE_FILL)
            probs = jnp.exp(scores - lse)
            d_probs = kdot(vals, do3, NT)
            d_scores = (probs * (d_probs - inner)).astype(LOW)
            dk_ref[place, cols] += kdot(d_scores, q3, NN)
            dv_ref[place, cols] += kdot(probs.astype(LOW), do3, NN)
            return acc + kdot(keys, d_scores, TN)

        acc = step(block, jnp.zeros((HEAD_SIZE, width), F32), own=True)
        acc = lax.fori_loop(0, block, step, acc)
        pieces += [acc[:, g * rows : (g + 1) * rows] for g in range(GROUP)]
    dq_ref[...] = jnp.concatenate(pieces, axis=0).T * SCALE


def attention_specs(ranks, rows, heads):
    length = ranks * rows
    q_spec = pl.BlockSpec((rows, heads * GROUP * HEAD_SIZE), lambda i, me: (i, 0))
    kv_spec = pl.BlockSpec((length, heads * HEAD_SIZE), lambda i, me: (0, 0))
    lo_spec = pl.BlockSpec((1, 1, rows), lambda i, me: (i, 0, 0))
    lse_spec = pl.BlockSpec((1, heads, GROUP * rows), lambda i, me: (i, 0, 0))
    return q_spec, kv_spec, lo_spec, lse_spec


def attend(me, queries, keys, values, bounds, ranks, heads):
    length = queries.shape[0]
    rows = length // ranks
    q_spec, kv_spec, lo_spec, lse_spec = attention_specs(ranks, rows, heads)
    return pl.pallas_call(
        functools.partial(attend_kernel, heads, rows),
        grid_spec=pltpu.PrefetchScalarGridSpec(
            num_scalar_prefetch=1,
            grid=(ranks,),
            in_specs=[q_spec, kv_spec, kv_spec, lo_spec],
            out_specs=[q_spec, lse_spec],
        ),
        out_shape=[
            jax.ShapeDtypeStruct(queries.shape, LOW),
            jax.ShapeDtypeStruct((ranks, heads, GROUP * rows), F32),
        ],
        compiler_params=pltpu.CompilerParams(vmem_limit_bytes=48 * 2**20),
        cost_estimate=pl.CostEstimate(
            flops=16 * length * length * heads * GROUP * HEAD_SIZE,
            bytes_accessed=32 * 2**20,
            transcendentals=length * length * heads * GROUP,
        ),
        name="attend",
    )(me, queries, keys, values, bounds)


def attend_back(me, queries, keys, values, bounds, attended, d_attended, lse, ranks, heads):
    length = queries.shape[0]
    rows = length // ranks
    q_spec, kv_spec, lo_spec, lse_spec = attention_specs(ranks, rows, heads)
    return pl.pallas_call(
        functools.partial(attend_back_kernel, heads, rows),
        grid_spec=pltpu.PrefetchScalarGridSpec(
            num_scalar_prefetch=1,
            grid=(ranks,),
            in_specs=[q_spec, kv_spec, kv_spec, lo_spec, q_spec, q_spec, lse_spec],
            out_specs=[q_spec, kv_spec, kv_spec],
        ),
        out_shape=[
            jax.ShapeDtypeStruct(queries.shape, F32),
            jax.ShapeDtypeStruct(keys.shape, F32),
            jax.ShapeDtypeStruct(keys.shape, F32),
        ],
        compiler_params=pltpu.CompilerParams(vmem_limit_bytes=48 * 2**20),
        cost_estimate=FREE,
        name="attend_back",
    )(me, queries, keys, values, bounds, attended, d_attended, lse)


def fold_kernel(ranks, ring, rows, core_ref, *refs):
    blocks, (all_ref, turned_ref), split = refs[:ranks], refs[ranks : ranks + 2], refs[ranks + 2 :]
    core = core_ref[0]
    depth = turned_ref.shape[0] // (2 * ring)
    for j in range(ranks):
        block = blocks[j][...]
        span = slice(j * rows, (j + 1) * rows)
        all_ref[span, :] = block
        turned_ref[:, span] = block.T
        if split:
            for i in range(ring):
                to = slice(i * depth, (i + 1) * depth)
                for side_ref, side in zip(split, (1 - core, core)):
                    first = pl.multiple_of((2 * i + side) * depth, 16)
                    side_ref[to, span] = turned_ref[pl.ds(first, depth), span]


def fold(core, blocks, ring, split=False):
    ranks = len(blocks)
    rows, width = blocks[0].shape
    length = ranks * rows
    whole = lambda shape: pl.BlockSpec(shape, lambda i: (0, 0))
    shapes = [(length, width), (width, length)] + ([(width // 2, length)] * 2 if split else [])
    return pl.pallas_call(
        functools.partial(fold_kernel, ranks, ring, rows),
        grid=(1,),
        in_specs=[pl.BlockSpec(memory_space=pltpu.SMEM)] + [whole((rows, width))] * ranks,
        out_specs=[whole(shape) for shape in shapes],
        out_shape=[jax.ShapeDtypeStruct(shape, LOW) for shape in shapes],
        compiler_params=pltpu.CompilerParams(vmem_limit_bytes=40 * 2**20),
        cost_estimate=FREE,
        name="fold",
    )(core, *blocks)


def place_kernel(ring, depth, at_ref, *refs):
    blocks = refs[: 2 * ring]
    full_ref, sems = refs[2 * ring :]
    stage, core = at_ref[0], at_ref[1]
    copies = []
    for hop in range(ring):
        owner = lax.rem(stage - hop + ring, ring)
        for half, side in enumerate((core, 1 - core)):
            first = pl.multiple_of((owner * 2 + side) * depth, 16)
            copies.append(
                pltpu.make_async_copy(
                    blocks[2 * hop + half], full_ref.at[pl.ds(first, depth)], sems.at[2 * hop + half]
                )
            )
    for copy in copies:
        copy.start()
    for copy in copies:
        copy.wait()


def place(at, blocks, ring):
    depth, cols = blocks[0].shape
    return pl.pallas_call(
        functools.partial(place_kernel, ring, depth),
        in_specs=[pl.BlockSpec(memory_space=pltpu.SMEM)]
        + [pl.BlockSpec(memory_space=pl.ANY)] * (2 * ring),
        grid=(1,),
        out_specs=pl.BlockSpec((2 * ring * depth, cols), lambda i: (0, 0)),
        out_shape=jax.ShapeDtypeStruct((2 * ring * depth, cols), LOW),
        scratch_shapes=[pltpu.SemaphoreType.DMA((2 * ring,))],
        compiler_params=pltpu.CompilerParams(vmem_limit_bytes=24 * 2**20),
        cost_estimate=FREE,
        name="place",
    )(at, *blocks)


def product_kernel(tiles, left_ref, *refs):
    for k, right in enumerate(refs[:-1]):

        @pl.when(pl.program_id(0) // tiles == k)
        def _(right=right):
            refs[-1][...] = jnp.dot(
                left_ref[...], right[...], preferred_element_type=F32
            ).astype(LOW)


def product(left, rights):
    depth, length = left.shape
    cols = rights[0].shape[1]
    tile = 256 if cols % 256 == 0 else 128
    tiles = cols // tile
    return pl.pallas_call(
        functools.partial(product_kernel, tiles),
        grid=(tiles * len(rights),),
        in_specs=[pl.BlockSpec((depth, length), lambda i: (0, 0))]
        + [
            pl.BlockSpec((length, tile), lambda i, k=k: (0, jnp.clip(i - k * tiles, 0, tiles - 1)))
            for k in range(len(rights))
        ],
        out_specs=pl.BlockSpec((depth, tile), lambda i: (0, i)),
        out_shape=jax.ShapeDtypeStruct((depth, cols * len(rights)), LOW),
        compiler_params=pltpu.CompilerParams(vmem_limit_bytes=56 * 2**20),
        cost_estimate=FREE,
        name="product",
    )(left, *rights)


def attn_products_kernel(*refs):
    lefts, rights, out_ref = refs[:2], refs[2:4], refs[4]
    first = 0
    for left, right in zip(lefts, rights):
        cols = right.shape[1]
        out_ref[:, first : first + cols] = jnp.dot(
            left[...], right[...], preferred_element_type=F32
        ).astype(LOW)
        first += cols


def attn_products(lefts, rights):
    depth = lefts[0].shape[0]
    tiles = 4
    part = lambda a: pl.BlockSpec((depth // tiles, a.shape[1]), lambda i: (i, 0))
    whole = lambda a: pl.BlockSpec(a.shape, lambda i: (0, 0))
    shape = jax.ShapeDtypeStruct((depth, sum(a.shape[1] for a in rights)), LOW)
    return pl.pallas_call(
        attn_products_kernel,
        grid=(tiles,),
        in_specs=[part(a) for a in lefts] + [whole(a) for a in rights],
        out_specs=part(shape),
        out_shape=shape,
        compiler_params=pltpu.CompilerParams(vmem_limit_bytes=40 * 2**20),
        cost_estimate=FREE,
        name="attn_products",
    )(*lefts, *rights)


def back_parts_kernel(rows, count, *refs):
    total = sum(kdot(refs[k][...], refs[count + k][0], NT) for k in range(count))
    for j, out_ref in enumerate(refs[2 * count :]):
        out_ref[...] = total[j * rows : (j + 1) * rows].astype(LOW)


def back_parts(lefts, weights, which, ranks):
    length, cols = lefts[0].shape
    width = weights.shape[1]
    rows = length // ranks
    tile = 256
    return pl.pallas_call(
        functools.partial(back_parts_kernel, rows, len(lefts)),
        grid=(width // tile,),
        in_specs=[pl.BlockSpec((length, cols), lambda i: (0, 0))] * len(lefts)
        + [pl.BlockSpec((1, tile, cols), lambda i, k=k: (k, i, 0)) for k in which],
        out_specs=[pl.BlockSpec((rows, tile), lambda i: (0, i))] * ranks,
        out_shape=[jax.ShapeDtypeStruct((rows, width), LOW)] * ranks,
        compiler_params=pltpu.CompilerParams(vmem_limit_bytes=48 * 2**20),
        cost_estimate=FREE,
        name="back_parts",
    )(*lefts, *([weights] * len(which)))


def join_kernel(flows, at_ref, *refs):
    total = refs[flows][...].astype(F32) + refs[flows + 1][...].astype(F32)
    if flows:
        total = total + refs[0][...].astype(F32)
    refs[-1][...] = total.astype(refs[-1].dtype)


def join(owner, flow, near, other, ring, dtype):
    depth, cols = near.shape[0] // ring, near.shape[1]
    flows = [] if flow is None else [flow]
    half = cols // 2 if cols % 256 == 0 else cols
    row = pl.BlockSpec((depth, half), lambda i, at: (0, i))
    chosen = pl.BlockSpec((depth, half), lambda i, at: (at[0], i))
    return pl.pallas_call(
        functools.partial(join_kernel, len(flows)),
        grid_spec=pltpu.PrefetchScalarGridSpec(
            num_scalar_prefetch=1,
            grid=(cols // half,),
            in_specs=[row] * len(flows) + [chosen] * 2,
            out_specs=row,
        ),
        out_shape=jax.ShapeDtypeStruct((depth, cols), dtype),
        compiler_params=pltpu.CompilerParams(vmem_limit_bytes=24 * 2**20),
        cost_estimate=FREE,
        name="join",
    )(owner.astype(jnp.int32).reshape(1), *flows, near, other)


def last_join_kernel(at_ref, flow_ref, near_ref, other_ref, *out_refs):
    total = flow_ref[...].astype(F32) + near_ref[...].astype(F32) + other_ref[...].astype(F32)
    width = total.shape[1] // len(out_refs)
    for k, out_ref in enumerate(out_refs):
        cols = out_ref.shape[1]
        out_ref[...] = total[:, k * width : k * width + cols]


def last_join(owner, flow, near, other, ring, cols, count):
    depth, wide = near.shape[0] // ring, near.shape[1]
    chosen = pl.BlockSpec((depth, wide), lambda i, at: (at[0], 0))
    return pl.pallas_call(
        last_join_kernel,
        grid_spec=pltpu.PrefetchScalarGridSpec(
            num_scalar_prefetch=1,
            grid=(1,),
            in_specs=[pl.BlockSpec((depth, wide), lambda i, at: (0, 0)), chosen, chosen],
            out_specs=[pl.BlockSpec((depth, cols), lambda i, at: (0, 0))] * count,
        ),
        out_shape=[jax.ShapeDtypeStruct((depth, cols), F32)] * count,
        compiler_params=pltpu.CompilerParams(vmem_limit_bytes=56 * 2**20),
        cost_estimate=FREE,
        name="last_join",
    )(owner.astype(jnp.int32).reshape(1), flow, near, other)


def cut_kernel(widths, grads_ref, *out_refs):
    first = 0
    for cols, out_ref in zip(widths[:-1], out_refs):
        out_ref[...] = grads_ref[:, first : first + cols].astype(F32)
        first += cols
    out_refs[-1][...] = grads_ref[:, first : first + widths[-1]].astype(F32).T


def cut_grads(grads, widths):
    depth = grads.shape[0]
    whole = lambda shape: pl.BlockSpec(shape, lambda i: (0, 0))
    shapes = [(depth, cols) for cols in widths[:-1]] + [(widths[-1], depth)]
    return pl.pallas_call(
        functools.partial(cut_kernel, widths),
        grid=(1,),
        in_specs=[whole(grads.shape)],
        out_specs=[whole(shape) for shape in shapes],
        out_shape=[jax.ShapeDtypeStruct(shape, F32) for shape in shapes],
        compiler_params=pltpu.CompilerParams(vmem_limit_bytes=24 * 2**20),
        cost_estimate=FREE,
        name="cut_grads",
    )(grads)


def sum_kernel(count, base_ref, *refs):
    total = base_ref[...].astype(F32)
    arrived = refs[0][...].astype(F32)
    for ref in refs[1:count]:
        arrived = arrived + ref[...].astype(F32)
    total = total + arrived
    refs[-1 if len(refs) == count + 1 else -2][...] = total
    if len(refs) > count + 1:
        gain_ref = refs[count]
        inverse = lax.rsqrt(jnp.mean(total * total, axis=-1, keepdims=True) + EPSILON)
        refs[-1][...] = (total * inverse * gain_ref[...]).astype(LOW)


def sum_up(base, parts, gain=None):
    rows, width = base.shape
    step = rows // 2
    by_row = pl.BlockSpec((step, width), lambda i: (i, 0))
    gains = [] if gain is None else [gain.reshape(1, -1)]
    outs = [jax.ShapeDtypeStruct((rows, width), F32)]
    if gains:
        outs.append(jax.ShapeDtypeStruct((rows, width), LOW))
    return pl.pallas_call(
        functools.partial(sum_kernel, len(parts)),
        grid=(2,),
        in_specs=[by_row] * (1 + len(parts)) + [pl.BlockSpec((1, width), lambda i: (0, 0))] * len(gains),
        out_specs=[by_row] * len(outs),
        out_shape=outs,
        compiler_params=pltpu.CompilerParams(vmem_limit_bytes=56 * 2**20),
        cost_estimate=FREE,
        name="sum_up",
    )(base, *parts, *gains)


def norm_back_kernel(count, value_ref, gain_ref, rest_ref, *refs):
    parts, outs = refs[:count], refs[count:]
    value = value_ref[...].astype(F32)
    grad = parts[0][...].astype(F32)
    for ref in parts[1:]:
        grad = grad + ref[...].astype(F32)
    inverse = lax.rsqrt(jnp.mean(value * value, axis=-1, keepdims=True) + EPSILON)
    hat = value * inverse
    scaled = grad * gain_ref[...]
    inner = jnp.mean(scaled * hat, axis=-1, keepdims=True)
    total = rest_ref[...].astype(F32) + (scaled - hat * inner) * inverse
    outs[0][...] = total
    if len(outs) > 1:
        outs[1][...] = total.astype(LOW)

        @pl.when(pl.program_id(0) == 0)
        def _():
            outs[2][...] = jnp.zeros_like(outs[2])

        outs[2][...] += jnp.sum(grad * hat, axis=0, keepdims=True)


def norm_back_sum(value, gain, rest, parts, more):
    rows, width = value.shape
    step = rows // 2
    by_row = pl.BlockSpec((step, width), lambda i: (i, 0))
    fixed = pl.BlockSpec((1, width), lambda i: (0, 0))
    shapes = [jax.ShapeDtypeStruct((rows, width), F32)]
    if more:
        shapes += [jax.ShapeDtypeStruct((rows, width), LOW), jax.ShapeDtypeStruct((1, width), F32)]
    return pl.pallas_call(
        functools.partial(norm_back_kernel, len(parts)),
        grid=(2,),
        in_specs=[by_row, fixed, by_row] + [by_row] * len(parts),
        out_specs=[by_row, by_row, fixed][: len(shapes)],
        out_shape=shapes,
        compiler_params=pltpu.CompilerParams(vmem_limit_bytes=56 * 2**20),
        cost_estimate=FREE,
        name="norm_back_sum",
    )(value, gain.reshape(1, -1), rest, *parts)


def rows_product_kernel(left_ref, right_ref, out_ref):
    out_ref[...] = jnp.dot(left_ref[...], right_ref[0], preferred_element_type=F32).astype(LOW)


def rows_product(left, right, ranks, grant):
    length, depth = left.shape
    rows = length // ranks
    return pl.pallas_call(
        rows_product_kernel,
        grid=(ranks,),
        in_specs=[
            pl.BlockSpec((rows, depth), lambda i: (i, 0)),
            pl.BlockSpec((1,) + right.shape[1:], lambda i: (0, 0, 0)),
        ],
        out_specs=pl.BlockSpec((rows, right.shape[2]), lambda i: (i, 0)),
        out_shape=jax.ShapeDtypeStruct((length, right.shape[2]), LOW),
        compiler_params=pltpu.CompilerParams(vmem_limit_bytes=grant * 2**20),
        cost_estimate=FREE,
        name="rows_product",
    )(left, right)


def gain_parts_kernel(normed_ref, gain_ref, two_ref, heads_ref, *refs):
    parts, out_ref = refs[:-1], refs[-1]
    rows, width = parts[0].shape
    total = jnp.zeros((1, width), F32)
    for j, ref in enumerate(parts):
        block = normed_ref[j * rows : (j + 1) * rows, :].astype(F32)
        total = total + jnp.sum(block * ref[...].astype(F32), axis=0, keepdims=True)
    out_ref[:, :width] = total / gain_ref[...]
    out_ref[:, width : 2 * width] = two_ref[...]
    out_ref[:, 2 * width :] = heads_ref[...]


def gain_parts(normed, gain, parts, two, heads):
    args = [normed, gain.reshape(1, -1), two, heads, *parts]
    whole = lambda a: pl.BlockSpec(a.shape, lambda i: (0, 0))
    shape = jax.ShapeDtypeStruct((1, 2 * normed.shape[1] + heads.shape[1]), F32)
    return pl.pallas_call(
        gain_parts_kernel,
        grid=(1,),
        in_specs=[whole(a) for a in args],
        out_specs=whole(shape),
        out_shape=shape,
        compiler_params=pltpu.CompilerParams(vmem_limit_bytes=56 * 2**20),
        cost_estimate=FREE,
        name="gain_parts",
    )(*args)


def group_mean(values):
    width = values.shape[1]
    part = 2 * HEAD_SIZE
    left = lax.broadcasted_iota(jnp.int32, (part, part), 0) // HEAD_SIZE
    right = lax.broadcasted_iota(jnp.int32, (part, part), 1) // HEAD_SIZE
    spread = jnp.where(left == right, 1.0 / HEAD_SIZE, 0.0).astype(F32)
    pieces = []
    for first in range(0, width, part):
        size = min(part, width - first)
        pieces.append(
            lax.dot_general(
                values[:, first : first + size],
                spread[:size, :size],
                NN,
                precision=lax.Precision.HIGHEST,
                preferred_element_type=F32,
            )
        )
    return jnp.concatenate(pieces, axis=1) if len(pieces) > 1 else pieces[0]


def across(table, width):
    part = table.shape[1]
    if width < part:
        return table[:, :width]
    return jnp.concatenate([table] * (width // part) + ([table[:, : width % part]] if width % part else []), axis=1)


def partner(values):
    width = values.shape[1]
    half = HEAD_SIZE // 2
    lane = lax.broadcasted_iota(jnp.int32, values.shape, 1) % HEAD_SIZE
    return jnp.where(lane < half, pltpu.roll(values, width - half, 1), pltpu.roll(values, half, 1))


def prepare_kernel(q_cols, kv_cols, x_ref, w_ref, cos_ref, sin_ref, gain_ref, q_ref, k_ref, v_ref, raw_ref):
    product = jnp.dot(x_ref[...], w_ref[...], preferred_element_type=F32)
    for first, cols, to in ((0, q_cols, q_ref), (q_cols, kv_cols, k_ref)):
        raw = product[:, first : first + cols]
        scaled = raw * lax.rsqrt(group_mean(raw * raw) + EPSILON) * gain_ref[:, first : first + cols]
        cos = across(cos_ref[...], cols)
        sin = across(sin_ref[...], cols)
        to[...] = (scaled * cos + partner(scaled) * sin).astype(LOW)
        raw_ref[:, first : first + cols] = raw
    v_ref[...] = product[:, q_cols + kv_cols :].astype(LOW)


def prepare(normed, weight, cosine, sine, gains, q_cols, kv_cols, ranks):
    length, width = normed.shape
    rows = length // ranks
    at_row = lambda i: (i, 0)
    fixed = lambda i: (0, 0)
    return pl.pallas_call(
        functools.partial(prepare_kernel, q_cols, kv_cols),
        grid=(ranks,),
        in_specs=[
            pl.BlockSpec((rows, width), at_row),
            pl.BlockSpec(weight.shape, fixed),
            pl.BlockSpec((rows, cosine.shape[1]), at_row),
            pl.BlockSpec((rows, cosine.shape[1]), at_row),
            pl.BlockSpec((1, q_cols + kv_cols), fixed),
        ],
        out_specs=[
            pl.BlockSpec((rows, q_cols), at_row),
            pl.BlockSpec((rows, kv_cols), at_row),
            pl.BlockSpec((rows, kv_cols), at_row),
            pl.BlockSpec((rows, q_cols + kv_cols), at_row),
        ],
        out_shape=[
            jax.ShapeDtypeStruct((length, q_cols), LOW),
            jax.ShapeDtypeStruct((length, kv_cols), LOW),
            jax.ShapeDtypeStruct((length, kv_cols), LOW),
            jax.ShapeDtypeStruct((length, q_cols + kv_cols), F32),
        ],
        compiler_params=pltpu.CompilerParams(vmem_limit_bytes=40 * 2**20),
        cost_estimate=FREE,
        name="prepare",
    )(normed, weight, cosine, sine, gains)


def prepare_back_kernel(
    q_cols, kv_cols, dq_ref, dk_ref, dv_ref, raw_ref, cos_ref, sin_ref, gain_ref, out_ref, gain_grad_ref
):
    @pl.when(pl.program_id(0) == 0)
    def _():
        gain_grad_ref[...] = jnp.zeros_like(gain_grad_ref)

    for first, cols, grad_ref in ((0, q_cols, dq_ref), (q_cols, kv_cols, dk_ref)):
        span = slice(first, first + cols)
        grad = grad_ref[...]
        turned = grad * across(cos_ref[...], cols) - partner(grad) * across(sin_ref[...], cols)
        raw = raw_ref[:, span]
        inverse = lax.rsqrt(group_mean(raw * raw) + EPSILON)
        hat = raw * inverse
        gain_grad_ref[:, span] += jnp.sum(turned * hat, axis=0, keepdims=True)
        scaled = turned * gain_ref[:, span]
        out_ref[:, span] = ((scaled - hat * group_mean(scaled * hat)) * inverse).astype(LOW)
    out_ref[:, q_cols + kv_cols :] = dv_ref[...].astype(LOW)


def prepare_back(d_queries, d_keys, d_values, raw, cosine, sine, gains, ranks):
    length, q_cols = d_queries.shape
    kv_cols = d_keys.shape[1]
    rows = length // ranks
    at_row = lambda i: (i, 0)
    fixed = lambda i: (0, 0)
    return pl.pallas_call(
        functools.partial(prepare_back_kernel, q_cols, kv_cols),
        grid=(ranks,),
        in_specs=[
            pl.BlockSpec((rows, q_cols), at_row),
            pl.BlockSpec((rows, kv_cols), at_row),
            pl.BlockSpec((rows, kv_cols), at_row),
            pl.BlockSpec((rows, q_cols + kv_cols), at_row),
            pl.BlockSpec((rows, cosine.shape[1]), at_row),
            pl.BlockSpec((rows, cosine.shape[1]), at_row),
            pl.BlockSpec((1, q_cols + kv_cols), fixed),
        ],
        out_specs=[
            pl.BlockSpec((rows, q_cols + 2 * kv_cols), at_row),
            pl.BlockSpec((1, q_cols + kv_cols), fixed),
        ],
        out_shape=[
            jax.ShapeDtypeStruct((length, q_cols + 2 * kv_cols), LOW),
            jax.ShapeDtypeStruct((1, q_cols + kv_cols), F32),
        ],
        compiler_params=pltpu.CompilerParams(vmem_limit_bytes=56 * 2**20),
        cost_estimate=FREE,
        name="prepare_back",
    )(d_queries, d_keys, d_values, raw, cosine, sine, gains)


def shards(
    dp_size,
    ranks,
    tokens,
    segments,
    attn_gain,
    w_query,
    key_weight,
    value_weight,
    query_gain,
    key_gain,
    w_out,
    ffn_gain,
    w_gate,
    w_up,
    w_down,
    cotangent,
):
    ring = dp_size // 2
    index = lax.axis_index("dp")
    stage = index // 2
    core = index % 2
    me = lax.axis_index("tensor")
    swap_pairs = [(i, i ^ 1) for i in range(dp_size)]
    ring_pairs = [(i, (i + 2) % dp_size) for i in range(dp_size)]
    heads = KEY_VALUE_HEADS // ranks
    rows = tokens.shape[0]
    length = segments.shape[0]
    q_cols = w_query.shape[1]
    kv_cols = key_weight.shape[1]

    hidden_cols = w_gate.shape[1]
    hidden_pad = -hidden_cols % 128

    def widen(weight):
        return jnp.pad(weight, ((0, 0), (0, hidden_pad)))

    def swap(v):
        return lax.ppermute(v, "dp", swap_pairs)

    def onward(v):
        return lax.ppermute(v, "dp", ring_pairs)

    core_array = core.astype(jnp.int32).reshape(1)
    at = jnp.stack([stage, core]).astype(jnp.int32)

    def hop(label, block):
        with jax.named_scope(label):
            return onward(block)

    def owner_after(count):
        return lax.rem(stage - 1 - count + 2 * ring, ring)

    def spread(label, block):
        with jax.named_scope(label):
            return [block] + [
                lax.ppermute(block, "tensor", [(i, i ^ j) for i in range(ranks)])
                for j in range(1, ranks)
            ]

    def send_parts(label, parts):
        with jax.named_scope(label):
            return [
                lax.ppermute(parts[j], "tensor", [(i, i ^ j) for i in range(ranks)])
                for j in range(1, ranks)
            ]

    def add_up(own, arrived):
        total = own.astype(F32)
        for piece in arrived:
            total = total + piece.astype(F32)
        return total

    def cut(matrix):
        return [matrix[j * rows : (j + 1) * rows] for j in range(ranks)]

    def tie(value, *others):
        return lax.optimization_barrier((value,) + others)[0]

    tokens_wide = tokens.astype(F32)
    normed_own = norm_rows(tokens_wide, attn_gain).astype(LOW)
    normed_one = spread("one_spread", normed_own)
    wide = hidden_cols + hidden_pad
    qkv_blocks = [jnp.concatenate([w_query, key_weight, value_weight], axis=1)]
    for count in range(1, ring):
        qkv_blocks.append(hop(f"qkv_hop{count}", qkv_blocks[-1]))
    ffn_full = lax.all_gather(
        tie(jnp.stack([widen(w_down.T), widen(w_gate), widen(w_up)]), qkv_blocks[2]),
        "dp",
        axis=1,
        tiled=True,
    )
    gate_full, up_full = ffn_full[1], ffn_full[2]
    grad_blocks = spread("cot_spread", tie(cotangent, *normed_one))
    first_start = jnp.sum((segments < 1).astype(jnp.int32))
    second_start = jnp.sum((segments < 2).astype(jnp.int32))
    ids = jnp.arange(length, dtype=jnp.int32).reshape(ranks, rows)
    begins = jnp.where(segments == 0, 0, jnp.where(segments == 1, first_start, second_start))
    begins = begins.astype(jnp.int32).reshape(ranks, rows)
    order = [me ^ j for j in range(ranks)]
    bounds = jnp.stack([lax.dynamic_index_in_dim(begins, o, 0, keepdims=False) for o in order])
    here = jnp.stack([lax.dynamic_index_in_dim(ids, o, 0, keepdims=False) for o in order])
    positions = (here - bounds).reshape(length).astype(F32)
    bounds = bounds.reshape(ranks, 1, rows)
    half = HEAD_SIZE // 2
    freqs = ROTARY_BASE ** (-2.0 * jnp.arange(half, dtype=F32) / HEAD_SIZE)
    angles = positions[:, None] * jnp.concatenate([freqs] * 4)[None, :]
    signs = jnp.concatenate([-jnp.ones(half, F32), jnp.ones(half, F32)] * 2)
    cosine = jnp.cos(angles)
    sine = jnp.sin(angles) * signs[None, :]
    head_gains = jnp.concatenate(
        [query_gain] * (q_cols // HEAD_SIZE) + [key_gain] * (kv_cols // HEAD_SIZE)
    ).reshape(1, -1)

    out_blocks = [w_out.T]
    normed_all, normed_one_t = fold(core_array, normed_one, ring)
    for count in range(1, ring):
        out_flow = hop(f"out_hop{count}", out_blocks[-1])
        if count < ring - 1:
            before = (cosine, sine, head_gains, bounds) if count == 1 else (normed_all,)
            out_blocks.append(tie(out_flow, qkv_blocks[count + 1], *before))

    def complete(blocks):
        return place(at, [b for block in blocks for b in (block, swap(block))], ring)

    w_qkv = complete(qkv_blocks)
    query_low, key_low, value_low, raw = prepare(
        normed_all, w_qkv, cosine, sine, head_gains, q_cols, kv_cols, ranks
    )
    me_array = me.astype(jnp.int32).reshape(1)
    attended, lse = attend(me_array, query_low, key_low, value_low, bounds, ranks, heads)

    attended_go = tie(attended, *grad_blocks)
    out_blocks.append(tie(out_flow, attended))
    out_t = complete(out_blocks)
    attn_parts = back_parts([attended_go], out_t[None], (0,), ranks)
    attn_arrived = send_parts("attn_sum", attn_parts)
    grad_all, grad_t = fold(core_array, [tie(grad_blocks[0], *attn_parts)] + grad_blocks[1:], ring)
    attn_arrived[0] = tie(attn_arrived[0], grad_all)
    hidden, normed_two_own = sum_up(tokens, [attn_parts[0]] + attn_arrived, ffn_gain)
    normed_two = spread("two_spread", normed_two_own)
    d_activation = rows_product(grad_all, ffn_full, ranks, 56)
    normed_two[-1] = tie(normed_two[-1], d_activation)
    normed_two_all, normed_two_t, *normed_two_pair = fold(core_array, normed_two, ring, True)

    gating = mm(normed_two_all, gate_full).astype(LOW).astype(F32)
    lifted = mm(normed_two_all, up_full)
    gate_sig = jax.nn.sigmoid(gating)
    silu = gating * gate_sig
    activation = (silu * lifted).astype(LOW)
    d_act_wide = d_activation.astype(F32)
    d_gating = (d_act_wide * lifted * gate_sig * (1.0 + gating * (1.0 - gate_sig))).astype(LOW)
    d_lifted = (d_act_wide * silu).astype(LOW)

    last = ring - 1

    def advance(label, flow, near, other, count):
        if count == last:
            return join(owner_after(count), flow, near, other, ring, F32), None
        block = join(owner_after(count), flow, near, other, ring, LOW)
        return block, hop(f"{label}_hop{count + 1}", block)

    def several(label, block, flow, near, other, first, end, *after):
        for count in range(first, end):
            block, flow = advance(label, tie(flow, *after), near, other, count)
        return block, flow

    down_full_grad = product(grad_t, [activation])
    down_grad = lax.psum_scatter(down_full_grad, "dp", scatter_dimension=0, tiled=True)
    two_parts = back_parts([tie(d_gating, down_full_grad), d_lifted], ffn_full, (1, 2), ranks)
    two_arrived = send_parts("two_sum", two_parts)
    gate_far = product(normed_two_pair[0], [tie(d_gating, *two_parts)])
    gate_near = product(normed_two_pair[1], [tie(d_gating, gate_far)])
    lift_full_grad = product(normed_two_t, [tie(d_lifted, gate_near)])
    *two_arrived, gate_far, gate_near, lift_full_grad = lax.optimization_barrier(
        (*two_arrived, gate_far, gate_near, lift_full_grad)
    )
    gate_other = swap(gate_far)
    d_hidden, d_hidden_low, ffn_gain_part = norm_back_sum(
        hidden, ffn_gain, cotangent, [two_parts[0]] + two_arrived, True
    )
    hidden_grad = spread("dh_spread", d_hidden_low)
    lift_grad = lax.psum_scatter(
        tie(lift_full_grad, down_grad, d_hidden_low), "dp", scatter_dimension=0, tiled=True
    )
    gate_block, gate_flow = advance("gate_grad", None, tie(gate_near, d_hidden_low), gate_other, 0)
    ffn_parts = back_parts([tie(activation, d_hidden_low)], ffn_full, (0,), ranks)
    hidden_grad[1] = tie(hidden_grad[1], *ffn_parts)
    gate_block, gate_flow = several(
        "gate_grad", gate_block, gate_flow, gate_near, gate_other, 1, last - 1, hidden_grad[1]
    )
    hidden_grad[-1] = tie(hidden_grad[-1], gate_block)
    hidden_grad_all, hidden_grad_t = fold(core_array, hidden_grad, ring)
    ffn_go = lax.optimization_barrier(tuple(ffn_parts) + tuple(hidden_grad))[:ranks]
    ffn_arrived = send_parts("ffn_sum", ffn_go)
    d_attended = rows_product(hidden_grad_all, out_t[None], ranks, 24)
    d_queries, d_keys, d_values = attend_back(
        me_array, query_low, key_low, value_low, bounds, attended, d_attended, lse, ranks, heads
    )
    d_raw, head_gain_parts = prepare_back(
        d_queries, d_keys, d_values, raw, cosine, sine, head_gains, ranks
    )
    gate_block, gate_flow = advance(
        "gate_grad", tie(gate_flow, *ffn_arrived), gate_near, gate_other, last - 1
    )
    one_parts = back_parts([tie(d_raw, gate_block, *ffn_arrived)], w_qkv[None], (0,), ranks)
    one_arrived = send_parts("one_sum", one_parts)
    attn_full_grad = attn_products([normed_one_t, hidden_grad_t], [tie(d_raw, *one_parts), attended])
    attn_grad = lax.psum_scatter(
        tie(attn_full_grad, lift_grad), "dp", scatter_dimension=0, tiled=True)
    gains = gain_parts(
        tie(normed_all, attn_full_grad), attn_gain, one_parts, ffn_gain_part, head_gain_parts
    )
    (output,) = sum_up(tie(hidden, gains), [ffn_parts[0]] + ffn_arrived)

    def exchange_sum(own, axis, offsets, size):
        pieces = [own] + [lax.ppermute(own, axis, [(i, i ^ j) for i in range(size)]) for j in offsets]
        while len(pieces) > 1:
            pieces = [a + b for a, b in zip(pieces[::2], pieces[1::2])]
        return pieces[0]

    gate_flow = tie(gate_flow, output, gains)
    (down_grad,) = cut_grads(tie(down_grad, output), (hidden_cols,))
    lift_grad = lift_grad[:, :hidden_cols].astype(F32)
    *one_arrived, gate_flow, total, down_grad, lift_grad = lax.optimization_barrier(
        (*one_arrived, gate_flow, gains, down_grad, lift_grad)
    )
    total = exchange_sum(total, "tensor", range(1, ranks), ranks)
    (gate_grad,) = last_join(
        owner_after(last), gate_flow, gate_near, gate_other, ring, hidden_cols, 1
    )
    (tokens_grad,) = norm_back_sum(tokens, attn_gain, d_hidden, [one_parts[0]] + one_arrived, False)
    query_grad, key_grad, value_grad, out_grad = cut_grads(
        attn_grad, (q_cols, kv_cols, kv_cols, q_cols)
    )

    total = tie(total, tokens_grad, gate_grad)
    total = exchange_sum(total, "dp", range(1, 2), dp_size)
    total = exchange_sum(total, "dp", range(2, dp_size, 2), dp_size)
    total = total.reshape(-1)
    a, b = attn_gain.shape[0], 2 * attn_gain.shape[0]
    query_gain_grad = jnp.sum(total[b : b + q_cols].reshape(-1, HEAD_SIZE), axis=0)
    key_gain_grad = jnp.sum(total[b + q_cols :].reshape(-1, HEAD_SIZE), axis=0)
    return (
        output,
        tokens_grad,
        total[:a],
        query_grad,
        key_grad,
        value_grad,
        query_gain_grad,
        key_gain_grad,
        out_grad,
        total[a:b],
        gate_grad,
        lift_grad,
        down_grad,
    )


def solution(mesh):
    in_specs = (
        P(("dp", "tensor"), None),
        P("dp"),
        P(),
        P("dp", "tensor"),
        P("dp", "tensor"),
        P("dp", "tensor"),
        P(),
        P(),
        P("tensor", "dp"),
        P(),
        P("dp", "tensor"),
        P("dp", "tensor"),
        P("tensor", "dp"),
        P(("dp", "tensor"), None),
    )
    out_specs = (
        P(("dp", "tensor"), None),
        P(("dp", "tensor"), None),
        P(),
        P("dp", "tensor"),
        P("dp", "tensor"),
        P("dp", "tensor"),
        P(),
        P(),
        P("tensor", "dp"),
        P(),
        P("dp", "tensor"),
        P("dp", "tensor"),
        P("tensor", "dp"),
    )
    body = functools.partial(shards, mesh.shape["dp"], mesh.shape["tensor"])
    return jax.shard_map(body, mesh=mesh, in_specs=in_specs, out_specs=out_specs, check_vma=False)
```
